32 devices in a mesh: wide: 8 (over y, x, core), narrow: 4 (over z).
Axes of the slice: x: 2, y: 2, z: 4, core: 2. Of those that a mesh axis runs over, the one named last changes fastest.
Arguments:
- patches: bfloat16 [6400, 4, 512], P(('wide', 'narrow')), may hold values from -6 to 6
- window_extent: int32 [64, 2], P('wide'), may hold values from 1 to 10, as said below
- merge_gain: float32 [2048], replicated, may hold values from 0.5 to 1.5
- merge_shift: float32 [2048], replicated, may hold values from -2 to 2
- merge_weight: bfloat16 [2048, 1024], replicated, may hold values from -0.125 to 0.125
- norm1_gain: float32 [1024], replicated, may hold values from 0.5 to 1.5
- norm1_shift: float32 [1024], replicated, may hold values from -2 to 2
- qkv_weight: bfloat16 [1024, 3072], replicated, may hold values from -0.25 to 0.25
- qkv_bias: float32 [3072], replicated, may hold values from -2 to 2
- rel_table: float32 [361, 32], P(None, 'narrow'), may hold values from -4 to 4
- proj_weight: bfloat16 [1024, 1024], P('narrow'), may hold values from -0.5 to 0.5
- proj_bias: float32 [1024], replicated, may hold values from -2 to 2
- norm2_gain: float32 [1024], replicated, may hold values from 0.5 to 1.5
- norm2_shift: float32 [1024], replicated, may hold values from -2 to 2
- fc1_weight: bfloat16 [1024, 4096], P(None, 'narrow'), may hold values from -0.1875 to 0.1875
- fc1_bias: float32 [4096], P('narrow'), may hold values from -2 to 2
- fc2_weight: bfloat16 [4096, 1024], P('narrow'), may hold values from -0.125 to 0.125
- fc2_bias: float32 [1024], replicated, may hold values from -2 to 2
- out_grad: bfloat16 [6400, 1024], P('wide'), may hold values from -6 to 6
Outputs:
- output: bfloat16 [6400, 1024], P(('wide', 'narrow'))
- patches_grad: bfloat16 [6400, 4, 512], P(('wide', 'narrow'))
- merge_gain_grad: float32 [2048], replicated
- merge_shift_grad: float32 [2048], replicated
- merge_weight_grad: float32 [2048, 1024], P(('wide', 'narrow'))
- norm1_gain_grad: float32 [1024], replicated
- norm1_shift_grad: float32 [1024], replicated
- qkv_weight_grad: float32 [1024, 3072], P(('wide', 'narrow'))
- qkv_bias_grad: float32 [3072], replicated
- rel_table_grad: float32 [361, 32], replicated
- proj_weight_grad: float32 [1024, 1024], P(('narrow', 'wide'))
- proj_bias_grad: float32 [1024], replicated
- norm2_gain_grad: float32 [1024], replicated
- norm2_shift_grad: float32 [1024], replicated
- fc1_weight_grad: float32 [1024, 4096], P('wide', 'narrow')
- fc1_bias_grad: float32 [4096], P(('narrow', 'wide'))
- fc2_weight_grad: float32 [4096, 1024], P(('narrow', 'wide'))
- fc2_bias_grad: float32 [1024], replicated
The draws below stay inside these ranges and needn't reach their ends.
Inputs may be any that keep to these rules, and one draw needn't show every extreme that they name: `window_extent`: each window's rows and columns on its page; many windows are whole, and window 0 is.
All inputs are finite; a program needn't handle non-finite values.
Results may differ from the reference program's by a relative error of at most 0.02.
Values may be sent and summed in bfloat16 or wider, within the bound.
No kernel may reach another device: no remote copies, remote signals or barrier semaphores. Data moves between devices by JAX's collectives and lax.ppermute only.
A program may use at most 128 MiB of HBM per device.

```python
import math
from functools import partial
import jax
import jax.numpy as jnp
from jax import lax

C3 = 512
D = 1024
HEADS = 32
HD = 32
FF = 4096
WIN = 10
WINDOWS = 64
TOKENS = 6400
RELSZ = 361


def draw_window_extent(key, part):
    key = jax.random.fold_in(key, 5)
    first, second = jax.random.split(key)
    sizes = jax.random.randint(first, (WINDOWS, 2), 1, WIN + 1)
    whole = jax.random.randint(second, (WINDOWS, 1), 0, 2)
    extent = jnp.where(whole == 1, WIN, sizes)
    return extent.at[0].set(WIN).astype(jnp.int32)


def shard_levels(key, shape, cuts, low, largest):
    level, own = 1.0, jax.random.fold_in(key, 6)
    for axis_at, parts in cuts:
        heights = jnp.exp(jax.random.uniform(jax.random.fold_in(own, axis_at), (parts,), jnp.float32, low / len(cuts), largest / len(cuts)))
        level = level * jnp.repeat(heights, shape[axis_at] // parts).reshape([-1 if axis == axis_at else 1 for axis in range(len(shape))])
    return level


def bell_draw(own_key, shape, scale, limit, pieces=(), held_as=jnp.bfloat16):
    values = scale * jax.random.normal(own_key, shape, jnp.float32)
    if pieces:
        values = values * shard_levels(own_key, shape, pieces, -0.22, 0.18)
    return jnp.clip(values, -limit, limit).astype(held_as)


def setup_inputs(seed: int = 0) -> dict:
    arg_keys = jax.random.split(jax.random.key(seed), 20)
    return {
        "patches": bell_draw(arg_keys[0], (TOKENS, 4, C3), 1.0, 6.0, ((0, 32),)),
        "window_extent": draw_window_extent(jax.random.fold_in(arg_keys[19], 71), 0),
        "merge_gain": jnp.clip(1.0 + 0.1 * jax.random.normal(arg_keys[2], (4 * C3,), jnp.float32), 0.5, 1.5),
        "merge_shift": bell_draw(arg_keys[3], (4 * C3,), 0.3, 2.0, (), jnp.float32),
        "merge_weight": bell_draw(arg_keys[4], (4 * C3, D), (4 * C3) ** -0.5, 0.125),
        "norm1_gain": jnp.clip(1.0 + 0.1 * jax.random.normal(arg_keys[5], (D,), jnp.float32), 0.5, 1.5),
        "norm1_shift": bell_draw(arg_keys[6], (D,), 0.3, 2.0, (), jnp.float32),
        "qkv_weight": bell_draw(arg_keys[7], (D, 3 * D), (D // 2) ** -0.5, 0.25),
        "qkv_bias": bell_draw(arg_keys[8], (3 * D,), 0.3, 2.0, (), jnp.float32),
        "rel_table": bell_draw(arg_keys[9], (RELSZ, HEADS), 1.0, 4.0, ((1, 4),), jnp.float32),
        "proj_weight": bell_draw(arg_keys[10], (D, D), (D // 8) ** -0.5, 0.5, ((0, 4),)),
        "proj_bias": bell_draw(arg_keys[11], (D,), 0.3, 2.0, (), jnp.float32),
        "norm2_gain": jnp.clip(1.0 + 0.1 * jax.random.normal(arg_keys[12], (D,), jnp.float32), 0.5, 1.5),
        "norm2_shift": bell_draw(arg_keys[13], (D,), 0.3, 2.0, (), jnp.float32),
        "fc1_weight": bell_draw(arg_keys[14], (D, FF), D ** -0.5, 0.1875, ((1, 4),)),
        "fc1_bias": bell_draw(arg_keys[15], (FF,), 0.3, 2.0, ((0, 4),), jnp.float32),
        "fc2_weight": bell_draw(arg_keys[16], (FF, D), (FF // 2) ** -0.5, 0.125, ((0, 4),)),
        "fc2_bias": bell_draw(arg_keys[17], (D,), 0.3, 2.0, (), jnp.float32),
        "out_grad": bell_draw(arg_keys[18], (TOKENS, D), 1.0, 6.0, ((0, 8),)),
    }


EPS = 1e-05

@jax.custom_vjp
def low(v):
    return lax.optimization_barrier(v.astype(jnp.bfloat16)).astype(jnp.float32)

@jax.custom_vjp
def low_back(v):
    return v

def low_keep(v):
    return (low(v), None)

def low_pass(kept, grad):
    return (grad,)

def back_keep(v):
    return (v, None)

def back_low(kept, grad):
    return (low(grad),)
low.defvjp(low_keep, low_pass)
low_back.defvjp(back_keep, back_low)

def layer_norm(values, gain, shift):
    average = lax.optimization_barrier(jnp.mean(values, -1, keepdims=True))
    centred = values - average
    spread = lax.optimization_barrier(jnp.mean(centred * centred, -1, keepdims=True))
    return centred * lax.rsqrt(spread + EPS) * gain + shift

def dense(left, right):
    return jnp.dot(left, right, precision=lax.Precision.HIGHEST)

def relative_index():
    positions = jnp.arange(WIN * WIN)
    pos_row = positions // WIN
    pos_col = positions % WIN
    offset = (pos_row[:, None] - pos_row[None, :] + WIN - 1) * (2 * WIN - 1) + pos_col[:, None] - pos_col[None, :] + WIN - 1
    return offset.astype(jnp.int32)

def forward(window_extent, patches, merge_gain, merge_shift, merge_weight, norm1_gain, norm1_shift, qkv_weight, qkv_bias, rel_table, proj_weight, proj_bias, norm2_gain, norm2_shift, fc1_weight, fc1_bias, fc2_weight, fc2_bias):
    flat_in = patches.reshape(TOKENS, 4 * C3)
    merged = low(layer_norm(flat_in, merge_gain, merge_shift))
    resid0 = low_back(dense(merged, merge_weight))
    normed1 = low(layer_norm(resid0, norm1_gain, norm1_shift))
    qkv = low(low_back(dense(normed1, qkv_weight) + qkv_bias))
    qkv_win = qkv.reshape(WINDOWS, WIN * WIN, 3, HEADS, HD)
    bias_heads = jnp.transpose(rel_table[relative_index()], (2, 0, 1))
    positions = jnp.arange(WIN * WIN)
    valid = ((positions // WIN)[None, :] < window_extent[:, 0:1]) & ((positions % WIN)[None, :] < window_extent[:, 1:2])
    block = math.gcd(WINDOWS, 32)
    scale = HD ** (-0.5)

    def attend(inputs):
        piece, keep = inputs
        query = piece[:, :, 0]
        keys = piece[:, :, 1]
        values = piece[:, :, 2]
        raw = jnp.einsum('wqhd,wkhd->whqk', query, keys, precision=lax.Precision.HIGHEST) * scale + bias_heads[None]
        raw = low_back(raw)
        raw = jnp.where(keep[:, None, None, :], raw, -1e+30)
        probs = jax.nn.softmax(raw, axis=-1)
        mixed = jnp.einsum('whqk,wkhd->wqhd', low(probs), values, precision=lax.Precision.HIGHEST)
        return low(low_back(mixed)).reshape(piece.shape[0], WIN * WIN, HEADS * HD)
    blocks = (qkv_win.reshape(WINDOWS // block, block, WIN * WIN, 3, HEADS, HD), valid.reshape(WINDOWS // block, block, WIN * WIN))
    heads_out = lax.map(jax.checkpoint(attend), blocks).reshape(TOKENS, D)
    resid1 = resid0 + low_back(dense(heads_out, proj_weight)) + proj_bias
    normed2 = low(layer_norm(resid1, norm2_gain, norm2_shift))
    pre = low_back(dense(normed2, fc1_weight) + fc1_bias)
    act = low(jax.nn.gelu(pre, approximate=False))
    return resid1 + low_back(dense(act, fc2_weight)) + fc2_bias

def reference(patches, window_extent, merge_gain, merge_shift, merge_weight, norm1_gain, norm1_shift, qkv_weight, qkv_bias, rel_table, proj_weight, proj_bias, norm2_gain, norm2_shift, fc1_weight, fc1_bias, fc2_weight, fc2_bias, out_grad):
    floats = (patches, merge_gain, merge_shift, merge_weight, norm1_gain, norm1_shift, qkv_weight, qkv_bias, rel_table, proj_weight, proj_bias, norm2_gain, norm2_shift, fc1_weight, fc1_bias, fc2_weight, fc2_bias)
    floats = tuple((item.astype(jnp.float32) for item in floats))
    result, pullback = jax.vjp(partial(forward, window_extent), *floats)
    grads = pullback(out_grad.astype(jnp.float32))
    return (result.astype(jnp.bfloat16), grads[0].astype(jnp.bfloat16), grads[1], grads[2], grads[3], grads[4], grads[5], grads[6], grads[7], grads[8], grads[9], grads[10], grads[11], grads[12], grads[13], grads[14], grads[15], grads[16])
```

```python
import functools

import jax
import jax.numpy as jnp
from jax import lax
from jax.experimental import pallas as pl
from jax.experimental.pallas import tpu as pltpu
from jax.sharding import PartitionSpec as P

WIN = 10
WINDOW_TOKENS = WIN * WIN
QUERY_ROWS = 112
KEY_ROWS = 128
EPS = 1e-05
MEBI = 1024 * 1024
PROBS_ROOM = 52
WAIT_US = 100.0
WEIGHT_US = {
    "attend_back": 7.2, "back1": 4.1, "proj_grad": 3.1, "back0": 3.3, "qkv_grad": 5.0, "merge_grad": 4.2,
    "second_join": 2.0, "qkv_join": 1.5,
}
WEIGHT_US |= dict.fromkeys(
    ("pack", "front", "cut", "pieces", "spread", "attend", "mine", "after", "slope", "feed", "second", "fc1_grad",
     "fc2_grad", "fc1_join", "fc2_join", "fc1_join2", "fc2_join2", "back2"), WAIT_US
)
FLOPS_PER_US = 10**9
BF = jnp.bfloat16
F32 = jnp.float32


def normalise(values):
    average = jnp.mean(values, -1, keepdims=True)
    centred = values - average
    inverse = lax.rsqrt(jnp.mean(centred * centred, -1, keepdims=True) + EPS)
    return centred * inverse, inverse


def norm_backward(grad_out, normal, inverse, gain):
    scaled = grad_out * gain
    return inverse * (
        scaled
        - jnp.mean(scaled, -1, keepdims=True)
        - normal * jnp.mean(scaled * normal, -1, keepdims=True)
    )


def matmul(left, right):
    return jnp.dot(left, right, preferred_element_type=jnp.float32)


def contract(left, right, left_dim, right_dim):
    return lax.dot_general(
        left, right, (((left_dim,), (right_dim,)), ((), ())), preferred_element_type=jnp.float32
    )


def low(array):
    return array.astype(BF)


def row(vector):
    return vector.reshape(1, -1)


def stays():
    return pl.BlockSpec(memory_space=pl.ANY)


def outside():
    return pl.BlockSpec(memory_space=pltpu.HBM)


def held():
    return pl.BlockSpec(memory_space=pltpu.VMEM)


def shape_of(shape, dtype):
    return jax.ShapeDtypeStruct(shape, dtype)


def whole(kernel, place, outs, *operands, leave=(), scratch=(), after=(), room=20, name=None):
    arrays = [a for a, _ in operands]
    count, skip = len(arrays), len(after)

    def body(place_ref, *refs):
        kernel(place_ref, *refs[:count], *refs[count + skip :])

    return pl.pallas_call(
        body,
        in_specs=[pl.BlockSpec(memory_space=pltpu.SMEM)]
        + [{True: held, False: outside, None: stays}[inside]() for _, inside in operands]
        + [stays()] * skip,
        out_specs=[outside() if k in leave else held() for k in range(len(outs))],
        out_shape=list(outs),
        scratch_shapes=list(scratch),
        compiler_params=pltpu.CompilerParams(vmem_limit_bytes=room * MEBI),
        cost_estimate=pl.CostEstimate(
            flops=int(WEIGHT_US.get(name, 0.7) * FLOPS_PER_US), bytes_accessed=0, transcendentals=0
        ),
        name=name,
    )(place, *arrays, *after)


def tie(array, *after):
    def body(*refs):
        del refs

    return pl.pallas_call(
        body,
        in_specs=[stays()] * (1 + len(after)),
        out_specs=stays(),
        out_shape=shape_of(array.shape, array.dtype),
        input_output_aliases={0: 0},
        name="tie",
    )(array, *after)


def swap(array, axis, mask):
    size = lax.axis_size(axis)
    return lax.ppermute(array, axis, [(i, i ^ mask) for i in range(size)])


def turn(array, axis, step):
    size = lax.axis_size(axis)
    return lax.ppermute(array, axis, [(i, (i + step) % size) for i in range(size)])


def sum_all(vector):
    mask = 1
    while mask < lax.axis_size("wide"):
        vector = vector + swap(vector, "wide", mask)
        mask *= 2
    mask = 1
    while mask < lax.axis_size("narrow"):
        vector = vector + swap(vector, "narrow", mask)
        mask *= 2
    return vector


def sum_high(parts, high):
    take = lambda index: lax.dynamic_index_in_dim(parts, index, 0, keepdims=False)
    total = take(high).astype(F32)
    for j in range(1, parts.shape[0]):
        total = total + swap(low(take(high ^ j)), "wide", 8 * j).astype(F32)
    return total


def grad_kernel(place_ref, *refs, lefts, rights, block, rows, riding):
    left_refs, right_refs = refs[: len(lefts)], refs[len(lefts) : len(lefts) + len(rights)]
    kept_ref, sent_ref, total_ref = refs[-3:]
    core = place_ref[1]
    if riding:
        give_sums(sent_ref, kept_ref.shape[0], refs[-4][...])

    @pl.loop(0, kept_ref.shape[0])
    def _(step):
        at = pl.ds(pl.multiple_of(step * block, block), block)
        total = None
        for l_ref, l_at, r_ref, r_at in zip(left_refs, lefts, right_refs, rights):
            left = l_ref[:, at] if l_at is None else l_ref[l_at, :, at]
            right = r_ref[: left.shape[0]] if r_at is None else r_ref[r_at]
            right = low(right)
            part = contract(left, right, 0, 0)
            total = part if total is None else total + part
        total_ref[...] = total
        for s in range(block // (2 * rows)):
            mine = pl.multiple_of((2 * s + core) * rows, rows)
            theirs = pl.multiple_of((2 * s + 1 - core) * rows, rows)
            kept_ref[step, s * rows : (s + 1) * rows] = total_ref[pl.ds(mine, rows)]
            sent_ref[step, s * rows : (s + 1) * rows] = low(total_ref[pl.ds(theirs, rows)])


def grad_call(place, lefts, rights, block, rows, name, after=(), sums=None):
    split = lambda item: item if isinstance(item, tuple) else (item, None)
    left_arrays, left_at = zip(*map(split, lefts))
    right_arrays, right_at = zip(*map(split, rights))
    deep, width = left_arrays[0].shape[-1], right_arrays[0].shape[-1]
    shape = (deep // block, block // 2, width)
    return whole(
        functools.partial(
            grad_kernel, lefts=left_at, rights=right_at, block=block, rows=rows,
            riding=sums is not None,
        ),
        place,
        [shape_of(shape, F32), shape_of((shape[0] + (sums is not None), *shape[1:]), BF)],
        *((a, True) for a in left_arrays + right_arrays + (() if sums is None else (sums,))),
        scratch=[pltpu.VMEM((block, width), F32)],
        after=after,
        name=name,
    )


def add_up(refs, lead, rows):
    total = None
    for ref in refs:
        part = ref[lead, rows, :].astype(F32)
        total = part if total is None else total + part
    return total


def join_call(place, groups, outs, name, after=(), sums=None):
    width = groups[0][0].shape[2]
    counts = [len(sources) for sources in groups]
    count = sum(counts)
    rows_of = [pieces[0]((0, 0, 0))[3] for _, pieces in outs]
    more = 2 * sums[0].shape[0] // rows_of[1] if sums else 0
    shapes = [
        shape_of((len(pieces) + (more if k else 0), rows, width), dtype)
        for k, ((dtype, pieces), rows) in enumerate(zip(outs, rows_of))
    ]
    if sums:
        shapes = [shape_of(sums[0].shape, F32)] + shapes

    def kernel(place_ref, *refs):
        place_now = (place_ref[0], place_ref[1], place_ref[2])
        ins, out_refs = refs[:count], refs[count:]
        if sums:
            own_ref, total_ref, out_refs = refs[count], refs[count + 1], refs[count + 2 :]
            total = own_ref[...] + take_sums(ins[counts[0] - 1], sums[1], own_ref.shape[0])
            total_ref[...] = total
        at = [sum(counts[:g]) for g in range(len(counts))]
        for k, (out_ref, (dtype, pieces)) in enumerate(zip(out_refs, outs)):
            for n, piece in enumerate(pieces):
                group, lead, start, rows = piece(place_now)
                if not isinstance(start, int):
                    start = pl.multiple_of(start, rows)
                part = add_up(ins[at[group] : at[group] + counts[group]], lead, pl.ds(start, rows))
                out_ref[n] = part.astype(dtype)
            if sums and k:
                give_sums(out_ref, len(pieces), total)

    arrays = [s for sources in groups for s in sources] + ([sums[0]] if sums else [])
    return whole(
        kernel, place, shapes, *((s, True) for s in arrays), after=after, name=name
    )


def give_sums(ref, first, values):
    high = low(values)
    parts = jnp.concatenate([high, low(values - high.astype(F32))], 0)
    size = ref.shape[1]
    for k in range(parts.shape[0] // size):
        ref[first + k] = parts[k * size : (k + 1) * size]
    rest = parts.shape[0] % size
    if rest:
        ref[first + parts.shape[0] // size, :rest] = parts[parts.shape[0] - rest :]


def take_sums(ref, first, rows):
    size = ref.shape[1]
    blocks = [ref[first + k].astype(F32) for k in range(-(-2 * rows // size))]
    parts = jnp.concatenate(blocks, 0) if len(blocks) > 1 else blocks[0]
    return parts[:rows] + parts[rows : 2 * rows]


def cut_kernel(place_ref, merged_ref, own_ref, sent_ref, onward_ref):
    quad = place_ref[2]
    lanes = own_ref.shape[1]
    take = lambda j: merged_ref[:, pl.ds(pl.multiple_of((quad ^ j) * lanes, lanes), lanes)]
    own_ref[...] = take(0)
    sent_ref[0] = take(2)
    sent_ref[1] = take(3)
    onward_ref[...] = take(1)


def pack_kernel(
    place_ref, proj_ref, table_ref, message_ref
):
    part = proj_ref.shape[0] // 8
    own_heads = table_ref.shape[1]
    room = message_ref.shape[1] // 2
    eighth = place_ref[2] * 2 + place_ref[1]
    message_ref[:part] = proj_ref[pl.ds(pl.multiple_of(eighth * part, part), part), :]
    offsets = table_ref.shape[0]
    table = jnp.concatenate(
        [table_ref[...], jnp.zeros((offsets, 128 - own_heads), F32)], 1
    )
    table = jnp.concatenate([table, jnp.zeros((room - offsets, 128), F32)], 0)
    table = jnp.transpose(table)[:own_heads]
    high = low(table).astype(F32)
    rows = jnp.concatenate([high, table - high], 1)
    spare = message_ref.shape[0] - part - own_heads
    message_ref[part:] = low(jnp.concatenate([rows, jnp.zeros((spare, 2 * room), F32)], 0))


def pieces_kernel(place_ref, *refs, part):
    del place_ref
    for j, ref in enumerate(refs[:-1]):
        refs[-1][j * part : (j + 1) * part] = ref[:part]


def front_kernel(
    place_ref, flat_ref, mg_ref, ms_ref, n1g_ref, n1s_ref, qb_ref, mw_any, qw_any,
    merged_ref, resid0_ref, normed1_ref, qkv_ref, mw_ref, qw_ref, sems,
):
    copy_m = pltpu.make_async_copy(mw_any, mw_ref, sems.at[0])
    copy_q = pltpu.make_async_copy(qw_any, qw_ref, sems.at[1])
    copy_m.start()
    copy_q.start()
    hat, _ = normalise(flat_ref[...].astype(F32))
    merged = low(hat * mg_ref[...] + ms_ref[...])
    merged_ref[...] = merged
    copy_m.wait()
    resid0 = matmul(merged, mw_ref[...])
    resid0_ref[...] = resid0
    hat1, _ = normalise(resid0)
    normed1 = low(hat1 * n1g_ref[...] + n1s_ref[...])
    normed1_ref[...] = normed1
    copy_q.wait()
    qkv_ref[...] = low(matmul(normed1, qw_ref[...]) + qb_ref[...])


def front_call(place, flat, mg, ms, n1g, n1s, qb, mw, qw):
    rows, deep = flat.shape
    width = mw.shape[1]
    return whole(
        front_kernel,
        place,
        [
            shape_of((rows, deep), BF),
            shape_of((rows, width), F32),
            shape_of((rows, width), BF),
            shape_of((rows, 3 * width), BF),
        ],
        (flat, True), (row(mg), True), (row(ms), True), (row(n1g), True), (row(n1s), True),
        (row(qb), True), (mw, False), (qw, False),
        scratch=[
            pltpu.VMEM(mw.shape, BF), pltpu.VMEM(qw.shape, BF), pltpu.SemaphoreType.DMA((2,)),
        ],
        room=28,
        name="front",
    )


def mine_kernel(place_ref, *refs):
    del place_ref
    rows = refs[0].shape[0]
    for q, ref in enumerate(refs[:-1]):
        refs[-1][q * rows : (q + 1) * rows] = ref[...]


def bring_proj(place_ref, own_any, mine_any, theirs_any, proj_ref, sems, groups):
    rank, core, quad = place_ref[0], place_ref[1], place_ref[2]
    shard = own_any.shape[0]
    part = shard // 8

    def bring(source, start, rows, sem):
        at = pl.ds(pl.multiple_of(start, rows), rows)
        copy = pltpu.make_async_copy(source, proj_ref.at[at], sems.at[sem])
        copy.start()
        return copy

    copies = [bring(own_any, rank * shard, shard, 0)]
    for k in range(4 * (groups - 1)):
        q, j = k // (groups - 1), k % (groups - 1)
        base = lax.rem(rank + groups - 1 - j, groups) * shard + (quad ^ q) * 2 * part
        rows = pl.ds(k * part, part)
        copies.append(bring(mine_any.at[rows], base + core * part, part, 1 + 2 * k))
        copies.append(bring(theirs_any.at[rows], base + (1 - core) * part, part, 2 + 2 * k))
    return copies


def after_kernel(
    place_ref, heads_ref, resid0_ref, pb_ref, n2g_ref, n2s_ref, own_any, mine_any, theirs_any,
    resid1_ref, normed2_ref, proj_ref, sems, *, groups,
):
    for copy in bring_proj(place_ref, own_any, mine_any, theirs_any, proj_ref, sems, groups):
        copy.wait()
    resid1 = resid0_ref[...] + matmul(heads_ref[...], proj_ref[...]) + pb_ref[...]
    resid1_ref[...] = resid1
    hat2, _ = normalise(resid1)
    normed2_ref[...] = low(hat2 * n2g_ref[...] + n2s_ref[...])


SQRT_HALF = 0.5**0.5
DENSITY = 0.3989422804014327


def gelu_pair(values):
    below = 0.5 * (1.0 + lax.erf(values * SQRT_HALF))
    density = jnp.exp(-0.5 * values * values) * DENSITY
    return values * below, below + values * density


def slope_kernel(
    place_ref, dy_ref, fc2_ref, rows_ref, own_ref, out_ref, wide_ref, *, groups, pad, chunk
):
    tokens, width = own_ref.shape
    wide_ref[...] = dy_ref[...].astype(F32)
    fill = jnp.zeros((pad - tokens, width), F32)
    for j in range(groups):
        at = lax.rem(place_ref[0] + groups - j, groups) * tokens
        block = wide_ref[pl.ds(pl.multiple_of(at, 8), tokens), :]
        rows_ref[j * pad : (j + 1) * pad] = low(jnp.concatenate([block, fill], 0))
        if j == 0:
            own_ref[...] = low(block)

    @pl.loop(0, fc2_ref.shape[0] // chunk)
    def _(step):
        at = pl.ds(pl.multiple_of(step * chunk, chunk), chunk)
        out_ref[:, at] = contract(rows_ref[...], fc2_ref[at, :], 1, 1)


def feed_kernel(
    place_ref, n0_ref, n1_ref, n2_ref, n3_ref, d_act_ref, fc1_ref, fc1b_ref,
    act_ref, dpre_ref, all_ref, db_ref, o0_ref, o1_ref, o2_ref, o3_ref, *, pad, chunk,
):
    del place_ref
    rows, width = n0_ref.shape
    for j, ref in enumerate((n0_ref, n1_ref, n2_ref, n3_ref)):
        all_ref[j * pad : j * pad + rows, :] = ref[...]
        all_ref[j * pad + rows : (j + 1) * pad, :] = jnp.zeros((pad - rows, width), BF)

    @pl.loop(0, fc1_ref.shape[1] // chunk)
    def _(step):
        at = pl.ds(pl.multiple_of(step * chunk, chunk), chunk)
        pre = matmul(all_ref[...], fc1_ref[:, at]) + fc1b_ref[:, at]
        act, slope = gelu_pair(pre)
        act_ref[:, at] = low(act)
        d_low = low(d_act_ref[:, at] * slope)
        dpre_ref[:, at] = d_low
        db_ref[:, at] = jnp.sum(d_low.astype(F32), 0, keepdims=True)

    for j, ref in enumerate((o0_ref, o1_ref, o2_ref, o3_ref)):
        part = contract(dpre_ref[j * pad : (j + 1) * pad, :], fc1_ref[...], 1, 1)
        ref[...] = low(part[:rows])


def second_kernel(place_ref, act_ref, fc2_ref, kept_ref, sent_ref, *, pad, groups):
    rank = place_ref[0]
    rows = kept_ref.shape[1]
    for ref, k, flip in ((sent_ref, 0, 1), (sent_ref, 1, 3), (kept_ref, 0, 0), (kept_ref, 1, 2)):
        block = lax.rem(rank + groups - (rank ^ flip), groups)
        at = pl.ds(pl.multiple_of(block * pad, pad), pad)
        ref[k] = low(matmul(act_ref[at, :], fc2_ref[...])[:rows])


def back2_kernel(
    place_ref, c0_ref, c1_ref, c2_ref, c3_ref, resid1_ref, dy_ref, n2g_ref, own_any, mine_any, theirs_any,
    dresid1_ref, dheads_ref, proj_ref, sems, *, groups,
):
    copies = bring_proj(place_ref, own_any, mine_any, theirs_any, proj_ref, sems, groups)
    rows = dheads_ref.shape[0]
    d_norm2 = (
        c0_ref[...].astype(F32) + c1_ref[...].astype(F32)
        + c2_ref[...].astype(F32) + c3_ref[...].astype(F32)
    )
    hat2, inv2 = normalise(resid1_ref[...])
    dy = dy_ref[...].astype(F32)
    d_resid1 = dy + norm_backward(d_norm2, hat2, inv2, n2g_ref[...])
    dresid1_ref[:rows] = d_resid1
    sums = (d_resid1, d_norm2 * hat2, d_norm2, dy)
    for k, part in enumerate(sums):
        dresid1_ref[rows + k : rows + k + 1] = jnp.sum(part, 0, keepdims=True)
    for copy in copies:
        copy.wait()
    dheads_ref[...] = low(contract(low(d_resid1), proj_ref[...], 1, 1))


def back1_kernel(
    place_ref, even_ref, odd_ref, dresid1_ref, resid0_ref, n1g_ref, qw_any,
    dresid0_ref, sums_ref, qw_ref, sems,
):
    rows, width = resid0_ref.shape
    quad = place_ref[2]
    lanes = width // 4
    copies = [
        pltpu.make_async_copy(qw_any.at[:, pl.ds(i * width, width)], qw_ref.at[i], sems.at[i])
        for i in range(3)
    ]
    for copy in copies:
        copy.start()
    hat1, inv1 = normalise(resid0_ref[...])
    d_norm1 = jnp.zeros((rows, width), F32)
    for i in range(3):
        copies[i].wait()
        for j in range(4):
            part = (odd_ref if j % 2 else even_ref)[j // 2, :, i * lanes : (i + 1) * lanes]
            at = pl.ds(pl.multiple_of((quad ^ j) * lanes, lanes), lanes)
            d_norm1 = d_norm1 + contract(part, qw_ref[i, :, at], 1, 1)
            sums_ref[2 + i : 3 + i, at] = jnp.sum(part.astype(F32), 0, keepdims=True)
    dresid0_ref[...] = low(
        dresid1_ref[:rows] + norm_backward(d_norm1, hat1, inv1, n1g_ref[...])
    )
    sums_ref[0:1] = jnp.sum(d_norm1 * hat1, 0, keepdims=True)
    sums_ref[1:2] = jnp.sum(d_norm1, 0, keepdims=True)


def back0_kernel(
    place_ref, dresid0_ref, flat_ref, mg_ref, mw_any, grad_ref, sums_ref, mw_ref, sems
):
    del place_ref
    copy = pltpu.make_async_copy(mw_any, mw_ref, sems.at[0])
    copy.start()
    hat, inv = normalise(flat_ref[...].astype(F32))
    copy.wait()
    d_merged = contract(dresid0_ref[...], mw_ref[...], 1, 1)
    grad_ref[...] = low(norm_backward(d_merged, hat, inv, mg_ref[...]))
    width = dresid0_ref.shape[1]
    gain = jnp.sum(d_merged * hat, 0, keepdims=True)
    shift = jnp.sum(d_merged, 0, keepdims=True)
    for i in range(gain.shape[1] // width):
        sums_ref[i : i + 1] = gain[:, i * width : (i + 1) * width]
        sums_ref[2 + i : 3 + i] = shift[:, i * width : (i + 1) * width]


SPAN = 2 * WIN - 1
OFFSETS = 384
STRIP = 256


def strip_picks(column, offsets_first):
    shape, o_dim = ((OFFSETS, STRIP), 0) if offsets_first else ((STRIP, OFFSETS), 1)
    offset = lax.broadcasted_iota(jnp.int32, shape, o_dim)
    lane = lax.broadcasted_iota(jnp.int32, shape, 1 - o_dim)
    wanted = (SPAN - 1 - lane // WIN) * SPAN + column - lane % WIN + WIN - 1
    hit = (offset == wanted) & (lane < SPAN * WIN)
    return jnp.where(hit, 1.0, 0.0).astype(BF)


def split3(values):
    first = low(values)
    rest = values - first.astype(F32)
    second = low(rest)
    third = low(rest - second.astype(F32))
    return first, second, third


def spread_kernel(place_ref, m0_ref, m1_ref, m2_ref, m3_ref, bias_ref, table_ref, *, part, groups):
    heads = table_ref.shape[0]
    own_heads = heads // groups
    room = m0_ref.shape[1] // 2
    for j, ref in enumerate((m0_ref, m1_ref, m2_ref, m3_ref)):
        both = ref[part : part + 2 * own_heads, :].astype(F32)[:own_heads]
        at = pl.multiple_of(lax.rem(place_ref[0] + groups - j, groups) * own_heads, own_heads)
        table_ref[pl.ds(at, own_heads), :] = both[:, :OFFSETS] + both[:, room : room + OFFSETS]
    table = table_ref[...]
    high = low(table)
    table = jnp.concatenate([high, low(table - high.astype(F32))], 0)
    for column in range(WIN):
        parts = matmul(table, strip_picks(column, True))
        strip = parts[:heads] + parts[heads:]
        for r in range(WIN):
            start = (WIN - 1 - r) * WIN
            at = (r * WIN + column) * heads
            bias_ref[at : at + heads, :] = strip[:, start : start + KEY_ROWS]
    bias_ref[WINDOW_TOKENS * heads :, :] = jnp.zeros(
        ((QUERY_ROWS - WINDOW_TOKENS) * heads, KEY_ROWS), F32
    )


def fold(grad_ref, heads):
    total = jnp.zeros((3 * heads, OFFSETS), F32)
    for column in range(WIN):
        strip = jnp.zeros((heads, STRIP), F32)
        for r in range(WIN):
            start = (WIN - 1 - r) * WIN
            at = (r * WIN + column) * heads
            part = grad_ref[at : at + heads, :]
            wide = jnp.concatenate([part, jnp.zeros((heads, STRIP - KEY_ROWS), F32)], 1)
            strip = strip + (pltpu.roll(wide, start, 1) if start else wide)
        total = total + matmul(jnp.concatenate(split3(strip), 0), strip_picks(column, False))
    return total[:heads] + total[heads : 2 * heads] + total[2 * heads :]


def window_rows(values, window, rows):
    part = values.astype(F32)[window * WINDOW_TOKENS : (window + 1) * WINDOW_TOKENS]
    zeros = jnp.zeros((rows - WINDOW_TOKENS, part.shape[1]), F32)
    return low(jnp.concatenate([part, zeros], 0))


def stack_heads(part, heads, head_dim):
    lane = lax.broadcasted_iota(jnp.int32, part.shape, 1) // head_dim
    zero = jnp.zeros_like(part)
    return jnp.concatenate([jnp.where(lane == h, part, zero) for h in range(heads)], 0)


def attend_kernel(
    place_ref, qkv_ref, bias_ref, mask_ref, out_ref, probs_any, probs_ref, sems, *, windows, head_dim
):
    del place_ref
    width = out_ref.shape[1]
    lanes = width // 4

    def keep(step):
        return pltpu.make_async_copy(probs_ref.at[step], probs_any.at[step], sems.at[step])

    @pl.loop(0, 4)
    def _(step):
        attend_group(
            step, qkv_ref, bias_ref, mask_ref, out_ref, probs_ref, windows, head_dim, width, lanes
        )
        keep(step).start()

    for step in range(4):
        keep(step).wait()


def attend_group(
    step, qkv_ref, bias_ref, mask_ref, out_ref, probs_ref, windows, head_dim, width, lanes
):
    heads, all_heads = lanes // head_dim, width // head_dim
    first = step * heads
    scale = head_dim ** (-0.5)
    at = lambda kind: pl.ds(pl.multiple_of(kind * width + step * lanes, lanes), lanes)
    q_all, k_all, v_all = (qkv_ref[:, at(kind)] for kind in range(3))
    outs = []
    for w in range(windows):
        query = window_rows(q_all, w, QUERY_ROWS)
        keys = stack_heads(window_rows(k_all, w, KEY_ROWS), heads, head_dim)
        values = stack_heads(window_rows(v_all, w, KEY_ROWS), heads, head_dim)
        scores = contract(query, keys, 1, 1) * scale
        mask = mask_ref[w]
        rounded = []
        for h in range(heads):
            bias = bias_ref[pl.ds(first + h, QUERY_ROWS, stride=all_heads), :]
            raw = scores[:, h * KEY_ROWS : (h + 1) * KEY_ROWS] + bias + mask
            expo = jnp.exp(raw - jnp.max(raw, -1, keepdims=True))
            probs = expo / jnp.sum(expo, -1, keepdims=True)
            probs_ref[step, w, h] = probs
            rounded.append(low(probs))
        mixed = matmul(jnp.concatenate(rounded, 1), values)
        outs.append(mixed[:WINDOW_TOKENS])
    out_ref[:, at(0)] = low(jnp.concatenate(outs, 0))


def attend_back_kernel(
    place_ref, qkv_ref, grad_ref, probs_any, even_ref, odd_ref, table_ref, dbias_ref, probs_ref, sems,
    *, windows, head_dim
):
    width = grad_ref.shape[1]

    def fetch(step):
        return pltpu.make_async_copy(
            probs_any.at[place_ref[2] ^ step], probs_ref.at[step], sems.at[step]
        )

    for step in range(4):
        fetch(step).start()

    @pl.loop(0, 4)
    def _(step):
        fetch(step).wait()
        attend_back_group(
            place_ref[2] ^ step, step, qkv_ref, grad_ref, probs_ref, even_ref, odd_ref, dbias_ref,
            windows, head_dim, width, width // 4,
        )

    table_ref[...] = fold(dbias_ref, table_ref.shape[0])


def attend_back_group(
    group, step, qkv_ref, grad_ref, probs_ref, even_ref, odd_ref, dbias_ref,
    windows, head_dim, width, lanes,
):
    heads, all_heads = lanes // head_dim, width // head_dim
    first = group * heads
    scale = head_dim ** (-0.5)
    at = lambda kind: pl.ds(pl.multiple_of(kind * width + group * lanes, lanes), lanes)
    q_all, k_all, v_all = (qkv_ref[:, at(kind)] for kind in range(3))
    g_all = grad_ref[:, at(0)]
    all_q, all_k, all_v = [], [], []
    d_first = []
    for w in range(windows):
        query = stack_heads(window_rows(q_all, w, QUERY_ROWS), heads, head_dim)
        keys = stack_heads(window_rows(k_all, w, KEY_ROWS), heads, head_dim)
        values = stack_heads(window_rows(v_all, w, KEY_ROWS), heads, head_dim)
        plain = window_rows(g_all, w, QUERY_ROWS)
        grad = stack_heads(plain, heads, head_dim)
        d_probs = contract(plain, values, 1, 1)
        d_list, p_list = [], []
        for h in range(heads):
            probs = probs_ref[step, w, h]
            part = d_probs[:, h * KEY_ROWS : (h + 1) * KEY_ROWS]
            total = jnp.sum(part * probs, -1, keepdims=True)
            d_scores = low(probs * (part - total))
            d_list.append(d_scores)
            p_list.append(low(probs))
            if w == 0:
                d_first.append(d_scores.astype(F32))
            else:
                d_first[h] = d_first[h] + d_scores.astype(F32)
            if w == windows - 1:
                dbias_ref[pl.ds(first + h, QUERY_ROWS, stride=all_heads), :] = d_first[h]
        d_query = matmul(jnp.concatenate(d_list, 1), keys) * scale
        d_keys = contract(jnp.concatenate(d_list, 0), query, 0, 0) * scale
        d_values = contract(jnp.concatenate(p_list, 0), grad, 0, 0)
        all_q.append(d_query[:WINDOW_TOKENS])
        all_k.append(d_keys[:WINDOW_TOKENS])
        all_v.append(d_values[:WINDOW_TOKENS])
    result = jnp.concatenate(
        [low(jnp.concatenate(parts, 0)) for parts in (all_q, all_k, all_v)], 1
    )

    @pl.when(step % 2 == 0)
    def _():
        even_ref[step // 2] = result

    @pl.when(step % 2 == 1)
    def _():
        odd_ref[step // 2] = result


def spots(heads, lines, vectors):
    columns = 3
    return [(k // columns, OFFSETS + 128 * (k % columns)) for k in range(vectors * lines)]


def collect_kernel(place_ref, s0_ref, s1_ref, d_ref, rel_ref, b_ref, out_ref):
    heads = rel_ref.shape[0]
    lines = s0_ref.shape[1] // 128
    out_ref[...] = jnp.zeros(out_ref.shape, F32)
    out_ref[:heads, :OFFSETS] = rel_ref[...]
    vectors = [ref[r : r + 1, :] for ref in (s0_ref, s1_ref) for r in range(ref.shape[0])]
    after = d_ref.shape[0] - 8
    vectors += [d_ref[after + r : after + r + 1, :] for r in range(4)]
    for k, (at, lane) in enumerate(spots(heads, lines, len(vectors))):
        piece = vectors[k // lines][:, 128 * (k % lines) : 128 * (k % lines + 1)]
        out_ref[at : at + 1, lane : lane + 128] = piece
    own = b_ref.shape[1] // 128
    first = heads + pl.multiple_of((place_ref[0] // 2) * own, own)
    block = jnp.concatenate([b_ref[:, k * 128 : (k + 1) * 128] for k in range(own)], 0)
    side = place_ref[0] % 2

    @pl.when(side == 0)
    def _():
        out_ref[pl.ds(first, own), 0:128] = block

    @pl.when(side == 1)
    def _():
        out_ref[pl.ds(first, own), 128:256] = block


def deliver_kernel(place_ref, all_ref, sums_ref, rel_ref, b_ref):
    heads = rel_ref.shape[0]
    vectors, width = sums_ref.shape
    lines = width // 128
    rel_ref[...] = all_ref[:heads, :OFFSETS]
    for k, (at, lane) in enumerate(spots(heads, lines, vectors)):
        sums_ref[k // lines : k // lines + 1, 128 * (k % lines) : 128 * (k % lines + 1)] = all_ref[
            at : at + 1, lane : lane + 128
        ]
    own = b_ref.shape[0]
    first = heads + pl.multiple_of((place_ref[0] // 2) * own, own)
    side = place_ref[0] % 2

    @pl.when(side == 0)
    def _():
        b_ref[...] = all_ref[pl.ds(first, own), 0:128]

    @pl.when(side == 1)
    def _():
        b_ref[...] = all_ref[pl.ds(first, own), 128:256]


def columns_kernel(place_ref, b0_ref, b1_ref, b2_ref, b3_ref, own_ref, out_ref, sums_ref):
    rows = out_ref.shape[0]
    lanes = b0_ref.shape[2] // 3
    total = own_ref[...]
    for j, ref in enumerate((b0_ref, b1_ref, b2_ref, b3_ref)):
        for part in range(3):
            at = pl.multiple_of((part * 4 + (place_ref[2] ^ j)) * lanes, lanes)
            out_ref[:, pl.ds(at, lanes)] = ref[0, :rows, part * lanes : (part + 1) * lanes].astype(F32)
        if j:
            total = total + take_sums(ref, 1, own_ref.shape[0])
    sums_ref[...] = total


def on_device(
    patches,
    window_extent,
    merge_gain,
    merge_shift,
    merge_weight,
    norm1_gain,
    norm1_shift,
    qkv_weight,
    qkv_bias,
    rel_table,
    proj_weight,
    proj_bias,
    norm2_gain,
    norm2_shift,
    fc1_weight,
    fc1_bias,
    fc2_weight,
    fc2_bias,
    out_grad,
):
    groups, wide = lax.axis_size("narrow"), lax.axis_size("wide")
    devices = wide * groups
    highs = wide // 8
    wide_at, rank = lax.axis_index("wide"), lax.axis_index("narrow")
    core, quad, high = wide_at % 2, (wide_at // 2) % 4, wide_at // 8
    place = jnp.stack([rank, core, quad]).astype(jnp.int32)
    tokens = patches.shape[0]
    width = qkv_weight.shape[0]
    own_heads = rel_table.shape[1]
    heads = own_heads * groups
    head_dim = width // heads
    windows = tokens // WINDOW_TOKENS
    pad = tokens + (-tokens) % 16

    def arrange(array, order):
        if highs == 1:
            return array
        sizes = {"h": highs, "q": 4, "c": 2, "n": groups}
        cut = [sizes[k] for k in order]
        rest = array.shape[1]
        for size in cut:
            rest //= size
        at = order.index("h") + 1
        moved = [i + 1 for i in range(len(order)) if i + 1 != at] + [at, len(order) + 1]
        return jnp.transpose(array.reshape(-1, *cut, rest), [0] + moved).reshape(array.shape)

    def settle(array):
        if highs == 1:
            return array[0]
        return sum_high(array[0].reshape(highs, -1, array.shape[2]), high)

    part = proj_weight.shape[0] // 8
    message = whole(
        pack_kernel,
        place,
        [shape_of((part + own_heads + (-(part + own_heads)) % 16, width), BF)],
        (proj_weight, True),
        (rel_table, True),
        name="pack",
    )[0]
    messages = [turn(message, "narrow", step) for step in range(1, groups)]

    flat = patches.reshape(tokens, -1)
    merged, resid0, normed1, qkv = front_call(
        place, flat, merge_gain, merge_shift, norm1_gain, norm1_shift, qkv_bias,
        merge_weight, qkv_weight,
    )
    mine = whole(
        functools.partial(pieces_kernel, part=part),
        place,
        [shape_of(((groups - 1) * part, width), BF)],
        *((m, True) for m in messages),
        name="pieces",
    )
    mine = list(mine) + [swap(mine[0], "wide", 2 * j) for j in (1, 2, 3)]

    merged_own, merged_sent, merged_onward = whole(
        cut_kernel,
        place,
        [
            shape_of((tokens, merged.shape[1] // 4), BF),
            shape_of((2, tokens, merged.shape[1] // 4), BF),
            shape_of((tokens, merged.shape[1] // 4), BF),
        ],
        (arrange(merged, "hqcn"), True),
        name="cut",
    )
    merged_near = swap(merged_sent, "wide", 4)
    normed1_cut = arrange(normed1, "hqcn")
    normed1_near = swap(normed1_cut, "wide", 2)

    positions = jnp.arange(KEY_ROWS)
    extent = lax.dynamic_slice_in_dim(window_extent, rank * windows, windows, 0)
    valid = (
        (positions[None, :] // WIN < extent[:, 0:1])
        & (positions[None, :] % WIN < extent[:, 1:2])
        & (positions[None, :] < WINDOW_TOKENS)
    )
    mask = jnp.where(valid, 0.0, -1e30).astype(F32)[:, None, :]
    bias = whole(
        functools.partial(spread_kernel, part=part, groups=groups),
        place,
        [shape_of((QUERY_ROWS * heads, KEY_ROWS), F32)],
        (message, True),
        *((m, True) for m in messages),
        scratch=[pltpu.VMEM((heads, OFFSETS), F32)],
        name="spread",
    )[0]
    heads_out, probs = whole(
        functools.partial(attend_kernel, windows=windows, head_dim=head_dim),
        place,
        [
            shape_of((tokens, width), BF),
            shape_of((PROBS_ROOM, windows, heads // 4, QUERY_ROWS, KEY_ROWS), F32),
        ],
        (qkv, True), (bias, True), (mask, True),
        leave=(1,),
        scratch=[
            pltpu.VMEM((4, windows, heads // 4, QUERY_ROWS, KEY_ROWS), F32),
            pltpu.SemaphoreType.DMA((4,)),
        ],
        name="attend",
    )

    mine = whole(
        mine_kernel,
        place,
        [shape_of((4 * mine[0].shape[0], width), BF)],
        *((m, True) for m in mine),
        after=(heads_out, merged_near, normed1_near),
        name="mine",
    )[0]
    theirs = swap(mine, "wide", 1)
    resid1, normed2 = whole(
        functools.partial(after_kernel, groups=groups),
        place,
        [shape_of((tokens, width), F32), shape_of((tokens, width), BF)],
        (heads_out, True), (resid0, True),
        (row(proj_bias), True), (row(norm2_gain), True), (row(norm2_shift), True),
        (proj_weight, None), (mine, None), (theirs, None),
        scratch=[pltpu.VMEM((width, width), BF), pltpu.SemaphoreType.DMA((1 + 8 * (groups - 1),))],
        name="after",
    )
    blocks = [normed2] + [turn(normed2, "narrow", step) for step in range(1, groups)]

    merged_onward = jnp.stack([tie(merged_onward, normed2), merged_near[1]])
    merged_far = swap(merged_onward, "wide", 2)
    normed1_both = jnp.stack([normed1_cut, tie(normed1_near, normed2)])
    normed1_far = swap(normed1_both, "wide", 4)

    total, units = groups * pad, fc1_weight.shape[1]
    dy_rows, dy_own, d_act = whole(
        functools.partial(slope_kernel, groups=groups, pad=pad, chunk=256),
        place,
        [
            shape_of((total, width), BF),
            shape_of((tokens, width), BF),
            shape_of((total, units), F32),
        ],
        (out_grad, True), (fc2_weight, True),
        scratch=[pltpu.VMEM(out_grad.shape, F32)],
        after=(normed2,),
        name="slope",
    )
    act, d_pre, rows_all, fc1_b_grad, *chunks = whole(
        functools.partial(feed_kernel, pad=pad, chunk=256),
        place,
        [
            shape_of((total, units), BF),
            shape_of((total, units), BF),
            shape_of((total, width), BF),
            shape_of((1, units), F32),
        ]
        + [shape_of((tokens, width), BF)] * 4,
        *((b, True) for b in blocks), (d_act, True), (fc1_weight, True), (row(fc1_bias), True),
        after=(normed1_far, merged_far),
        name="feed",
    )
    arrived = [chunks[0]] + [turn(chunks[j], "narrow", -j) for j in range(1, groups)]

    fc1_kept, fc1_sent = grad_call(place, [arrange(rows_all, "hqc")], [d_pre], 256, 128, "fc1_grad")
    fc2_kept, fc2_sent = grad_call(place, [arrange(act, "hqc")], [dy_rows], 256, 128, "fc2_grad")
    fc1_come, fc2_come = swap(fc1_sent, "wide", 1), swap(fc2_sent, "wide", 1)
    fc1_kept, fc1_sent = join_call(
        place, [(fc1_kept, fc1_come)],
        [
            (F32, [lambda p, y=y: (0, 2 * y + p[2] % 2, 0, 128) for y in range(2)]),
            (BF, [lambda p, y=y: (0, 2 * y + 1 - p[2] % 2, 0, 128) for y in range(2)]),
        ],
        "fc1_join",
    )
    fc2_kept, fc2_sent = join_call(
        place, [(fc2_kept, fc2_come)],
        [
            (F32, [lambda p, x=x: (0, 2 * (p[2] // 2) + x, 0, 128) for x in range(2)]),
            (BF, [lambda p, x=x: (0, 2 * (1 - p[2] // 2) + x, 0, 128) for x in range(2)]),
        ],
        "fc2_join",
    )
    fc1_come, fc2_come = swap(fc1_sent, "wide", 2), swap(fc2_sent, "wide", 4)
    fc1_kept, fc1_sent = join_call(
        place, [(fc1_kept, fc1_come)],
        [
            (F32, [lambda p: (0, p[2] // 2, 0, 128)]),
            (BF, [lambda p: (0, 1 - p[2] // 2, 0, 128)]),
        ],
        "fc1_join2",
    )
    fc2_kept, fc2_sent = join_call(
        place, [(fc2_kept, fc2_come)],
        [
            (F32, [lambda p: (0, p[2] % 2, 0, 128)]),
            (BF, [lambda p: (0, 1 - p[2] % 2, 0, 128)]),
        ],
        "fc2_join2",
    )
    fc1_come, fc2_come = swap(fc1_sent, "wide", 4), swap(fc2_sent, "wide", 2)
    fc1_out = settle(fc1_kept + fc1_come.astype(F32))
    fc2_out = settle(fc2_kept + fc2_come.astype(F32))

    second_kept, second_sent = whole(
        functools.partial(second_kernel, pad=pad, groups=groups),
        place,
        [shape_of((2, tokens, width), BF)] * 2,
        (act, True),
        (fc2_weight, True),
        name="second",
    )
    d_resid1, d_heads = whole(
        functools.partial(back2_kernel, groups=groups),
        place,
        [shape_of((tokens + 8, width), F32), shape_of((tokens, width), BF)],
        *((a, True) for a in arrived),
        (resid1, True), (dy_own, True), (row(norm2_gain), True),
        (proj_weight, None), (mine, None), (theirs, None),
        scratch=[pltpu.VMEM((width, width), BF), pltpu.SemaphoreType.DMA((1 + 8 * (groups - 1),))],
        after=(fc1_sent, fc2_sent, second_sent),
        name="back2",
    )
    second_come = swap(tie(second_sent, d_heads), "narrow", 1)
    d_even, d_odd, rel_part = whole(
        functools.partial(attend_back_kernel, windows=windows, head_dim=head_dim),
        place,
        [shape_of((2, tokens, 3 * width // 4), BF)] * 2 + [shape_of((heads, OFFSETS), F32)],
        (qkv, True), (d_heads, True), (probs, False),
        scratch=[
            pltpu.VMEM((QUERY_ROWS * heads, KEY_ROWS), F32),
            pltpu.VMEM((4, *probs.shape[1:]), F32),
            pltpu.SemaphoreType.DMA((4,)),
        ],
        name="attend_back",
    )
    d_near = swap(d_odd, "wide", 2)

    d_resid0, sums1 = whole(
        back1_kernel,
        place,
        [shape_of((tokens, width), BF), shape_of((5, width), F32)],
        (d_even, True), (d_odd, True), (d_resid1, True), (resid0, True),
        (row(norm1_gain), True), (qkv_weight, False),
        room=56,
        scratch=[pltpu.VMEM((3, width, width), BF), pltpu.SemaphoreType.DMA((3,))],
        after=(fc1_come, fc2_come),
        name="back1",
    )
    r_near = swap(d_resid0, "wide", 4)
    proj_kept, proj_sent = grad_call(
        place, [arrange(heads_out, "nhqc")], [d_resid1], 256, 32, "proj_grad", after=(d_resid0,)
    )
    proj_come = swap(proj_sent, "wide", 1)
    d_onward = jnp.stack([d_even[1], d_near[1]])
    d_far = swap(d_onward, "wide", 4)
    r_both = jnp.stack([d_resid0, r_near])
    r_far = swap(r_both, "wide", 2)

    d_flat, sums0 = whole(
        back0_kernel,
        place,
        [shape_of(flat.shape, BF), shape_of((2 * flat.shape[1] // width, width), F32)],
        (d_resid0, True), (flat, True), (row(merge_gain), True), (merge_weight, False),
        scratch=[pltpu.VMEM(merge_weight.shape, BF), pltpu.SemaphoreType.DMA((1,))],
        after=(d_onward, r_both),
        name="back0",
    )
    patches_grad = d_flat.reshape(patches.shape)

    second_own, second_sent = join_call(
        place, [(second_kept, second_come)],
        [(F32, [lambda p: (0, 0, 0, tokens)]), (BF, [lambda p: (0, 1, 0, tokens)])],
        "second_join",
        after=(d_onward, r_both),
    )
    second_come = swap(second_sent, "narrow", 2)

    own_sums = whole(
        collect_kernel,
        place,
        [shape_of((48, 3 * width // 4), F32)],
        (sums0, True), (sums1, True), (d_resid1, True), (rel_part, True), (fc1_b_grad, True),
        name="collect",
    )[0]
    qkv_kept, qkv_sent = grad_call(
        place,
        [normed1_cut, (normed1_both, 1), (normed1_far, 0), (normed1_far, 1)],
        [(d_even, 0), (d_near, 0), (d_far, 0), (d_far, 1)],
        256, 128, "qkv_grad", sums=own_sums, after=(second_sent,),
    )
    qkv_come = swap(qkv_sent, "wide", 1)
    merge_kept, merge_sent = grad_call(
        place,
        [merged_own, (merged_near, 0), (merged_far, 0), (merged_far, 1)],
        [d_resid0, (r_both, 1), (r_far, 0), (r_far, 1)],
        merged_own.shape[1], merged_own.shape[1] // 2, "merge_grad", after=(qkv_sent,),
    )
    merge_come = swap(merge_sent, "wide", 1)

    side = lambda pick_x: [
        lambda p, n=n, y=y: (0, n, (2 * y + pick_x(p[2] % 2)) * 32, 32)
        for n in range(groups) for y in range(2)
    ]
    proj_kept, proj_sent = join_call(
        place, [(proj_kept, proj_come)],
        [(F32, side(lambda x: x)), (BF, side(lambda x: 1 - x))],
        "proj_join",
        after=(qkv_sent,),
    )
    proj_come = swap(proj_sent, "wide", 2)

    rows = 128 // groups
    qkv_pieces = lambda flip: [
        lambda p, g=g, k=k: (0, g, (2 * k + (p[0] + flip) % 2) * rows, rows)
        for k in range(2) for g in range(4)
    ]
    own_sums, qkv_kept, qkv_sent = join_call(
        place, [(qkv_kept, qkv_come)], [(F32, qkv_pieces(0)), (BF, qkv_pieces(1))], "qkv_join",
        sums=(own_sums, 4),
    )
    qkv_come = swap(qkv_sent, "narrow", 1)

    merge_rows = merged_own.shape[1] // 2 // groups
    merge_pieces = lambda flip: [
        lambda p, k=k: (0, 0, (2 * k + (p[0] + flip) % 2) * merge_rows, merge_rows)
        for k in range(2)
    ]
    merge_kept, merge_sent = join_call(
        place, [(merge_kept, merge_come)],
        [(F32, merge_pieces(0)), (BF, merge_pieces(1))],
        "merge_join",
        after=(qkv_sent,),
    )
    merge_come = swap(merge_sent, "narrow", 1)

    second_pieces = lambda flip: [
        lambda p, g=g: (0, ((p[0] // 2 + flip) % 2) * 4 + g, 0, rows) for g in range(4)
    ]
    own_sums, qkv_kept, qkv_sent = join_call(
        place, [(qkv_kept, qkv_come)],
        [(F32, second_pieces(0)), (BF, second_pieces(1))],
        "qkv_join2",
        sums=(own_sums, 8),
    )
    qkv_come = swap(qkv_sent, "narrow", 2)
    last_pieces = lambda flip, size: [lambda p: (0, (p[0] // 2 + flip) % 2, 0, size)]
    merge_kept, merge_sent = join_call(
        place, [(merge_kept, merge_come)],
        [(F32, last_pieces(0, merge_rows)), (BF, last_pieces(1, merge_rows))],
        "merge_join2",
        after=(qkv_sent,),
    )
    merge_come = swap(merge_sent, "narrow", 2)

    proj_kept, proj_sent = join_call(
        place, [(proj_kept, proj_come)],
        [
            (F32, [lambda p, n=n: (0, 2 * n + p[2] // 2, 0, 32) for n in range(groups)]),
            (BF, [lambda p, n=n: (0, 2 * n + 1 - p[2] // 2, 0, 32) for n in range(groups)]),
        ],
        "proj_join2",
        after=(qkv_sent,),
    )
    proj_come = swap(proj_sent, "wide", 4)
    proj_pieces = lambda flip: [
        lambda p, k=k: (0, 2 * k + (p[0] + flip) % 2, 0, 32) for k in range(2)
    ]
    proj_kept, proj_sent = join_call(
        place, [(proj_kept, proj_come)], [(F32, proj_pieces(0)), (BF, proj_pieces(1))],
        "proj_join3",
    )
    proj_come = swap(proj_sent, "narrow", 1)
    proj_kept, proj_sent = join_call(
        place, [(proj_kept, proj_come)],
        [(F32, last_pieces(0, 32)), (BF, last_pieces(1, 32))],
        "proj_join4",
    )
    proj_come = swap(proj_sent, "narrow", 2)

    own_sums, *cuts = join_call(
        place, [(qkv_kept, qkv_come)],
        [(BF, [lambda p, j=j: (0, p[2] ^ j, 0, rows)]) for j in range(4)],
        "qkv_join3",
        sums=(own_sums, 4),
    )
    cuts = [cuts[0]] + [swap(cuts[j], "wide", 2 * j) for j in (1, 2, 3)]
    qkv_out, all_sums = whole(
        columns_kernel,
        place,
        [shape_of((rows, 3 * width), F32), shape_of(own_sums.shape, F32)],
        *((c, True) for c in cuts), (own_sums, True),
        name="columns",
    )
    qkv_out = settle(qkv_out[None])
    mask = 8
    while mask < wide:
        all_sums = all_sums + swap(all_sums, "wide", mask)
        mask *= 2
    merge_out = settle(merge_kept + merge_come.astype(F32))
    proj_out = settle(proj_kept + proj_come.astype(F32))

    output = low(resid1 + row(fc2_bias) + second_own[0] + second_come[0].astype(F32))

    sums, rel_sum, fc1_b_mine = whole(
        deliver_kernel,
        place,
        [
            shape_of((13, width), F32),
            shape_of((heads, OFFSETS), F32),
            shape_of((units // 128, 128), F32),
        ],
        (all_sums, True),
        name="deliver",
    )
    rel_grad = jnp.transpose(rel_sum[:, : rel_table.shape[0]])
    fc1_b_out = lax.dynamic_index_in_dim(
        fc1_b_mine.reshape(wide, -1), wide_at, 0, keepdims=False
    )

    return (
        output,
        patches_grad,
        sums[0:2].reshape(-1),
        sums[2:4].reshape(-1),
        merge_out,
        sums[4],
        sums[5],
        qkv_out,
        sums[6:9].reshape(-1),
        rel_grad,
        proj_out,
        sums[9],
        sums[10],
        sums[11],
        fc1_out,
        fc1_b_out,
        fc2_out,
        sums[12],
    )


def solution(mesh):
    in_specs = (
        P(("wide", "narrow"), None, None),
        P("wide", None),
        P(),
        P(),
        P(),
        P(),
        P(),
        P(),
        P(),
        P(None, "narrow"),
        P("narrow", None),
        P(),
        P(),
        P(),
        P(None, "narrow"),
        P("narrow"),
        P("narrow", None),
        P(),
        P("wide", None),
    )
    out_specs = (
        P(("wide", "narrow"), None),
        P(("wide", "narrow"), None, None),
        P(),
        P(),
        P(("wide", "narrow"), None),
        P(),
        P(),
        P(("wide", "narrow"), None),
        P(),
        P(),
        P(("narrow", "wide"), None),
        P(),
        P(),
        P(),
        P("wide", "narrow"),
        P(("narrow", "wide")),
        P(("narrow", "wide"), None),
        P(),
    )
    return jax.shard_map(
        on_device, mesh=mesh, in_specs=in_specs, out_specs=out_specs, check_vma=False
    )
```

```python
import functools

import jax
import jax.numpy as jnp
from jax import lax
from jax.experimental import pallas as pl
from jax.experimental.pallas import tpu as pltpu
from jax.sharding import PartitionSpec as P

WIN = 10
WINDOW_TOKENS = WIN * WIN
QUERY_ROWS = 112
KEY_ROWS = 128
EPS = 1e-05
MEBI = 1024 * 1024
PROBS_ROOM = 52
WAIT_US = 100.0
WEIGHT_US = {"back1": 20, "proj_grad": 20, "back0": 20, "second_join": 20, "proj_join": 20}
WEIGHT_US |= dict.fromkeys(
    ("pack", "front", "cut", "pieces", "spread", "attend", "mine", "after", "slope", "feed", "second", "fc1_grad",
     "fc2_grad", "fc1_join", "fc2_join", "fc1_join2", "fc2_join2"), WAIT_US
)
FLOPS_PER_US = 10**9
BF = jnp.bfloat16
F32 = jnp.float32


def normalise(values):
    average = jnp.mean(values, -1, keepdims=True)
    centred = values - average
    inverse = lax.rsqrt(jnp.mean(centred * centred, -1, keepdims=True) + EPS)
    return centred * inverse, inverse


def norm_backward(grad_out, normal, inverse, gain):
    scaled = grad_out * gain
    return inverse * (
        scaled
        - jnp.mean(scaled, -1, keepdims=True)
        - normal * jnp.mean(scaled * normal, -1, keepdims=True)
    )


def matmul(left, right):
    return jnp.dot(left, right, preferred_element_type=jnp.float32)


def contract(left, right, left_dim, right_dim):
    return lax.dot_general(
        left, right, (((left_dim,), (right_dim,)), ((), ())), preferred_element_type=jnp.float32
    )


def low(array):
    return array.astype(BF)


def row(vector):
    return vector.reshape(1, -1)


def stays():
    return pl.BlockSpec(memory_space=pl.ANY)


def outside():
    return pl.BlockSpec(memory_space=pltpu.HBM)


def held():
    return pl.BlockSpec(memory_space=pltpu.VMEM)


def shape_of(shape, dtype):
    return jax.ShapeDtypeStruct(shape, dtype)


def whole(
    kernel, place, outs, *operands, leave=(), scratch=(), after=(), through=(), room=20, name=None
):
    arrays = [a for a, _ in operands]
    count, skip, given = len(arrays), len(after) + len(through), len(outs)

    def body(place_ref, *refs):
        own_outs = refs[count + skip : count + skip + given]
        kernel(place_ref, *refs[:count], *own_outs, *refs[count + skip + given + len(through) :])

    return pl.pallas_call(
        body,
        in_specs=[pl.BlockSpec(memory_space=pltpu.SMEM)]
        + [{True: held, False: outside, None: stays}[inside]() for _, inside in operands]
        + [stays()] * skip,
        out_specs=[outside() if k in leave else held() for k in range(given)]
        + [stays()] * len(through),
        out_shape=list(outs) + [shape_of(a.shape, a.dtype) for a in through],
        input_output_aliases={1 + count + len(after) + k: given + k for k in range(len(through))},
        scratch_shapes=list(scratch),
        compiler_params=pltpu.CompilerParams(vmem_limit_bytes=room * MEBI),
        cost_estimate=pl.CostEstimate(
            flops=int(WEIGHT_US.get(name, 5) * FLOPS_PER_US), bytes_accessed=0, transcendentals=0
        ),
        name=name,
    )(place, *arrays, *after, *through)


def tie(array, *after):
    def body(*refs):
        del refs

    return pl.pallas_call(
        body,
        in_specs=[stays()] * (1 + len(after)),
        out_specs=stays(),
        out_shape=shape_of(array.shape, array.dtype),
        input_output_aliases={0: 0},
        name="tie",
    )(array, *after)


def swap(array, axis, mask):
    size = lax.axis_size(axis)
    return lax.ppermute(array, axis, [(i, i ^ mask) for i in range(size)])


def turn(array, axis, step):
    size = lax.axis_size(axis)
    return lax.ppermute(array, axis, [(i, (i + step) % size) for i in range(size)])


def sum_all(vector):
    mask = 1
    while mask < lax.axis_size("wide"):
        vector = vector + swap(vector, "wide", mask)
        mask *= 2
    mask = 1
    while mask < lax.axis_size("narrow"):
        vector = vector + swap(vector, "narrow", mask)
        mask *= 2
    return vector


def sum_high(parts, high):
    take = lambda index: lax.dynamic_index_in_dim(parts, index, 0, keepdims=False)
    total = take(high).astype(F32)
    for j in range(1, parts.shape[0]):
        total = total + swap(low(take(high ^ j)), "wide", 8 * j).astype(F32)
    return total


def grad_kernel(place_ref, *refs, lefts, rights, block, rows, riding):
    left_refs, right_refs = refs[: len(lefts)], refs[len(lefts) : len(lefts) + len(rights)]
    kept_ref, sent_ref, total_ref = refs[-3:]
    core = place_ref[1]
    if riding:
        give_sums(sent_ref, kept_ref.shape[0], refs[-4][...])

    @pl.loop(0, kept_ref.shape[0])
    def _(step):
        at = pl.ds(pl.multiple_of(step * block, block), block)
        total = None
        for l_ref, l_at, r_ref, r_at in zip(left_refs, lefts, right_refs, rights):
            left = l_ref[:, at] if l_at is None else l_ref[l_at, :, at]
            right = r_ref[: left.shape[0]] if r_at is None else r_ref[r_at]
            right = low(right)
            part = contract(left, right, 0, 0)
            total = part if total is None else total + part
        total_ref[...] = total
        for s in range(block // (2 * rows)):
            mine = pl.multiple_of((2 * s + core) * rows, rows)
            theirs = pl.multiple_of((2 * s + 1 - core) * rows, rows)
            kept_ref[step, s * rows : (s + 1) * rows] = total_ref[pl.ds(mine, rows)]
            sent_ref[step, s * rows : (s + 1) * rows] = low(total_ref[pl.ds(theirs, rows)])


def grad_call(place, lefts, rights, block, rows, name, after=(), sums=None):
    split = lambda item: item if isinstance(item, tuple) else (item, None)
    left_arrays, left_at = zip(*map(split, lefts))
    right_arrays, right_at = zip(*map(split, rights))
    deep, width = left_arrays[0].shape[-1], right_arrays[0].shape[-1]
    shape = (deep // block, block // 2, width)
    return whole(
        functools.partial(
            grad_kernel, lefts=left_at, rights=right_at, block=block, rows=rows,
            riding=sums is not None,
        ),
        place,
        [shape_of(shape, F32), shape_of((shape[0] + (sums is not None), *shape[1:]), BF)],
        *((a, True) for a in left_arrays + right_arrays + (() if sums is None else (sums,))),
        scratch=[pltpu.VMEM((block, width), F32)],
        after=after,
        name=name,
    )


def add_up(refs, lead, rows):
    total = None
    for ref in refs:
        part = ref[lead, rows, :].astype(F32)
        total = part if total is None else total + part
    return total


def join_call(place, groups, outs, name, after=(), through=(), sums=None):
    width = groups[0][0].shape[2]
    counts = [len(sources) for sources in groups]
    count = sum(counts)
    rows_of = [pieces[0]((0, 0, 0))[3] for _, pieces in outs]
    more = -(-sums[0].shape[0] // rows_of[1]) if sums else 0
    shapes = [
        shape_of((len(pieces) + (more if k else 0), rows, width), dtype)
        for k, ((dtype, pieces), rows) in enumerate(zip(outs, rows_of))
    ]
    if sums:
        shapes = [shape_of(sums[0].shape, F32)] + shapes

    def kernel(place_ref, *refs):
        place_now = (place_ref[0], place_ref[1], place_ref[2])
        ins, out_refs = refs[:count], refs[count:]
        if sums:
            own_ref, total_ref, out_refs = refs[count], refs[count + 1], refs[count + 2 :]
            total = own_ref[...] + take_sums(ins[counts[0] - 1], sums[1], own_ref.shape[0])
            total_ref[...] = total
        at = [sum(counts[:g]) for g in range(len(counts))]
        for k, (out_ref, (dtype, pieces)) in enumerate(zip(out_refs, outs)):
            for n, piece in enumerate(pieces):
                group, lead, start, rows = piece(place_now)
                if not isinstance(start, int):
                    start = pl.multiple_of(start, rows)
                part = add_up(ins[at[group] : at[group] + counts[group]], lead, pl.ds(start, rows))
                out_ref[n] = part.astype(dtype)
            if sums and k:
                give_sums(out_ref, len(pieces), total)

    arrays = [s for sources in groups for s in sources] + ([sums[0]] if sums else [])
    return whole(
        kernel, place, shapes, *((s, True) for s in arrays), after=after, through=through, name=name
    )


def give_sums(ref, first, values):
    parts = low(values)
    size = ref.shape[1]
    for k in range(parts.shape[0] // size):
        ref[first + k] = parts[k * size : (k + 1) * size]
    rest = parts.shape[0] % size
    if rest:
        ref[first + parts.shape[0] // size, :rest] = parts[parts.shape[0] - rest :]


def take_sums(ref, first, rows):
    size = ref.shape[1]
    blocks = [ref[first + k].astype(F32) for k in range(-(-rows // size))]
    return (jnp.concatenate(blocks, 0) if len(blocks) > 1 else blocks[0])[:rows]


def cut_kernel(place_ref, merged_ref, own_ref, sent_ref, onward_ref):
    quad = place_ref[2]
    lanes = own_ref.shape[1]
    take = lambda j: merged_ref[:, pl.ds(pl.multiple_of((quad ^ j) * lanes, lanes), lanes)]
    own_ref[...] = take(0)
    sent_ref[0] = take(2)
    sent_ref[1] = take(3)
    onward_ref[...] = take(1)


def pack_kernel(
    place_ref, proj_ref, table_ref, message_ref
):
    part = proj_ref.shape[0] // 8
    own_heads = table_ref.shape[1]
    room = message_ref.shape[1] // 2
    eighth = place_ref[2] * 2 + place_ref[1]
    message_ref[:part] = proj_ref[pl.ds(pl.multiple_of(eighth * part, part), part), :]
    offsets = table_ref.shape[0]
    table = jnp.concatenate(
        [table_ref[...], jnp.zeros((offsets, 128 - own_heads), F32)], 1
    )
    table = jnp.concatenate([table, jnp.zeros((room - offsets, 128), F32)], 0)
    table = jnp.transpose(table)[:own_heads]
    high = low(table).astype(F32)
    rows = jnp.concatenate([high, table - high], 1)
    spare = message_ref.shape[0] - part - own_heads
    message_ref[part:] = low(jnp.concatenate([rows, jnp.zeros((spare, 2 * room), F32)], 0))


def pieces_kernel(place_ref, *refs, part):
    del place_ref
    for j, ref in enumerate(refs[:-1]):
        refs[-1][j * part : (j + 1) * part] = ref[:part]


def front_kernel(
    place_ref, flat_ref, mg_ref, ms_ref, n1g_ref, n1s_ref, qb_ref, mw_any, qw_any,
    merged_ref, resid0_ref, normed1_ref, qkv_ref, mw_ref, qw_ref, sems,
):
    copy_m = pltpu.make_async_copy(mw_any, mw_ref, sems.at[0])
    copy_q = pltpu.make_async_copy(qw_any, qw_ref, sems.at[1])
    copy_m.start()
    copy_q.start()
    hat, _ = normalise(flat_ref[...].astype(F32))
    merged = low(hat * mg_ref[...] + ms_ref[...])
    merged_ref[...] = merged
    copy_m.wait()
    resid0 = matmul(merged, mw_ref[...])
    resid0_ref[...] = resid0
    hat1, _ = normalise(resid0)
    normed1 = low(hat1 * n1g_ref[...] + n1s_ref[...])
    normed1_ref[...] = normed1
    copy_q.wait()
    qkv_ref[...] = low(matmul(normed1, qw_ref[...]) + qb_ref[...])


def front_call(place, flat, mg, ms, n1g, n1s, qb, mw, qw):
    rows, deep = flat.shape
    width = mw.shape[1]
    return whole(
        front_kernel,
        place,
        [
            shape_of((rows, deep), BF),
            shape_of((rows, width), F32),
            shape_of((rows, width), BF),
            shape_of((rows, 3 * width), BF),
        ],
        (flat, True), (row(mg), True), (row(ms), True), (row(n1g), True), (row(n1s), True),
        (row(qb), True), (mw, False), (qw, False),
        scratch=[
            pltpu.VMEM(mw.shape, BF), pltpu.VMEM(qw.shape, BF), pltpu.SemaphoreType.DMA((2,)),
        ],
        room=28,
        name="front",
    )


def mine_kernel(place_ref, *refs):
    del place_ref
    rows = refs[0].shape[0]
    for q, ref in enumerate(refs[:-1]):
        refs[-1][q * rows : (q + 1) * rows] = ref[...]


def bring_proj(place_ref, own_any, mine_any, theirs_any, proj_ref, sems, groups):
    rank, core, quad = place_ref[0], place_ref[1], place_ref[2]
    shard = own_any.shape[0]
    part = shard // 8

    def bring(source, start, rows, sem):
        at = pl.ds(pl.multiple_of(start, rows), rows)
        copy = pltpu.make_async_copy(source, proj_ref.at[at], sems.at[sem])
        copy.start()
        return copy

    copies = [bring(own_any, rank * shard, shard, 0)]
    for k in range(4 * (groups - 1)):
        q, j = k // (groups - 1), k % (groups - 1)
        base = lax.rem(rank + groups - 1 - j, groups) * shard + (quad ^ q) * 2 * part
        rows = pl.ds(k * part, part)
        copies.append(bring(mine_any.at[rows], base + core * part, part, 1 + 2 * k))
        copies.append(bring(theirs_any.at[rows], base + (1 - core) * part, part, 2 + 2 * k))
    return copies


def after_kernel(
    place_ref, heads_ref, resid0_ref, pb_ref, n2g_ref, n2s_ref, own_any, mine_any, theirs_any,
    resid1_ref, normed2_ref, proj_ref, sems, *, groups,
):
    for copy in bring_proj(place_ref, own_any, mine_any, theirs_any, proj_ref, sems, groups):
        copy.wait()
    resid1 = resid0_ref[...] + matmul(heads_ref[...], proj_ref[...]) + pb_ref[...]
    resid1_ref[...] = resid1
    hat2, _ = normalise(resid1)
    normed2_ref[...] = low(hat2 * n2g_ref[...] + n2s_ref[...])


SQRT_HALF = 0.5**0.5
DENSITY = 0.3989422804014327


def gelu_pair(values):
    below = 0.5 * (1.0 + lax.erf(values * SQRT_HALF))
    density = jnp.exp(-0.5 * values * values) * DENSITY
    return values * below, below + values * density


def slope_kernel(
    place_ref, dy_ref, fc2_ref, rows_ref, own_ref, out_ref, wide_ref, *, groups, pad, chunk
):
    tokens, width = own_ref.shape
    wide_ref[...] = dy_ref[...].astype(F32)
    fill = jnp.zeros((pad - tokens, width), F32)
    for j in range(groups):
        at = lax.rem(place_ref[0] + groups - j, groups) * tokens
        block = wide_ref[pl.ds(pl.multiple_of(at, 8), tokens), :]
        rows_ref[j * pad : (j + 1) * pad] = low(jnp.concatenate([block, fill], 0))
        if j == 0:
            own_ref[...] = low(block)

    @pl.loop(0, fc2_ref.shape[0] // chunk)
    def _(step):
        at = pl.ds(pl.multiple_of(step * chunk, chunk), chunk)
        out_ref[:, at] = contract(rows_ref[...], fc2_ref[at, :], 1, 1)


def feed_kernel(
    place_ref, n0_ref, n1_ref, n2_ref, n3_ref, d_act_ref, fc1_ref, fc1b_ref,
    act_ref, dpre_ref, all_ref, db_ref, o0_ref, o1_ref, o2_ref, o3_ref, *, pad, chunk,
):
    del place_ref
    rows, width = n0_ref.shape
    for j, ref in enumerate((n0_ref, n1_ref, n2_ref, n3_ref)):
        all_ref[j * pad : j * pad + rows, :] = ref[...]
        all_ref[j * pad + rows : (j + 1) * pad, :] = jnp.zeros((pad - rows, width), BF)

    @pl.loop(0, fc1_ref.shape[1] // chunk)
    def _(step):
        at = pl.ds(pl.multiple_of(step * chunk, chunk), chunk)
        pre = matmul(all_ref[...], fc1_ref[:, at]) + fc1b_ref[:, at]
        act, slope = gelu_pair(pre)
        act_ref[:, at] = low(act)
        d_low = low(d_act_ref[:, at] * slope)
        dpre_ref[:, at] = d_low
        db_ref[:, at] = jnp.sum(d_low.astype(F32), 0, keepdims=True)

    for j, ref in enumerate((o0_ref, o1_ref, o2_ref, o3_ref)):
        part = contract(dpre_ref[j * pad : (j + 1) * pad, :], fc1_ref[...], 1, 1)
        ref[...] = low(part[:rows])


def second_kernel(place_ref, act_ref, fc2_ref, kept_ref, sent_ref, *, pad, groups):
    rank = place_ref[0]
    rows = kept_ref.shape[1]
    for ref, k, flip in ((sent_ref, 0, 1), (sent_ref, 1, 3), (kept_ref, 0, 0), (kept_ref, 1, 2)):
        block = lax.rem(rank + groups - (rank ^ flip), groups)
        at = pl.ds(pl.multiple_of(block * pad, pad), pad)
        ref[k] = low(matmul(act_ref[at, :], fc2_ref[...])[:rows])


def back2_kernel(
    place_ref, c0_ref, c1_ref, c2_ref, c3_ref, resid1_ref, dy_ref, n2g_ref, own_any, mine_any, theirs_any,
    dresid1_ref, dheads_ref, proj_ref, sems, *, groups,
):
    copies = bring_proj(place_ref, own_any, mine_any, theirs_any, proj_ref, sems, groups)
    rows = dheads_ref.shape[0]
    d_norm2 = (
        c0_ref[...].astype(F32) + c1_ref[...].astype(F32)
        + c2_ref[...].astype(F32) + c3_ref[...].astype(F32)
    )
    hat2, inv2 = normalise(resid1_ref[...])
    dy = dy_ref[...].astype(F32)
    d_resid1 = dy + norm_backward(d_norm2, hat2, inv2, n2g_ref[...])
    dresid1_ref[:rows] = d_resid1
    sums = (d_resid1, d_norm2 * hat2, d_norm2, dy)
    for k, part in enumerate(sums):
        dresid1_ref[rows + k : rows + k + 1] = jnp.sum(part, 0, keepdims=True)
    for copy in copies:
        copy.wait()
    dheads_ref[...] = low(contract(low(d_resid1), proj_ref[...], 1, 1))


def back1_kernel(
    place_ref, d0_ref, d1_ref, d2_ref, d3_ref, dresid1_ref, resid0_ref, n1g_ref, qw_any,
    dresid0_ref, sums_ref, qw_ref, sems,
):
    rows, width = resid0_ref.shape
    quad = place_ref[2]
    lanes = width // 4
    copies = [
        pltpu.make_async_copy(qw_any.at[:, pl.ds(i * width, width)], qw_ref.at[i], sems.at[i])
        for i in range(3)
    ]
    for copy in copies:
        copy.start()
    hat1, inv1 = normalise(resid0_ref[...])
    d_norm1 = jnp.zeros((rows, width), F32)
    for i in range(3):
        copies[i].wait()
        for j, d_ref in enumerate((d0_ref, d1_ref, d2_ref, d3_ref)):
            part = d_ref[:, i * lanes : (i + 1) * lanes]
            at = pl.ds(pl.multiple_of((quad ^ j) * lanes, lanes), lanes)
            d_norm1 = d_norm1 + contract(part, qw_ref[i, :, at], 1, 1)
            sums_ref[2 + i : 3 + i, at] = jnp.sum(part.astype(F32), 0, keepdims=True)
    dresid0_ref[...] = low(
        dresid1_ref[:rows] + norm_backward(d_norm1, hat1, inv1, n1g_ref[...])
    )
    sums_ref[0:1] = jnp.sum(d_norm1 * hat1, 0, keepdims=True)
    sums_ref[1:2] = jnp.sum(d_norm1, 0, keepdims=True)


def back0_kernel(
    place_ref, dresid0_ref, flat_ref, mg_ref, mw_any, grad_ref, sums_ref, mw_ref, sems
):
    del place_ref
    copy = pltpu.make_async_copy(mw_any, mw_ref, sems.at[0])
    copy.start()
    hat, inv = normalise(flat_ref[...].astype(F32))
    copy.wait()
    d_merged = contract(dresid0_ref[...], mw_ref[...], 1, 1)
    grad_ref[...] = low(norm_backward(d_merged, hat, inv, mg_ref[...]))
    width = dresid0_ref.shape[1]
    gain = jnp.sum(d_merged * hat, 0, keepdims=True)
    shift = jnp.sum(d_merged, 0, keepdims=True)
    for i in range(gain.shape[1] // width):
        sums_ref[i : i + 1] = gain[:, i * width : (i + 1) * width]
        sums_ref[2 + i : 3 + i] = shift[:, i * width : (i + 1) * width]


SPAN = 2 * WIN - 1
OFFSETS = 384
STRIP = 256


def strip_picks(column, offsets_first):
    shape, o_dim = ((OFFSETS, STRIP), 0) if offsets_first else ((STRIP, OFFSETS), 1)
    offset = lax.broadcasted_iota(jnp.int32, shape, o_dim)
    lane = lax.broadcasted_iota(jnp.int32, shape, 1 - o_dim)
    wanted = (SPAN - 1 - lane // WIN) * SPAN + column - lane % WIN + WIN - 1
    hit = (offset == wanted) & (lane < SPAN * WIN)
    return jnp.where(hit, 1.0, 0.0).astype(BF)


def split3(values):
    first = low(values)
    rest = values - first.astype(F32)
    second = low(rest)
    third = low(rest - second.astype(F32))
    return first, second, third


def spread_kernel(place_ref, m0_ref, m1_ref, m2_ref, m3_ref, bias_ref, table_ref, *, part, groups):
    heads = table_ref.shape[0]
    own_heads = heads // groups
    room = m0_ref.shape[1] // 2
    for j, ref in enumerate((m0_ref, m1_ref, m2_ref, m3_ref)):
        both = ref[part : part + 2 * own_heads, :].astype(F32)[:own_heads]
        at = pl.multiple_of(lax.rem(place_ref[0] + groups - j, groups) * own_heads, own_heads)
        table_ref[pl.ds(at, own_heads), :] = both[:, :OFFSETS] + both[:, room : room + OFFSETS]
    table = table_ref[...]
    high = low(table)
    table = jnp.concatenate([high, low(table - high.astype(F32))], 0)
    for column in range(WIN):
        parts = matmul(table, strip_picks(column, True))
        strip = parts[:heads] + parts[heads:]
        for r in range(WIN):
            start = (WIN - 1 - r) * WIN
            at = (r * WIN + column) * heads
            bias_ref[at : at + heads, :] = strip[:, start : start + KEY_ROWS]
    bias_ref[WINDOW_TOKENS * heads :, :] = jnp.zeros(
        ((QUERY_ROWS - WINDOW_TOKENS) * heads, KEY_ROWS), F32
    )


def fold(grad_ref, heads):
    total = jnp.zeros((3 * heads, OFFSETS), F32)
    for column in range(WIN):
        strip = jnp.zeros((heads, STRIP), F32)
        for r in range(WIN):
            start = (WIN - 1 - r) * WIN
            at = (r * WIN + column) * heads
            part = grad_ref[at : at + heads, :]
            wide = jnp.concatenate([part, jnp.zeros((heads, STRIP - KEY_ROWS), F32)], 1)
            strip = strip + (pltpu.roll(wide, start, 1) if start else wide)
        total = total + matmul(jnp.concatenate(split3(strip), 0), strip_picks(column, False))
    return total[:heads] + total[heads : 2 * heads] + total[2 * heads :]


def window_rows(values, window, rows):
    part = values.astype(F32)[window * WINDOW_TOKENS : (window + 1) * WINDOW_TOKENS]
    zeros = jnp.zeros((rows - WINDOW_TOKENS, part.shape[1]), F32)
    return low(jnp.concatenate([part, zeros], 0))


def stack_heads(part, heads, head_dim):
    lane = lax.broadcasted_iota(jnp.int32, part.shape, 1) // head_dim
    zero = jnp.zeros_like(part)
    return jnp.concatenate([jnp.where(lane == h, part, zero) for h in range(heads)], 0)


def attend_kernel(
    place_ref, qkv_ref, bias_ref, mask_ref, out_ref, probs_any, probs_ref, sems, *, windows, head_dim
):
    del place_ref
    width = out_ref.shape[1]
    lanes = width // 4

    def keep(step):
        return pltpu.make_async_copy(probs_ref.at[step], probs_any.at[step], sems.at[step])

    @pl.loop(0, 4)
    def _(step):
        attend_group(
            step, qkv_ref, bias_ref, mask_ref, out_ref, probs_ref, windows, head_dim, width, lanes
        )
        keep(step).start()

    for step in range(4):
        keep(step).wait()


def attend_group(
    step, qkv_ref, bias_ref, mask_ref, out_ref, probs_ref, windows, head_dim, width, lanes
):
    heads, all_heads = lanes // head_dim, width // head_dim
    first = step * heads
    scale = head_dim ** (-0.5)
    at = lambda kind: pl.ds(pl.multiple_of(kind * width + step * lanes, lanes), lanes)
    q_all, k_all, v_all = (qkv_ref[:, at(kind)] for kind in range(3))
    outs = []
    for w in range(windows):
        query = window_rows(q_all, w, QUERY_ROWS)
        keys = stack_heads(window_rows(k_all, w, KEY_ROWS), heads, head_dim)
        values = stack_heads(window_rows(v_all, w, KEY_ROWS), heads, head_dim)
        scores = contract(query, keys, 1, 1) * scale
        mask = mask_ref[w]
        rounded = []
        for h in range(heads):
            bias = bias_ref[pl.ds(first + h, QUERY_ROWS, stride=all_heads), :]
            raw = scores[:, h * KEY_ROWS : (h + 1) * KEY_ROWS] + bias + mask
            expo = jnp.exp(raw - jnp.max(raw, -1, keepdims=True))
            probs = expo / jnp.sum(expo, -1, keepdims=True)
            probs_ref[step, w, h] = probs
            rounded.append(low(probs))
        mixed = matmul(jnp.concatenate(rounded, 1), values)
        outs.append(mixed[:WINDOW_TOKENS])
    out_ref[:, at(0)] = low(jnp.concatenate(outs, 0))


def attend_back_kernel(
    place_ref, qkv_ref, grad_ref, probs_any, d0_ref, d1_ref, d2_ref, d3_ref, table_ref, dbias_ref, probs_ref, sems,
    *, windows, head_dim
):
    width = grad_ref.shape[1]

    def fetch(step):
        return pltpu.make_async_copy(
            probs_any.at[place_ref[2] ^ step], probs_ref.at[step], sems.at[step]
        )

    for step in range(4):
        fetch(step).start()

    @pl.loop(0, 4)
    def _(step):
        fetch(step).wait()
        attend_back_group(
            place_ref[2] ^ step, step, qkv_ref, grad_ref, probs_ref, (d0_ref, d1_ref, d2_ref, d3_ref), dbias_ref,
            windows, head_dim, width, width // 4,
        )

    table_ref[...] = fold(dbias_ref, table_ref.shape[0])


def attend_back_group(
    group, step, qkv_ref, grad_ref, probs_ref, d_refs, dbias_ref,
    windows, head_dim, width, lanes,
):
    heads, all_heads = lanes // head_dim, width // head_dim
    first = group * heads
    scale = head_dim ** (-0.5)
    at = lambda kind: pl.ds(pl.multiple_of(kind * width + group * lanes, lanes), lanes)
    q_all, k_all, v_all = (qkv_ref[:, at(kind)] for kind in range(3))
    g_all = grad_ref[:, at(0)]
    all_q, all_k, all_v = [], [], []
    d_first = []
    for w in range(windows):
        query = stack_heads(window_rows(q_all, w, QUERY_ROWS), heads, head_dim)
        keys = stack_heads(window_rows(k_all, w, KEY_ROWS), heads, head_dim)
        values = stack_heads(window_rows(v_all, w, KEY_ROWS), heads, head_dim)
        plain = window_rows(g_all, w, QUERY_ROWS)
        grad = stack_heads(plain, heads, head_dim)
        d_probs = contract(plain, values, 1, 1)
        d_list, p_list = [], []
        for h in range(heads):
            probs = probs_ref[step, w, h]
            part = d_probs[:, h * KEY_ROWS : (h + 1) * KEY_ROWS]
            total = jnp.sum(part * probs, -1, keepdims=True)
            d_scores = low(probs * (part - total))
            d_list.append(d_scores)
            p_list.append(low(probs))
            if w == 0:
                d_first.append(d_scores.astype(F32))
            else:
                d_first[h] = d_first[h] + d_scores.astype(F32)
            if w == windows - 1:
                dbias_ref[pl.ds(first + h, QUERY_ROWS, stride=all_heads), :] = d_first[h]
        d_query = matmul(jnp.concatenate(d_list, 1), keys) * scale
        d_keys = contract(jnp.concatenate(d_list, 0), query, 0, 0) * scale
        d_values = contract(jnp.concatenate(p_list, 0), grad, 0, 0)
        all_q.append(d_query[:WINDOW_TOKENS])
        all_k.append(d_keys[:WINDOW_TOKENS])
        all_v.append(d_values[:WINDOW_TOKENS])
    result = jnp.concatenate(
        [low(jnp.concatenate(parts, 0)) for parts in (all_q, all_k, all_v)], 1
    )

    for k, d_ref in enumerate(d_refs):

        @pl.when(step == k)
        def _(d_ref=d_ref):
            d_ref[...] = result


def spots(heads, lines, vectors):
    columns = 3
    return [(k // columns, OFFSETS + 128 * (k % columns)) for k in range(vectors * lines)]


def collect_kernel(place_ref, s0_ref, s1_ref, d_ref, rel_ref, b_ref, out_ref):
    heads = rel_ref.shape[0]
    lines = s0_ref.shape[1] // 128
    out_ref[...] = jnp.zeros(out_ref.shape, F32)
    out_ref[:heads, :OFFSETS] = rel_ref[...]
    vectors = [ref[r : r + 1, :] for ref in (s0_ref, s1_ref) for r in range(ref.shape[0])]
    after = d_ref.shape[0] - 8
    vectors += [d_ref[after + r : after + r + 1, :] for r in range(4)]
    for k, (at, lane) in enumerate(spots(heads, lines, len(vectors))):
        piece = vectors[k // lines][:, 128 * (k % lines) : 128 * (k % lines + 1)]
        out_ref[at : at + 1, lane : lane + 128] = piece
    own = b_ref.shape[1] // 128
    first = heads + pl.multiple_of((place_ref[0] // 2) * own, own)
    block = jnp.concatenate([b_ref[:, k * 128 : (k + 1) * 128] for k in range(own)], 0)
    side = place_ref[0] % 2

    @pl.when(side == 0)
    def _():
        out_ref[pl.ds(first, own), 0:128] = block

    @pl.when(side == 1)
    def _():
        out_ref[pl.ds(first, own), 128:256] = block


def deliver_kernel(place_ref, all_ref, *refs, heads):
    *vector_refs, rel_ref, b_ref = refs
    offsets = rel_ref.shape[0]
    rel = jnp.concatenate([all_ref[:heads, :OFFSETS], jnp.zeros((128 - heads, OFFSETS), F32)], 0)
    rel_ref[...] = jnp.transpose(rel)[:offsets, :heads]
    lines = [ref.shape[0] // 128 for ref in vector_refs]
    places = iter(spots(heads, 1, sum(lines)))
    for ref, count in zip(vector_refs, lines):
        for k in range(count):
            at, lane = next(places)
            ref[128 * k : 128 * (k + 1)] = all_ref[at, lane : lane + 128]
    own = b_ref.shape[0]
    first = heads + pl.multiple_of((place_ref[0] // 2) * own, own)
    side = place_ref[0] % 2

    @pl.when(side == 0)
    def _():
        b_ref[...] = all_ref[pl.ds(first, own), 0:128]

    @pl.when(side == 1)
    def _():
        b_ref[...] = all_ref[pl.ds(first, own), 128:256]


def columns_kernel(place_ref, b0_ref, b1_ref, b2_ref, b3_ref, own_ref, out_ref, sums_ref):
    rows = out_ref.shape[0]
    lanes = b0_ref.shape[2] // 3
    total = own_ref[...]
    for j, ref in enumerate((b0_ref, b1_ref, b2_ref, b3_ref)):
        for part in range(3):
            at = pl.multiple_of((part * 4 + (place_ref[2] ^ j)) * lanes, lanes)
            out_ref[:, pl.ds(at, lanes)] = ref[0, :rows, part * lanes : (part + 1) * lanes].astype(F32)
        if j:
            total = total + take_sums(ref, 1, own_ref.shape[0])
    sums_ref[...] = total


def on_device(
    patches,
    window_extent,
    merge_gain,
    merge_shift,
    merge_weight,
    norm1_gain,
    norm1_shift,
    qkv_weight,
    qkv_bias,
    rel_table,
    proj_weight,
    proj_bias,
    norm2_gain,
    norm2_shift,
    fc1_weight,
    fc1_bias,
    fc2_weight,
    fc2_bias,
    out_grad,
):
    groups, wide = lax.axis_size("narrow"), lax.axis_size("wide")
    devices = wide * groups
    highs = wide // 8
    wide_at, rank = lax.axis_index("wide"), lax.axis_index("narrow")
    core, quad, high = wide_at % 2, (wide_at // 2) % 4, wide_at // 8
    place = jnp.stack([rank, core, quad]).astype(jnp.int32)
    tokens = patches.shape[0]
    width = qkv_weight.shape[0]
    own_heads = rel_table.shape[1]
    heads = own_heads * groups
    head_dim = width // heads
    windows = tokens // WINDOW_TOKENS
    pad = tokens + (-tokens) % 16

    def arrange(array, order):
        if highs == 1:
            return array
        sizes = {"h": highs, "q": 4, "c": 2, "n": groups}
        cut = [sizes[k] for k in order]
        rest = array.shape[1]
        for size in cut:
            rest //= size
        at = order.index("h") + 1
        moved = [i + 1 for i in range(len(order)) if i + 1 != at] + [at, len(order) + 1]
        return jnp.transpose(array.reshape(-1, *cut, rest), [0] + moved).reshape(array.shape)

    def settle(array):
        if highs == 1:
            return array[0]
        return sum_high(array[0].reshape(highs, -1, array.shape[2]), high)

    part = proj_weight.shape[0] // 8
    message = whole(
        pack_kernel,
        place,
        [shape_of((part + own_heads + (-(part + own_heads)) % 16, width), BF)],
        (proj_weight, True),
        (rel_table, True),
        name="pack",
    )[0]
    messages = [turn(message, "narrow", step) for step in range(1, groups)]

    flat = patches.reshape(tokens, -1)
    merged, resid0, normed1, qkv = front_call(
        place, flat, merge_gain, merge_shift, norm1_gain, norm1_shift, qkv_bias,
        merge_weight, qkv_weight,
    )
    mine = whole(
        functools.partial(pieces_kernel, part=part),
        place,
        [shape_of(((groups - 1) * part, width), BF)],
        *((m, True) for m in messages),
        name="pieces",
    )
    mine = list(mine) + [swap(mine[0], "wide", 2 * j) for j in (1, 2, 3)]

    merged_own, merged_sent, merged_onward = whole(
        cut_kernel,
        place,
        [
            shape_of((tokens, merged.shape[1] // 4), BF),
            shape_of((2, tokens, merged.shape[1] // 4), BF),
            shape_of((tokens, merged.shape[1] // 4), BF),
        ],
        (arrange(merged, "hqcn"), True),
        name="cut",
    )
    merged_near = swap(merged_sent, "wide", 4)
    normed1_cut = arrange(normed1, "hqcn")
    normed1_near = swap(normed1_cut, "wide", 2)

    positions = jnp.arange(KEY_ROWS)
    extent = lax.dynamic_slice_in_dim(window_extent, rank * windows, windows, 0)
    valid = (
        (positions[None, :] // WIN < extent[:, 0:1])
        & (positions[None, :] % WIN < extent[:, 1:2])
        & (positions[None, :] < WINDOW_TOKENS)
    )
    mask = jnp.where(valid, 0.0, -1e30).astype(F32)[:, None, :]
    bias = whole(
        functools.partial(spread_kernel, part=part, groups=groups),
        place,
        [shape_of((QUERY_ROWS * heads, KEY_ROWS), F32)],
        (message, True),
        *((m, True) for m in messages),
        scratch=[pltpu.VMEM((heads, OFFSETS), F32)],
        name="spread",
    )[0]
    heads_out, probs = whole(
        functools.partial(attend_kernel, windows=windows, head_dim=head_dim),
        place,
        [
            shape_of((tokens, width), BF),
            shape_of((PROBS_ROOM, windows, heads // 4, QUERY_ROWS, KEY_ROWS), F32),
        ],
        (qkv, True), (bias, True), (mask, True),
        leave=(1,),
        scratch=[
            pltpu.VMEM((4, windows, heads // 4, QUERY_ROWS, KEY_ROWS), F32),
            pltpu.SemaphoreType.DMA((4,)),
        ],
        name="attend",
    )

    mine = whole(
        mine_kernel,
        place,
        [shape_of((4 * mine[0].shape[0], width), BF)],
        *((m, True) for m in mine),
        after=(heads_out, merged_near, normed1_near),
        name="mine",
    )[0]
    theirs = swap(mine, "wide", 1)
    resid1, normed2 = whole(
        functools.partial(after_kernel, groups=groups),
        place,
        [shape_of((tokens, width), F32), shape_of((tokens, width), BF)],
        (heads_out, True), (resid0, True),
        (row(proj_bias), True), (row(norm2_gain), True), (row(norm2_shift), True),
        (proj_weight, None), (mine, None), (theirs, None),
        scratch=[pltpu.VMEM((width, width), BF), pltpu.SemaphoreType.DMA((1 + 8 * (groups - 1),))],
        name="after",
    )
    blocks = [normed2] + [turn(normed2, "narrow", step) for step in range(1, groups)]

    merged_onward = jnp.stack([tie(merged_onward, normed2), merged_near[1]])
    merged_far = swap(merged_onward, "wide", 2)
    normed1_both = jnp.stack([normed1_cut, tie(normed1_near, normed2)])
    normed1_far = swap(normed1_both, "wide", 4)

    total, units = groups * pad, fc1_weight.shape[1]
    dy_rows, dy_own, d_act = whole(
        functools.partial(slope_kernel, groups=groups, pad=pad, chunk=256),
        place,
        [
            shape_of((total, width), BF),
            shape_of((tokens, width), BF),
            shape_of((total, units), F32),
        ],
        (out_grad, True), (fc2_weight, True),
        scratch=[pltpu.VMEM(out_grad.shape, F32)],
        after=(normed2,),
        name="slope",
    )
    act, d_pre, rows_all, fc1_b_grad, *chunks = whole(
        functools.partial(feed_kernel, pad=pad, chunk=256),
        place,
        [
            shape_of((total, units), BF),
            shape_of((total, units), BF),
            shape_of((total, width), BF),
            shape_of((1, units), F32),
        ]
        + [shape_of((tokens, width), BF)] * 4,
        *((b, True) for b in blocks), (d_act, True), (fc1_weight, True), (row(fc1_bias), True),
        after=(normed1_far, merged_far),
        name="feed",
    )
    arrived = [chunks[0]] + [turn(chunks[j], "narrow", -j) for j in range(1, groups)]

    fc1_kept, fc1_sent = grad_call(place, [arrange(rows_all, "hqc")], [d_pre], 256, 128, "fc1_grad")
    fc2_kept, fc2_sent = grad_call(place, [arrange(act, "hqc")], [dy_rows], 256, 128, "fc2_grad")
    fc1_come, fc2_come = swap(fc1_sent, "wide", 1), swap(fc2_sent, "wide", 1)
    fc1_kept, fc1_sent = join_call(
        place, [(fc1_kept, fc1_come)],
        [
            (F32, [lambda p, y=y: (0, 2 * y + p[2] % 2, 0, 128) for y in range(2)]),
            (BF, [lambda p, y=y: (0, 2 * y + 1 - p[2] % 2, 0, 128) for y in range(2)]),
        ],
        "fc1_join",
    )
    fc2_kept, fc2_sent = join_call(
        place, [(fc2_kept, fc2_come)],
        [
            (F32, [lambda p, x=x: (0, 2 * (p[2] // 2) + x, 0, 128) for x in range(2)]),
            (BF, [lambda p, x=x: (0, 2 * (1 - p[2] // 2) + x, 0, 128) for x in range(2)]),
        ],
        "fc2_join",
    )
    fc1_come, fc2_come = swap(fc1_sent, "wide", 2), swap(fc2_sent, "wide", 4)
    fc1_kept, fc1_sent = join_call(
        place, [(fc1_kept, fc1_come)],
        [
            (F32, [lambda p: (0, p[2] // 2, 0, 128)]),
            (BF, [lambda p: (0, 1 - p[2] // 2, 0, 128)]),
        ],
        "fc1_join2",
    )
    fc2_kept, fc2_sent = join_call(
        place, [(fc2_kept, fc2_come)],
        [
            (F32, [lambda p: (0, p[2] % 2, 0, 128)]),
            (BF, [lambda p: (0, 1 - p[2] % 2, 0, 128)]),
        ],
        "fc2_join2",
    )
    fc1_come, fc2_come = swap(fc1_sent, "wide", 4), swap(fc2_sent, "wide", 2)
    second_kept, second_sent = whole(
        functools.partial(second_kernel, pad=pad, groups=groups),
        place,
        [shape_of((2, tokens, width), BF)] * 2,
        (act, True),
        (fc2_weight, True),
        name="second",
    )
    d_resid1, d_heads, second_sent = whole(
        functools.partial(back2_kernel, groups=groups),
        place,
        [shape_of((tokens + 8, width), F32), shape_of((tokens, width), BF)],
        *((a, True) for a in arrived),
        (resid1, True), (dy_own, True), (row(norm2_gain), True),
        (proj_weight, None), (mine, None), (theirs, None),
        scratch=[pltpu.VMEM((width, width), BF), pltpu.SemaphoreType.DMA((1 + 8 * (groups - 1),))],
        after=(fc1_sent, fc2_sent),
        through=(second_sent,),
        name="back2",
    )
    second_come = swap(second_sent, "narrow", 1)
    *d_parts, rel_part = whole(
        functools.partial(attend_back_kernel, windows=windows, head_dim=head_dim),
        place,
        [shape_of((tokens, 3 * width // 4), BF)] * 4 + [shape_of((heads, OFFSETS), F32)],
        (qkv, True), (d_heads, True), (probs, False),
        scratch=[
            pltpu.VMEM((QUERY_ROWS * heads, KEY_ROWS), F32),
            pltpu.VMEM((4, *probs.shape[1:]), F32),
            pltpu.SemaphoreType.DMA((4,)),
        ],
        after=(fc1_come, fc2_come),
        name="attend_back",
    )
    d_come = [swap(d_parts[j], "wide", 2 * j) for j in (1, 2, 3)]

    d_resid0, sums1 = whole(
        back1_kernel,
        place,
        [shape_of((tokens, width), BF), shape_of((5, width), F32)],
        *((d, True) for d in d_parts), (d_resid1, True), (resid0, True),
        (row(norm1_gain), True), (qkv_weight, False),
        room=56,
        scratch=[pltpu.VMEM((3, width, width), BF), pltpu.SemaphoreType.DMA((3,))],
        name="back1",
    )
    d_flat, sums0 = whole(
        back0_kernel,
        place,
        [shape_of(flat.shape, BF), shape_of((2 * flat.shape[1] // width, width), F32)],
        (d_resid0, True), (flat, True), (row(merge_gain), True), (merge_weight, False),
        scratch=[pltpu.VMEM(merge_weight.shape, BF), pltpu.SemaphoreType.DMA((1,))],
        name="back0",
    )

    second_own, second_sent = join_call(
        place, [(second_kept, second_come)],
        [(F32, [lambda p: (0, 0, 0, tokens)]), (BF, [lambda p: (0, 1, 0, tokens)])],
        "second_join",
    )
    second_come = swap(second_sent, "narrow", 2)

    proj_kept, proj_sent = grad_call(
        place, [arrange(heads_out, "nhqc")], [d_resid1], 256, 32, "proj_grad", after=(d_resid0,)
    )
    proj_come = swap(proj_sent, "wide", 1)

    side = lambda pick_x: [
        lambda p, n=n, y=y: (0, n, (2 * y + pick_x(p[2] % 2)) * 32, 32)
        for n in range(groups) for y in range(2)
    ]
    proj_kept, proj_sent = join_call(
        place, [(proj_kept, proj_come)],
        [(F32, side(lambda x: x)), (BF, side(lambda x: 1 - x))],
        "proj_join",
    )
    proj_come = swap(proj_sent, "wide", 2)

    own_sums, d_resid0 = whole(
        collect_kernel,
        place,
        [shape_of((48, 3 * width // 4), F32)],
        (sums0, True), (sums1, True), (d_resid1, True), (rel_part, True), (fc1_b_grad, True),
        after=(*d_come, second_sent, proj_sent),
        through=(d_resid0,),
        name="collect",
    )
    r_come = [swap(d_resid0, "wide", 2 * j) for j in (1, 2, 3)]
    qkv_kept, qkv_sent = grad_call(
        place,
        [normed1_cut, (normed1_both, 1), (normed1_far, 0), (normed1_far, 1)],
        [d_parts[0], *d_come],
        256, 128, "qkv_grad", sums=own_sums, after=(second_sent,),
    )
    qkv_come = swap(qkv_sent, "wide", 1)
    rows = 128 // groups
    qkv_pieces = lambda flip: [
        lambda p, g=g, k=k: (0, g, (2 * k + (p[0] + flip) % 2) * rows, rows)
        for k in range(2) for g in range(4)
    ]
    own_sums, qkv_kept, qkv_sent = join_call(
        place, [(qkv_kept, qkv_come)], [(F32, qkv_pieces(0)), (BF, qkv_pieces(1))], "qkv_join",
        sums=(own_sums, 4),
    )
    qkv_come = swap(qkv_sent, "narrow", 1)

    merge_kept, merge_sent = grad_call(
        place,
        [merged_own, (merged_far, 0), (merged_near, 0), (merged_far, 1)],
        [d_resid0, *r_come],
        merged_own.shape[1], merged_own.shape[1] // 2, "merge_grad", after=(qkv_sent,),
    )
    merge_come = swap(merge_sent, "wide", 1)

    second_pieces = lambda flip: [
        lambda p, g=g: (0, ((p[0] // 2 + flip) % 2) * 4 + g, 0, rows) for g in range(4)
    ]
    own_sums, qkv_kept, qkv_sent = join_call(
        place, [(qkv_kept, qkv_come)],
        [(F32, second_pieces(0)), (BF, second_pieces(1))],
        "qkv_join2",
        sums=(own_sums, 8),
        after=(merge_sent,),
    )
    qkv_come = swap(qkv_sent, "narrow", 2)
    merge_rows = merged_own.shape[1] // 2 // groups
    merge_pieces = lambda flip: [
        lambda p, k=k: (0, 0, (2 * k + (p[0] + flip) % 2) * merge_rows, merge_rows)
        for k in range(2)
    ]
    merge_kept, merge_sent, fc1_come, fc2_come, d_flat = join_call(
        place, [(merge_kept, merge_come)],
        [(F32, merge_pieces(0)), (BF, merge_pieces(1))],
        "merge_join",
        after=(qkv_sent,),
        through=(fc1_come, fc2_come, d_flat),
    )
    merge_first = merge_sent
    merge_come = swap(merge_sent, "narrow", 1)

    last_pieces = lambda flip, size: [lambda p: (0, (p[0] // 2 + flip) % 2, 0, size)]
    merge_kept, merge_sent = join_call(
        place, [(merge_kept, merge_come)],
        [(F32, last_pieces(0, merge_rows)), (BF, last_pieces(1, merge_rows))],
        "merge_join2",
        after=(qkv_sent,),
    )
    merge_last = merge_sent
    merge_come = swap(merge_sent, "narrow", 2)

    proj_kept, proj_sent = join_call(
        place, [(proj_kept, proj_come)],
        [
            (F32, [lambda p, n=n: (0, 2 * n + p[2] // 2, 0, 32) for n in range(groups)]),
            (BF, [lambda p, n=n: (0, 2 * n + 1 - p[2] // 2, 0, 32) for n in range(groups)]),
        ],
        "proj_join2",
        after=(merge_first,),
    )
    proj_come = swap(proj_sent, "wide", 4)
    proj_pieces = lambda flip: [
        lambda p, k=k: (0, 2 * k + (p[0] + flip) % 2, 0, 32) for k in range(2)
    ]
    proj_kept, proj_sent = join_call(
        place, [(proj_kept, proj_come)], [(F32, proj_pieces(0)), (BF, proj_pieces(1))],
        "proj_join3",
        after=(merge_sent,),
    )
    proj_come = swap(proj_sent, "narrow", 1)
    proj_kept, proj_sent = join_call(
        place, [(proj_kept, proj_come)],
        [(F32, last_pieces(0, 32)), (BF, last_pieces(1, 32))],
        "proj_join4",
    )
    proj_come = swap(proj_sent, "narrow", 2)

    own_sums, *cuts = join_call(
        place, [(qkv_kept, qkv_come)],
        [(BF, [lambda p, j=j: (0, p[2] ^ j, 0, rows)]) for j in range(4)],
        "qkv_join3",
        sums=(own_sums, 4),
        after=(merge_last,),
    )
    cuts = [cuts[0]] + [swap(cuts[j], "wide", 2 * j) for j in (1, 2, 3)]
    qkv_out, all_sums = whole(
        columns_kernel,
        place,
        [shape_of((rows, 3 * width), F32), shape_of(own_sums.shape, F32)],
        *((c, True) for c in cuts), (own_sums, True),
        name="columns",
    )
    qkv_out = settle(qkv_out[None])
    mask = 8
    while mask < wide:
        all_sums = all_sums + swap(all_sums, "wide", mask)
        mask *= 2
    merge_out = settle(merge_kept + merge_come.astype(F32))
    proj_out = settle(proj_kept + proj_come.astype(F32))

    fc1_out = settle(fc1_kept + fc1_come.astype(F32))
    fc2_out = settle(fc2_kept + fc2_come.astype(F32))
    patches_grad = d_flat.reshape(patches.shape)
    output = low(resid1 + row(fc2_bias) + second_own[0] + second_come[0].astype(F32))

    deep = merged.shape[1]
    *vectors, rel_grad, fc1_b_mine = whole(
        functools.partial(deliver_kernel, heads=heads),
        place,
        [
            shape_of((size,), F32)
            for size in (deep, deep, width, width, 3 * width, width, width, width, width)
        ]
        + [shape_of((rel_table.shape[0], heads), F32), shape_of((units // 128, 128), F32)],
        (all_sums, True),
        name="deliver",
    )
    fc1_b_out = lax.dynamic_index_in_dim(
        fc1_b_mine.reshape(wide, -1), wide_at, 0, keepdims=False
    )

    return (
        output,
        patches_grad,
        vectors[0],
        vectors[1],
        merge_out,
        vectors[2],
        vectors[3],
        qkv_out,
        vectors[4],
        rel_grad,
        proj_out,
        vectors[5],
        vectors[6],
        vectors[7],
        fc1_out,
        fc1_b_out,
        fc2_out,
        vectors[8],
    )


def solution(mesh):
    in_specs = (
        P(("wide", "narrow"), None, None),
        P("wide", None),
        P(),
        P(),
        P(),
        P(),
        P(),
        P(),
        P(),
        P(None, "narrow"),
        P("narrow", None),
        P(),
        P(),
        P(),
        P(None, "narrow"),
        P("narrow"),
        P("narrow", None),
        P(),
        P("wide", None),
    )
    out_specs = (
        P(("wide", "narrow"), None),
        P(("wide", "narrow"), None, None),
        P(),
        P(),
        P(("wide", "narrow"), None),
        P(),
        P(),
        P(("wide", "narrow"), None),
        P(),
        P(),
        P(("narrow", "wide"), None),
        P(),
        P(),
        P(),
        P("wide", "narrow"),
        P(("narrow", "wide")),
        P(("narrow", "wide"), None),
        P(),
    )
    return jax.shard_map(
        on_device, mesh=mesh, in_specs=in_specs, out_specs=out_specs, check_vma=False
    )
```

```python
import functools

import jax
import jax.numpy as jnp
from jax import lax
from jax.experimental import pallas as pl
from jax.experimental.pallas import tpu as pltpu
from jax.sharding import PartitionSpec as P

WIN = 10
WINDOW_TOKENS = WIN * WIN
QUERY_ROWS = 112
KEY_ROWS = 128
EPS = 1e-05
MEBI = 1024 * 1024
PROBS_ROOM = 52
WAIT_US = 100.0
WEIGHT_US = {"back1": 20, "proj_grad": 20, "back0": 20, "second_join": 20, "proj_join": 20}
WEIGHT_US |= dict.fromkeys(
    ("pack", "front", "cut", "pieces", "spread", "attend", "mine", "after", "slope", "feed", "second", "fc1_grad",
     "fc2_grad", "fc1_join", "fc2_join", "fc1_join2", "fc2_join2"), WAIT_US
)
FLOPS_PER_US = 10**9
BF = jnp.bfloat16
F32 = jnp.float32


def normalise(values):
    average = jnp.mean(values, -1, keepdims=True)
    centred = values - average
    inverse = lax.rsqrt(jnp.mean(centred * centred, -1, keepdims=True) + EPS)
    return centred * inverse, inverse


def norm_backward(grad_out, normal, inverse, gain):
    scaled = grad_out * gain
    return inverse * (
        scaled
        - jnp.mean(scaled, -1, keepdims=True)
        - normal * jnp.mean(scaled * normal, -1, keepdims=True)
    )


def matmul(left, right):
    return jnp.dot(left, right, preferred_element_type=jnp.float32)


def contract(left, right, left_dim, right_dim):
    return lax.dot_general(
        left, right, (((left_dim,), (right_dim,)), ((), ())), preferred_element_type=jnp.float32
    )


def low(array):
    return array.astype(BF)


def row(vector):
    return vector.reshape(1, -1)


def stays():
    return pl.BlockSpec(memory_space=pl.ANY)


def outside():
    return pl.BlockSpec(memory_space=pltpu.HBM)


def held():
    return pl.BlockSpec(memory_space=pltpu.VMEM)


def shape_of(shape, dtype):
    return jax.ShapeDtypeStruct(shape, dtype)


def whole(
    kernel, place, outs, *operands, leave=(), scratch=(), after=(), through=(), room=20, name=None
):
    arrays = [a for a, _ in operands]
    count, skip, given = len(arrays), len(after) + len(through), len(outs)

    def body(place_ref, *refs):
        own_outs = refs[count + skip : count + skip + given]
        kernel(place_ref, *refs[:count], *own_outs, *refs[count + skip + given + len(through) :])

    return pl.pallas_call(
        body,
        in_specs=[pl.BlockSpec(memory_space=pltpu.SMEM)]
        + [{True: held, False: outside, None: stays}[inside]() for _, inside in operands]
        + [stays()] * skip,
        out_specs=[outside() if k in leave else held() for k in range(given)]
        + [stays()] * len(through),
        out_shape=list(outs) + [shape_of(a.shape, a.dtype) for a in through],
        input_output_aliases={1 + count + len(after) + k: given + k for k in range(len(through))},
        scratch_shapes=list(scratch),
        compiler_params=pltpu.CompilerParams(vmem_limit_bytes=room * MEBI),
        cost_estimate=pl.CostEstimate(
            flops=int(WEIGHT_US.get(name, 5) * FLOPS_PER_US), bytes_accessed=0, transcendentals=0
        ),
        name=name,
    )(place, *arrays, *after, *through)


def tie(array, *after):
    def body(*refs):
        del refs

    return pl.pallas_call(
        body,
        in_specs=[stays()] * (1 + len(after)),
        out_specs=stays(),
        out_shape=shape_of(array.shape, array.dtype),
        input_output_aliases={0: 0},
        name="tie",
    )(array, *after)


def swap(array, axis, mask):
    size = lax.axis_size(axis)
    return lax.ppermute(array, axis, [(i, i ^ mask) for i in range(size)])


def turn(array, axis, step):
    size = lax.axis_size(axis)
    return lax.ppermute(array, axis, [(i, (i + step) % size) for i in range(size)])


def sum_all(vector):
    mask = 1
    while mask < lax.axis_size("wide"):
        vector = vector + swap(vector, "wide", mask)
        mask *= 2
    mask = 1
    while mask < lax.axis_size("narrow"):
        vector = vector + swap(vector, "narrow", mask)
        mask *= 2
    return vector


def sum_high(parts, high):
    take = lambda index: lax.dynamic_index_in_dim(parts, index, 0, keepdims=False)
    total = take(high).astype(F32)
    for j in range(1, parts.shape[0]):
        total = total + swap(low(take(high ^ j)), "wide", 8 * j).astype(F32)
    return total


def grad_kernel(place_ref, *refs, lefts, rights, block, rows, riding):
    left_refs, right_refs = refs[: len(lefts)], refs[len(lefts) : len(lefts) + len(rights)]
    kept_ref, sent_ref, total_ref = refs[-3:]
    core = place_ref[1]
    if riding:
        give_sums(sent_ref, kept_ref.shape[0], refs[-4][...])

    @pl.loop(0, kept_ref.shape[0])
    def _(step):
        at = pl.ds(pl.multiple_of(step * block, block), block)
        total = None
        for l_ref, l_at, r_ref, r_at in zip(left_refs, lefts, right_refs, rights):
            left = l_ref[:, at] if l_at is None else l_ref[l_at, :, at]
            right = r_ref[: left.shape[0]] if r_at is None else r_ref[r_at]
            right = low(right)
            part = contract(left, right, 0, 0)
            total = part if total is None else total + part
        total_ref[...] = total
        for s in range(block // (2 * rows)):
            mine = pl.multiple_of((2 * s + core) * rows, rows)
            theirs = pl.multiple_of((2 * s + 1 - core) * rows, rows)
            kept_ref[step, s * rows : (s + 1) * rows] = total_ref[pl.ds(mine, rows)]
            sent_ref[step, s * rows : (s + 1) * rows] = low(total_ref[pl.ds(theirs, rows)])


def grad_call(place, lefts, rights, block, rows, name, after=(), sums=None):
    split = lambda item: item if isinstance(item, tuple) else (item, None)
    left_arrays, left_at = zip(*map(split, lefts))
    right_arrays, right_at = zip(*map(split, rights))
    deep, width = left_arrays[0].shape[-1], right_arrays[0].shape[-1]
    shape = (deep // block, block // 2, width)
    return whole(
        functools.partial(
            grad_kernel, lefts=left_at, rights=right_at, block=block, rows=rows,
            riding=sums is not None,
        ),
        place,
        [shape_of(shape, F32), shape_of((shape[0] + (sums is not None), *shape[1:]), BF)],
        *((a, True) for a in left_arrays + right_arrays + (() if sums is None else (sums,))),
        scratch=[pltpu.VMEM((block, width), F32)],
        after=after,
        name=name,
    )


def add_up(refs, lead, rows):
    total = None
    for ref in refs:
        part = ref[lead, rows, :].astype(F32)
        total = part if total is None else total + part
    return total


def join_call(place, groups, outs, name, after=(), through=(), sums=None):
    width = groups[0][0].shape[2]
    counts = [len(sources) for sources in groups]
    count = sum(counts)
    rows_of = [pieces[0]((0, 0, 0))[3] for _, pieces in outs]
    more = -(-sums[0].shape[0] // rows_of[1]) if sums else 0
    shapes = [
        shape_of((len(pieces) + (more if k else 0), rows, width), dtype)
        for k, ((dtype, pieces), rows) in enumerate(zip(outs, rows_of))
    ]
    if sums:
        shapes = [shape_of(sums[0].shape, F32)] + shapes

    def kernel(place_ref, *refs):
        place_now = (place_ref[0], place_ref[1], place_ref[2])
        ins, out_refs = refs[:count], refs[count:]
        if sums:
            own_ref, total_ref, out_refs = refs[count], refs[count + 1], refs[count + 2 :]
            total = own_ref[...] + take_sums(ins[counts[0] - 1], sums[1], own_ref.shape[0])
            total_ref[...] = total
        at = [sum(counts[:g]) for g in range(len(counts))]
        for k, (out_ref, (dtype, pieces)) in enumerate(zip(out_refs, outs)):
            for n, piece in enumerate(pieces):
                group, lead, start, rows = piece(place_now)
                if not isinstance(start, int):
                    start = pl.multiple_of(start, rows)
                part = add_up(ins[at[group] : at[group] + counts[group]], lead, pl.ds(start, rows))
                out_ref[n] = part.astype(dtype)
            if sums and k:
                give_sums(out_ref, len(pieces), total)

    arrays = [s for sources in groups for s in sources] + ([sums[0]] if sums else [])
    return whole(
        kernel, place, shapes, *((s, True) for s in arrays), after=after, through=through, name=name
    )


def give_sums(ref, first, values):
    parts = low(values)
    size = ref.shape[1]
    for k in range(parts.shape[0] // size):
        ref[first + k] = parts[k * size : (k + 1) * size]
    rest = parts.shape[0] % size
    if rest:
        ref[first + parts.shape[0] // size, :rest] = parts[parts.shape[0] - rest :]


def take_sums(ref, first, rows):
    size = ref.shape[1]
    blocks = [ref[first + k].astype(F32) for k in range(-(-rows // size))]
    return (jnp.concatenate(blocks, 0) if len(blocks) > 1 else blocks[0])[:rows]


def cut_kernel(place_ref, merged_ref, own_ref, sent_ref, onward_ref):
    quad = place_ref[2]
    lanes = own_ref.shape[1]
    take = lambda j: merged_ref[:, pl.ds(pl.multiple_of((quad ^ j) * lanes, lanes), lanes)]
    own_ref[...] = take(0)
    sent_ref[0] = take(2)
    sent_ref[1] = take(3)
    onward_ref[...] = take(1)


def pack_kernel(
    place_ref, proj_ref, table_ref, message_ref
):
    part = proj_ref.shape[0] // 8
    own_heads = table_ref.shape[1]
    room = message_ref.shape[1] // 2
    eighth = place_ref[2] * 2 + place_ref[1]
    message_ref[:part] = proj_ref[pl.ds(pl.multiple_of(eighth * part, part), part), :]
    offsets = table_ref.shape[0]
    table = jnp.concatenate(
        [table_ref[...], jnp.zeros((offsets, 128 - own_heads), F32)], 1
    )
    table = jnp.concatenate([table, jnp.zeros((room - offsets, 128), F32)], 0)
    table = jnp.transpose(table)[:own_heads]
    high = low(table).astype(F32)
    rows = jnp.concatenate([high, table - high], 1)
    spare = message_ref.shape[0] - part - own_heads
    message_ref[part:] = low(jnp.concatenate([rows, jnp.zeros((spare, 2 * room), F32)], 0))


def pieces_kernel(place_ref, *refs, part):
    del place_ref
    for j, ref in enumerate(refs[:-1]):
        refs[-1][j * part : (j + 1) * part] = ref[:part]


def front_kernel(
    place_ref, flat_ref, mg_ref, ms_ref, n1g_ref, n1s_ref, qb_ref, mw_any, qw_any,
    merged_ref, resid0_ref, normed1_ref, qkv_ref, mw_ref, qw_ref, sems,
):
    copy_m = pltpu.make_async_copy(mw_any, mw_ref, sems.at[0])
    copy_q = pltpu.make_async_copy(qw_any, qw_ref, sems.at[1])
    copy_m.start()
    copy_q.start()
    hat, _ = normalise(flat_ref[...].astype(F32))
    merged = low(hat * mg_ref[...] + ms_ref[...])
    merged_ref[...] = merged
    copy_m.wait()
    resid0 = matmul(merged, mw_ref[...])
    resid0_ref[...] = resid0
    hat1, _ = normalise(resid0)
    normed1 = low(hat1 * n1g_ref[...] + n1s_ref[...])
    normed1_ref[...] = normed1
    copy_q.wait()
    qkv_ref[...] = low(matmul(normed1, qw_ref[...]) + qb_ref[...])


def front_call(place, flat, mg, ms, n1g, n1s, qb, mw, qw):
    rows, deep = flat.shape
    width = mw.shape[1]
    return whole(
        front_kernel,
        place,
        [
            shape_of((rows, deep), BF),
            shape_of((rows, width), F32),
            shape_of((rows, width), BF),
            shape_of((rows, 3 * width), BF),
        ],
        (flat, True), (row(mg), True), (row(ms), True), (row(n1g), True), (row(n1s), True),
        (row(qb), True), (mw, False), (qw, False),
        scratch=[
            pltpu.VMEM(mw.shape, BF), pltpu.VMEM(qw.shape, BF), pltpu.SemaphoreType.DMA((2,)),
        ],
        room=28,
        name="front",
    )


def mine_kernel(place_ref, *refs):
    del place_ref
    rows = refs[0].shape[0]
    for q, ref in enumerate(refs[:-1]):
        refs[-1][q * rows : (q + 1) * rows] = ref[...]


def whole_proj(place_ref, own_ref, mine_ref, theirs_ref, proj_ref, groups):
    rank, core, quad = place_ref[0], place_ref[1], place_ref[2]
    shard = own_ref.shape[0]
    part = shard // 8
    proj_ref[pl.ds(pl.multiple_of(rank * shard, shard), shard), :] = own_ref[...]
    for k in range(4 * (groups - 1)):
        q, j = k // (groups - 1), k % (groups - 1)
        base = lax.rem(rank + groups - 1 - j, groups) * shard + (quad ^ q) * 2 * part
        rows = slice(k * part, (k + 1) * part)
        proj_ref[pl.ds(pl.multiple_of(base + core * part, part), part), :] = mine_ref[rows]
        proj_ref[pl.ds(pl.multiple_of(base + (1 - core) * part, part), part), :] = theirs_ref[rows]


def after_kernel(
    place_ref, heads_ref, resid0_ref, pb_ref, n2g_ref, n2s_ref, own_ref, mine_ref, theirs_ref,
    resid1_ref, normed2_ref, proj_ref, *, groups,
):
    whole_proj(place_ref, own_ref, mine_ref, theirs_ref, proj_ref, groups)
    resid1 = resid0_ref[...] + matmul(heads_ref[...], proj_ref[...]) + pb_ref[...]
    resid1_ref[...] = resid1
    hat2, _ = normalise(resid1)
    normed2_ref[...] = low(hat2 * n2g_ref[...] + n2s_ref[...])


SQRT_HALF = 0.5**0.5
DENSITY = 0.3989422804014327


def gelu_pair(values):
    below = 0.5 * (1.0 + lax.erf(values * SQRT_HALF))
    density = jnp.exp(-0.5 * values * values) * DENSITY
    return values * below, below + values * density


def slope_kernel(
    place_ref, dy_ref, fc2_ref, rows_ref, own_ref, out_ref, wide_ref, *, groups, pad, chunk
):
    tokens, width = own_ref.shape
    wide_ref[...] = dy_ref[...].astype(F32)
    fill = jnp.zeros((pad - tokens, width), F32)
    for j in range(groups):
        at = lax.rem(place_ref[0] + groups - j, groups) * tokens
        block = wide_ref[pl.ds(pl.multiple_of(at, 8), tokens), :]
        rows_ref[j * pad : (j + 1) * pad] = low(jnp.concatenate([block, fill], 0))
        if j == 0:
            own_ref[...] = low(block)

    @pl.loop(0, fc2_ref.shape[0] // chunk)
    def _(step):
        at = pl.ds(pl.multiple_of(step * chunk, chunk), chunk)
        out_ref[:, at] = contract(rows_ref[...], fc2_ref[at, :], 1, 1)


def feed_kernel(
    place_ref, n0_ref, n1_ref, n2_ref, n3_ref, d_act_ref, fc1_ref, fc1b_ref,
    act_ref, dpre_ref, all_ref, db_ref, o0_ref, o1_ref, o2_ref, o3_ref, *, pad, chunk,
):
    del place_ref
    rows, width = n0_ref.shape
    for j, ref in enumerate((n0_ref, n1_ref, n2_ref, n3_ref)):
        all_ref[j * pad : j * pad + rows, :] = ref[...]
        all_ref[j * pad + rows : (j + 1) * pad, :] = jnp.zeros((pad - rows, width), BF)

    @pl.loop(0, fc1_ref.shape[1] // chunk)
    def _(step):
        at = pl.ds(pl.multiple_of(step * chunk, chunk), chunk)
        pre = matmul(all_ref[...], fc1_ref[:, at]) + fc1b_ref[:, at]
        act, slope = gelu_pair(pre)
        act_ref[:, at] = low(act)
        d_low = low(d_act_ref[:, at] * slope)
        dpre_ref[:, at] = d_low
        db_ref[:, at] = jnp.sum(d_low.astype(F32), 0, keepdims=True)

    for j, ref in enumerate((o0_ref, o1_ref, o2_ref, o3_ref)):
        part = contract(dpre_ref[j * pad : (j + 1) * pad, :], fc1_ref[...], 1, 1)
        ref[...] = low(part[:rows])


def second_kernel(place_ref, act_ref, fc2_ref, kept_ref, sent_ref, *, pad, groups):
    rank = place_ref[0]
    rows = kept_ref.shape[1]
    for ref, k, flip in ((sent_ref, 0, 1), (sent_ref, 1, 3), (kept_ref, 0, 0), (kept_ref, 1, 2)):
        block = lax.rem(rank + groups - (rank ^ flip), groups)
        at = pl.ds(pl.multiple_of(block * pad, pad), pad)
        ref[k] = low(matmul(act_ref[at, :], fc2_ref[...])[:rows])


def back2_kernel(
    place_ref, c0_ref, c1_ref, c2_ref, c3_ref, resid1_ref, dy_ref, n2g_ref, own_ref, mine_ref, theirs_ref,
    dresid1_ref, dheads_ref, proj_ref, *, groups,
):
    whole_proj(place_ref, own_ref, mine_ref, theirs_ref, proj_ref, groups)
    rows = dheads_ref.shape[0]
    d_norm2 = (
        c0_ref[...].astype(F32) + c1_ref[...].astype(F32)
        + c2_ref[...].astype(F32) + c3_ref[...].astype(F32)
    )
    hat2, inv2 = normalise(resid1_ref[...])
    dy = dy_ref[...].astype(F32)
    d_resid1 = dy + norm_backward(d_norm2, hat2, inv2, n2g_ref[...])
    dresid1_ref[:rows] = d_resid1
    sums = (d_resid1, d_norm2 * hat2, d_norm2, dy)
    for k, part in enumerate(sums):
        dresid1_ref[rows + k : rows + k + 1] = jnp.sum(part, 0, keepdims=True)
    dheads_ref[...] = low(contract(low(d_resid1), proj_ref[...], 1, 1))


def back1_kernel(
    place_ref, d0_ref, d1_ref, d2_ref, d3_ref, dresid1_ref, resid0_ref, n1g_ref, qw_any,
    dresid0_ref, sums_ref, qw_ref, sems,
):
    rows, width = resid0_ref.shape
    quad = place_ref[2]
    lanes = width // 4
    copies = [
        pltpu.make_async_copy(qw_any.at[:, pl.ds(i * width, width)], qw_ref.at[i], sems.at[i])
        for i in range(3)
    ]
    for copy in copies:
        copy.start()
    hat1, inv1 = normalise(resid0_ref[...])
    d_norm1 = jnp.zeros((rows, width), F32)
    for i in range(3):
        copies[i].wait()
        for j, d_ref in enumerate((d0_ref, d1_ref, d2_ref, d3_ref)):
            part = d_ref[:, i * lanes : (i + 1) * lanes]
            at = pl.ds(pl.multiple_of((quad ^ j) * lanes, lanes), lanes)
            d_norm1 = d_norm1 + contract(part, qw_ref[i, :, at], 1, 1)
            sums_ref[2 + i : 3 + i, at] = jnp.sum(part.astype(F32), 0, keepdims=True)
    dresid0_ref[...] = low(
        dresid1_ref[:rows] + norm_backward(d_norm1, hat1, inv1, n1g_ref[...])
    )
    sums_ref[0:1] = jnp.sum(d_norm1 * hat1, 0, keepdims=True)
    sums_ref[1:2] = jnp.sum(d_norm1, 0, keepdims=True)


def back0_kernel(
    place_ref, dresid0_ref, flat_ref, mg_ref, mw_any, grad_ref, sums_ref, mw_ref, sems
):
    del place_ref
    copy = pltpu.make_async_copy(mw_any, mw_ref, sems.at[0])
    copy.start()
    hat, inv = normalise(flat_ref[...].astype(F32))
    copy.wait()
    d_merged = contract(dresid0_ref[...], mw_ref[...], 1, 1)
    grad_ref[...] = low(norm_backward(d_merged, hat, inv, mg_ref[...]))
    width = dresid0_ref.shape[1]
    gain = jnp.sum(d_merged * hat, 0, keepdims=True)
    shift = jnp.sum(d_merged, 0, keepdims=True)
    for i in range(gain.shape[1] // width):
        sums_ref[i : i + 1] = gain[:, i * width : (i + 1) * width]
        sums_ref[2 + i : 3 + i] = shift[:, i * width : (i + 1) * width]


SPAN = 2 * WIN - 1
OFFSETS = 384
STRIP = 256


def strip_picks(column, offsets_first):
    shape, o_dim = ((OFFSETS, STRIP), 0) if offsets_first else ((STRIP, OFFSETS), 1)
    offset = lax.broadcasted_iota(jnp.int32, shape, o_dim)
    lane = lax.broadcasted_iota(jnp.int32, shape, 1 - o_dim)
    wanted = (SPAN - 1 - lane // WIN) * SPAN + column - lane % WIN + WIN - 1
    hit = (offset == wanted) & (lane < SPAN * WIN)
    return jnp.where(hit, 1.0, 0.0).astype(BF)


def split3(values):
    first = low(values)
    rest = values - first.astype(F32)
    second = low(rest)
    third = low(rest - second.astype(F32))
    return first, second, third


def spread_kernel(place_ref, m0_ref, m1_ref, m2_ref, m3_ref, bias_ref, table_ref, *, part, groups):
    heads = table_ref.shape[0]
    own_heads = heads // groups
    room = m0_ref.shape[1] // 2
    for j, ref in enumerate((m0_ref, m1_ref, m2_ref, m3_ref)):
        both = ref[part : part + 2 * own_heads, :].astype(F32)[:own_heads]
        at = pl.multiple_of(lax.rem(place_ref[0] + groups - j, groups) * own_heads, own_heads)
        table_ref[pl.ds(at, own_heads), :] = both[:, :OFFSETS] + both[:, room : room + OFFSETS]
    table = table_ref[...]
    high = low(table)
    table = jnp.concatenate([high, low(table - high.astype(F32))], 0)
    for column in range(WIN):
        parts = matmul(table, strip_picks(column, True))
        strip = parts[:heads] + parts[heads:]
        for r in range(WIN):
            start = (WIN - 1 - r) * WIN
            at = (r * WIN + column) * heads
            bias_ref[at : at + heads, :] = strip[:, start : start + KEY_ROWS]
    bias_ref[WINDOW_TOKENS * heads :, :] = jnp.zeros(
        ((QUERY_ROWS - WINDOW_TOKENS) * heads, KEY_ROWS), F32
    )


def fold(grad_ref, heads):
    total = jnp.zeros((3 * heads, OFFSETS), F32)
    for column in range(WIN):
        strip = jnp.zeros((heads, STRIP), F32)
        for r in range(WIN):
            start = (WIN - 1 - r) * WIN
            at = (r * WIN + column) * heads
            part = grad_ref[at : at + heads, :]
            wide = jnp.concatenate([part, jnp.zeros((heads, STRIP - KEY_ROWS), F32)], 1)
            strip = strip + (pltpu.roll(wide, start, 1) if start else wide)
        total = total + matmul(jnp.concatenate(split3(strip), 0), strip_picks(column, False))
    return total[:heads] + total[heads : 2 * heads] + total[2 * heads :]


def window_rows(values, window, rows):
    part = values.astype(F32)[window * WINDOW_TOKENS : (window + 1) * WINDOW_TOKENS]
    zeros = jnp.zeros((rows - WINDOW_TOKENS, part.shape[1]), F32)
    return low(jnp.concatenate([part, zeros], 0))


def stack_heads(part, heads, head_dim):
    lane = lax.broadcasted_iota(jnp.int32, part.shape, 1) // head_dim
    zero = jnp.zeros_like(part)
    return jnp.concatenate([jnp.where(lane == h, part, zero) for h in range(heads)], 0)


def attend_kernel(
    place_ref, qkv_ref, bias_ref, mask_ref, out_ref, probs_any, probs_ref, sems, *, windows, head_dim
):
    del place_ref
    width = out_ref.shape[1]
    lanes = width // 4

    def keep(step):
        return pltpu.make_async_copy(probs_ref.at[step], probs_any.at[step], sems.at[step])

    @pl.loop(0, 4)
    def _(step):
        attend_group(
            step, qkv_ref, bias_ref, mask_ref, out_ref, probs_ref, windows, head_dim, width, lanes
        )
        keep(step).start()

    for step in range(4):
        keep(step).wait()


def attend_group(
    step, qkv_ref, bias_ref, mask_ref, out_ref, probs_ref, windows, head_dim, width, lanes
):
    heads, all_heads = lanes // head_dim, width // head_dim
    first = step * heads
    scale = head_dim ** (-0.5)
    at = lambda kind: pl.ds(pl.multiple_of(kind * width + step * lanes, lanes), lanes)
    q_all, k_all, v_all = (qkv_ref[:, at(kind)] for kind in range(3))
    outs = []
    for w in range(windows):
        query = window_rows(q_all, w, QUERY_ROWS)
        keys = stack_heads(window_rows(k_all, w, KEY_ROWS), heads, head_dim)
        values = stack_heads(window_rows(v_all, w, KEY_ROWS), heads, head_dim)
        scores = contract(query, keys, 1, 1) * scale
        mask = mask_ref[w]
        rounded = []
        for h in range(heads):
            bias = bias_ref[pl.ds(first + h, QUERY_ROWS, stride=all_heads), :]
            raw = scores[:, h * KEY_ROWS : (h + 1) * KEY_ROWS] + bias + mask
            expo = jnp.exp(raw - jnp.max(raw, -1, keepdims=True))
            probs = expo / jnp.sum(expo, -1, keepdims=True)
            probs_ref[step, w, h] = probs
            rounded.append(low(probs))
        mixed = matmul(jnp.concatenate(rounded, 1), values)
        outs.append(mixed[:WINDOW_TOKENS])
    out_ref[:, at(0)] = low(jnp.concatenate(outs, 0))


def attend_back_kernel(
    place_ref, qkv_ref, grad_ref, probs_any, d0_ref, d1_ref, d2_ref, d3_ref, table_ref, dbias_ref, probs_ref, sems,
    *, windows, head_dim
):
    width = grad_ref.shape[1]

    def fetch(step):
        return pltpu.make_async_copy(
            probs_any.at[place_ref[2] ^ step], probs_ref.at[step], sems.at[step]
        )

    for step in range(4):
        fetch(step).start()

    @pl.loop(0, 4)
    def _(step):
        fetch(step).wait()
        attend_back_group(
            place_ref[2] ^ step, step, qkv_ref, grad_ref, probs_ref, (d0_ref, d1_ref, d2_ref, d3_ref), dbias_ref,
            windows, head_dim, width, width // 4,
        )

    table_ref[...] = fold(dbias_ref, table_ref.shape[0])


def attend_back_group(
    group, step, qkv_ref, grad_ref, probs_ref, d_refs, dbias_ref,
    windows, head_dim, width, lanes,
):
    heads, all_heads = lanes // head_dim, width // head_dim
    first = group * heads
    scale = head_dim ** (-0.5)
    at = lambda kind: pl.ds(pl.multiple_of(kind * width + group * lanes, lanes), lanes)
    q_all, k_all, v_all = (qkv_ref[:, at(kind)] for kind in range(3))
    g_all = grad_ref[:, at(0)]
    all_q, all_k, all_v = [], [], []
    d_first = []
    for w in range(windows):
        query = stack_heads(window_rows(q_all, w, QUERY_ROWS), heads, head_dim)
        keys = stack_heads(window_rows(k_all, w, KEY_ROWS), heads, head_dim)
        values = stack_heads(window_rows(v_all, w, KEY_ROWS), heads, head_dim)
        plain = window_rows(g_all, w, QUERY_ROWS)
        grad = stack_heads(plain, heads, head_dim)
        d_probs = contract(plain, values, 1, 1)
        d_list, p_list = [], []
        for h in range(heads):
            probs = probs_ref[step, w, h]
            part = d_probs[:, h * KEY_ROWS : (h + 1) * KEY_ROWS]
            total = jnp.sum(part * probs, -1, keepdims=True)
            d_scores = low(probs * (part - total))
            d_list.append(d_scores)
            p_list.append(low(probs))
            if w == 0:
                d_first.append(d_scores.astype(F32))
            else:
                d_first[h] = d_first[h] + d_scores.astype(F32)
            if w == windows - 1:
                dbias_ref[pl.ds(first + h, QUERY_ROWS, stride=all_heads), :] = d_first[h]
        d_query = matmul(jnp.concatenate(d_list, 1), keys) * scale
        d_keys = contract(jnp.concatenate(d_list, 0), query, 0, 0) * scale
        d_values = contract(jnp.concatenate(p_list, 0), grad, 0, 0)
        all_q.append(d_query[:WINDOW_TOKENS])
        all_k.append(d_keys[:WINDOW_TOKENS])
        all_v.append(d_values[:WINDOW_TOKENS])
    result = jnp.concatenate(
        [low(jnp.concatenate(parts, 0)) for parts in (all_q, all_k, all_v)], 1
    )

    for k, d_ref in enumerate(d_refs):

        @pl.when(step == k)
        def _(d_ref=d_ref):
            d_ref[...] = result


def spots(heads, lines, vectors):
    columns = 3
    return [(k // columns, OFFSETS + 128 * (k % columns)) for k in range(vectors * lines)]


def collect_kernel(place_ref, s0_ref, s1_ref, d_ref, rel_ref, b_ref, out_ref):
    heads = rel_ref.shape[0]
    lines = s0_ref.shape[1] // 128
    out_ref[...] = jnp.zeros(out_ref.shape, F32)
    out_ref[:heads, :OFFSETS] = rel_ref[...]
    vectors = [ref[r : r + 1, :] for ref in (s0_ref, s1_ref) for r in range(ref.shape[0])]
    after = d_ref.shape[0] - 8
    vectors += [d_ref[after + r : after + r + 1, :] for r in range(4)]
    for k, (at, lane) in enumerate(spots(heads, lines, len(vectors))):
        piece = vectors[k // lines][:, 128 * (k % lines) : 128 * (k % lines + 1)]
        out_ref[at : at + 1, lane : lane + 128] = piece
    own = b_ref.shape[1] // 128
    first = heads + pl.multiple_of((place_ref[0] // 2) * own, own)
    block = jnp.concatenate([b_ref[:, k * 128 : (k + 1) * 128] for k in range(own)], 0)
    side = place_ref[0] % 2

    @pl.when(side == 0)
    def _():
        out_ref[pl.ds(first, own), 0:128] = block

    @pl.when(side == 1)
    def _():
        out_ref[pl.ds(first, own), 128:256] = block


def deliver_kernel(place_ref, all_ref, *refs, heads):
    *vector_refs, rel_ref, b_ref = refs
    rel_ref[...] = all_ref[:heads, : rel_ref.shape[1]]
    lines = [ref.shape[0] // 128 for ref in vector_refs]
    places = iter(spots(heads, 1, sum(lines)))
    for ref, count in zip(vector_refs, lines):
        for k in range(count):
            at, lane = next(places)
            ref[128 * k : 128 * (k + 1)] = all_ref[at, lane : lane + 128]
    own = b_ref.shape[0]
    first = heads + pl.multiple_of((place_ref[0] // 2) * own, own)
    side = place_ref[0] % 2

    @pl.when(side == 0)
    def _():
        b_ref[...] = all_ref[pl.ds(first, own), 0:128]

    @pl.when(side == 1)
    def _():
        b_ref[...] = all_ref[pl.ds(first, own), 128:256]


def columns_kernel(place_ref, b0_ref, b1_ref, b2_ref, b3_ref, own_ref, out_ref, sums_ref):
    rows = out_ref.shape[0]
    lanes = b0_ref.shape[2] // 3
    total = own_ref[...]
    for j, ref in enumerate((b0_ref, b1_ref, b2_ref, b3_ref)):
        for part in range(3):
            at = pl.multiple_of((part * 4 + (place_ref[2] ^ j)) * lanes, lanes)
            out_ref[:, pl.ds(at, lanes)] = ref[0, :rows, part * lanes : (part + 1) * lanes].astype(F32)
        if j:
            total = total + take_sums(ref, 1, own_ref.shape[0])
    sums_ref[...] = total


def on_device(
    patches,
    window_extent,
    merge_gain,
    merge_shift,
    merge_weight,
    norm1_gain,
    norm1_shift,
    qkv_weight,
    qkv_bias,
    rel_table,
    proj_weight,
    proj_bias,
    norm2_gain,
    norm2_shift,
    fc1_weight,
    fc1_bias,
    fc2_weight,
    fc2_bias,
    out_grad,
):
    groups, wide = lax.axis_size("narrow"), lax.axis_size("wide")
    devices = wide * groups
    highs = wide // 8
    wide_at, rank = lax.axis_index("wide"), lax.axis_index("narrow")
    core, quad, high = wide_at % 2, (wide_at // 2) % 4, wide_at // 8
    place = jnp.stack([rank, core, quad]).astype(jnp.int32)
    tokens = patches.shape[0]
    width = qkv_weight.shape[0]
    own_heads = rel_table.shape[1]
    heads = own_heads * groups
    head_dim = width // heads
    windows = tokens // WINDOW_TOKENS
    pad = tokens + (-tokens) % 16

    def arrange(array, order):
        if highs == 1:
            return array
        sizes = {"h": highs, "q": 4, "c": 2, "n": groups}
        cut = [sizes[k] for k in order]
        rest = array.shape[1]
        for size in cut:
            rest //= size
        at = order.index("h") + 1
        moved = [i + 1 for i in range(len(order)) if i + 1 != at] + [at, len(order) + 1]
        return jnp.transpose(array.reshape(-1, *cut, rest), [0] + moved).reshape(array.shape)

    def settle(array):
        if highs == 1:
            return array[0]
        return sum_high(array[0].reshape(highs, -1, array.shape[2]), high)

    part = proj_weight.shape[0] // 8
    message = whole(
        pack_kernel,
        place,
        [shape_of((part + own_heads + (-(part + own_heads)) % 16, width), BF)],
        (proj_weight, True),
        (rel_table, True),
        name="pack",
    )[0]
    messages = [turn(message, "narrow", step) for step in range(1, groups)]

    flat = patches.reshape(tokens, -1)
    merged, resid0, normed1, qkv = front_call(
        place, flat, merge_gain, merge_shift, norm1_gain, norm1_shift, qkv_bias,
        merge_weight, qkv_weight,
    )
    mine = whole(
        functools.partial(pieces_kernel, part=part),
        place,
        [shape_of(((groups - 1) * part, width), BF)],
        *((m, True) for m in messages),
        name="pieces",
    )
    mine = list(mine) + [swap(mine[0], "wide", 2 * j) for j in (1, 2, 3)]

    merged_own, merged_sent, merged_onward = whole(
        cut_kernel,
        place,
        [
            shape_of((tokens, merged.shape[1] // 4), BF),
            shape_of((2, tokens, merged.shape[1] // 4), BF),
            shape_of((tokens, merged.shape[1] // 4), BF),
        ],
        (arrange(merged, "hqcn"), True),
        name="cut",
    )
    merged_near = swap(merged_sent, "wide", 4)
    normed1_cut = arrange(normed1, "hqcn")
    normed1_near = swap(normed1_cut, "wide", 2)

    positions = jnp.arange(KEY_ROWS)
    extent = lax.dynamic_slice_in_dim(window_extent, rank * windows, windows, 0)
    valid = (
        (positions[None, :] // WIN < extent[:, 0:1])
        & (positions[None, :] % WIN < extent[:, 1:2])
        & (positions[None, :] < WINDOW_TOKENS)
    )
    mask = jnp.where(valid, 0.0, -1e30).astype(F32)[:, None, :]
    bias = whole(
        functools.partial(spread_kernel, part=part, groups=groups),
        place,
        [shape_of((QUERY_ROWS * heads, KEY_ROWS), F32)],
        (message, True),
        *((m, True) for m in messages),
        scratch=[pltpu.VMEM((heads, OFFSETS), F32)],
        name="spread",
    )[0]
    heads_out, probs = whole(
        functools.partial(attend_kernel, windows=windows, head_dim=head_dim),
        place,
        [
            shape_of((tokens, width), BF),
            shape_of((PROBS_ROOM, windows, heads // 4, QUERY_ROWS, KEY_ROWS), F32),
        ],
        (qkv, True), (bias, True), (mask, True),
        leave=(1,),
        scratch=[
            pltpu.VMEM((4, windows, heads // 4, QUERY_ROWS, KEY_ROWS), F32),
            pltpu.SemaphoreType.DMA((4,)),
        ],
        name="attend",
    )

    mine = whole(
        mine_kernel,
        place,
        [shape_of((4 * mine[0].shape[0], width), BF)],
        *((m, True) for m in mine),
        after=(heads_out, merged_near, normed1_near),
        name="mine",
    )[0]
    theirs = swap(mine, "wide", 1)
    resid1, normed2 = whole(
        functools.partial(after_kernel, groups=groups),
        place,
        [shape_of((tokens, width), F32), shape_of((tokens, width), BF)],
        (heads_out, True), (resid0, True),
        (row(proj_bias), True), (row(norm2_gain), True), (row(norm2_shift), True),
        (proj_weight, True), (mine, True), (theirs, True),
        scratch=[pltpu.VMEM((width, width), BF)],
        name="after",
    )
    blocks = [normed2] + [turn(normed2, "narrow", step) for step in range(1, groups)]

    merged_onward = jnp.stack([tie(merged_onward, normed2), merged_near[1]])
    merged_far = swap(merged_onward, "wide", 2)
    normed1_both = jnp.stack([normed1_cut, tie(normed1_near, normed2)])
    normed1_far = swap(normed1_both, "wide", 4)

    total, units = groups * pad, fc1_weight.shape[1]
    dy_rows, dy_own, d_act = whole(
        functools.partial(slope_kernel, groups=groups, pad=pad, chunk=256),
        place,
        [
            shape_of((total, width), BF),
            shape_of((tokens, width), BF),
            shape_of((total, units), F32),
        ],
        (out_grad, True), (fc2_weight, True),
        scratch=[pltpu.VMEM(out_grad.shape, F32)],
        after=(normed2,),
        name="slope",
    )
    act, d_pre, rows_all, fc1_b_grad, *chunks = whole(
        functools.partial(feed_kernel, pad=pad, chunk=256),
        place,
        [
            shape_of((total, units), BF),
            shape_of((total, units), BF),
            shape_of((total, width), BF),
            shape_of((1, units), F32),
        ]
        + [shape_of((tokens, width), BF)] * 4,
        *((b, True) for b in blocks), (d_act, True), (fc1_weight, True), (row(fc1_bias), True),
        after=(normed1_far, merged_far),
        name="feed",
    )
    arrived = [chunks[0]] + [turn(chunks[j], "narrow", -j) for j in range(1, groups)]

    fc1_kept, fc1_sent = grad_call(place, [arrange(rows_all, "hqc")], [d_pre], 256, 128, "fc1_grad")
    fc2_kept, fc2_sent = grad_call(place, [arrange(act, "hqc")], [dy_rows], 256, 128, "fc2_grad")
    fc1_come, fc2_come = swap(fc1_sent, "wide", 1), swap(fc2_sent, "wide", 1)
    fc1_kept, fc1_sent = join_call(
        place, [(fc1_kept, fc1_come)],
        [
            (F32, [lambda p, y=y: (0, 2 * y + p[2] % 2, 0, 128) for y in range(2)]),
            (BF, [lambda p, y=y: (0, 2 * y + 1 - p[2] % 2, 0, 128) for y in range(2)]),
        ],
        "fc1_join",
    )
    fc2_kept, fc2_sent = join_call(
        place, [(fc2_kept, fc2_come)],
        [
            (F32, [lambda p, x=x: (0, 2 * (p[2] // 2) + x, 0, 128) for x in range(2)]),
            (BF, [lambda p, x=x: (0, 2 * (1 - p[2] // 2) + x, 0, 128) for x in range(2)]),
        ],
        "fc2_join",
    )
    fc1_come, fc2_come = swap(fc1_sent, "wide", 2), swap(fc2_sent, "wide", 4)
    fc1_kept, fc1_sent = join_call(
        place, [(fc1_kept, fc1_come)],
        [
            (F32, [lambda p: (0, p[2] // 2, 0, 128)]),
            (BF, [lambda p: (0, 1 - p[2] // 2, 0, 128)]),
        ],
        "fc1_join2",
    )
    fc2_kept, fc2_sent = join_call(
        place, [(fc2_kept, fc2_come)],
        [
            (F32, [lambda p: (0, p[2] % 2, 0, 128)]),
            (BF, [lambda p: (0, 1 - p[2] % 2, 0, 128)]),
        ],
        "fc2_join2",
    )
    fc1_come, fc2_come = swap(fc1_sent, "wide", 4), swap(fc2_sent, "wide", 2)
    second_kept, second_sent = whole(
        functools.partial(second_kernel, pad=pad, groups=groups),
        place,
        [shape_of((2, tokens, width), BF)] * 2,
        (act, True),
        (fc2_weight, True),
        name="second",
    )
    d_resid1, d_heads, second_sent = whole(
        functools.partial(back2_kernel, groups=groups),
        place,
        [shape_of((tokens + 8, width), F32), shape_of((tokens, width), BF)],
        *((a, True) for a in arrived),
        (resid1, True), (dy_own, True), (row(norm2_gain), True),
        (proj_weight, True), (mine, True), (theirs, True),
        scratch=[pltpu.VMEM((width, width), BF)],
        after=(fc1_sent, fc2_sent),
        through=(second_sent,),
        name="back2",
    )
    second_come = swap(second_sent, "narrow", 1)
    *d_parts, rel_part = whole(
        functools.partial(attend_back_kernel, windows=windows, head_dim=head_dim),
        place,
        [shape_of((tokens, 3 * width // 4), BF)] * 4 + [shape_of((heads, OFFSETS), F32)],
        (qkv, True), (d_heads, True), (probs, False),
        scratch=[
            pltpu.VMEM((QUERY_ROWS * heads, KEY_ROWS), F32),
            pltpu.VMEM((4, *probs.shape[1:]), F32),
            pltpu.SemaphoreType.DMA((4,)),
        ],
        after=(fc1_come, fc2_come),
        name="attend_back",
    )
    d_come = [swap(d_parts[j], "wide", 2 * j) for j in (1, 2, 3)]

    d_resid0, sums1 = whole(
        back1_kernel,
        place,
        [shape_of((tokens, width), BF), shape_of((5, width), F32)],
        *((d, True) for d in d_parts), (d_resid1, True), (resid0, True),
        (row(norm1_gain), True), (qkv_weight, False),
        scratch=[
            pltpu.VMEM((3, width, width), BF),
            pltpu.SemaphoreType.DMA((3,)),
        ],
        name="back1",
    )
    d_flat, sums0 = whole(
        back0_kernel,
        place,
        [shape_of(flat.shape, BF), shape_of((2 * flat.shape[1] // width, width), F32)],
        (d_resid0, True), (flat, True), (row(merge_gain), True), (merge_weight, False),
        scratch=[pltpu.VMEM(merge_weight.shape, BF), pltpu.SemaphoreType.DMA((1,))],
        name="back0",
    )

    second_own, second_sent = join_call(
        place, [(second_kept, second_come)],
        [(F32, [lambda p: (0, 0, 0, tokens)]), (BF, [lambda p: (0, 1, 0, tokens)])],
        "second_join",
    )
    second_come = swap(second_sent, "narrow", 2)

    proj_kept, proj_sent = grad_call(
        place, [arrange(heads_out, "nhqc")], [d_resid1], 256, 32, "proj_grad", after=(d_resid0,)
    )
    proj_come = swap(proj_sent, "wide", 1)

    side = lambda pick_x: [
        lambda p, n=n, y=y: (0, n, (2 * y + pick_x(p[2] % 2)) * 32, 32)
        for n in range(groups) for y in range(2)
    ]
    proj_kept, proj_sent = join_call(
        place, [(proj_kept, proj_come)],
        [(F32, side(lambda x: x)), (BF, side(lambda x: 1 - x))],
        "proj_join",
    )
    proj_come = swap(proj_sent, "wide", 2)

    own_sums, d_resid0 = whole(
        collect_kernel,
        place,
        [shape_of((48, 3 * width // 4), F32)],
        (sums0, True), (sums1, True), (d_resid1, True), (rel_part, True), (fc1_b_grad, True),
        after=(*d_come, second_sent, proj_sent),
        through=(d_resid0,),
        name="collect",
    )
    r_come = [swap(d_resid0, "wide", 2 * j) for j in (1, 2, 3)]
    qkv_kept, qkv_sent = grad_call(
        place,
        [normed1_cut, (normed1_both, 1), (normed1_far, 0), (normed1_far, 1)],
        [d_parts[0], *d_come],
        256, 128, "qkv_grad", sums=own_sums, after=(second_sent,),
    )
    qkv_come = swap(qkv_sent, "wide", 1)
    rows = 128 // groups
    qkv_pieces = lambda flip: [
        lambda p, g=g, k=k: (0, g, (2 * k + (p[0] + flip) % 2) * rows, rows)
        for k in range(2) for g in range(4)
    ]
    own_sums, qkv_kept, qkv_sent = join_call(
        place, [(qkv_kept, qkv_come)], [(F32, qkv_pieces(0)), (BF, qkv_pieces(1))], "qkv_join",
        sums=(own_sums, 4),
    )
    qkv_come = swap(qkv_sent, "narrow", 1)

    merge_kept, merge_sent = grad_call(
        place,
        [merged_own, (merged_far, 0), (merged_near, 0), (merged_far, 1)],
        [d_resid0, *r_come],
        merged_own.shape[1], merged_own.shape[1] // 2, "merge_grad", after=(qkv_sent,),
    )
    merge_come = swap(merge_sent, "wide", 1)

    second_pieces = lambda flip: [
        lambda p, g=g: (0, ((p[0] // 2 + flip) % 2) * 4 + g, 0, rows) for g in range(4)
    ]
    own_sums, qkv_kept, qkv_sent = join_call(
        place, [(qkv_kept, qkv_come)],
        [(F32, second_pieces(0)), (BF, second_pieces(1))],
        "qkv_join2",
        sums=(own_sums, 8),
        after=(merge_sent,),
    )
    qkv_come = swap(qkv_sent, "narrow", 2)
    merge_rows = merged_own.shape[1] // 2 // groups
    merge_pieces = lambda flip: [
        lambda p, k=k: (0, 0, (2 * k + (p[0] + flip) % 2) * merge_rows, merge_rows)
        for k in range(2)
    ]
    merge_kept, merge_sent, fc1_come, fc2_come, d_flat = join_call(
        place, [(merge_kept, merge_come)],
        [(F32, merge_pieces(0)), (BF, merge_pieces(1))],
        "merge_join",
        after=(qkv_sent,),
        through=(fc1_come, fc2_come, d_flat),
    )
    merge_first = merge_sent
    merge_come = swap(merge_sent, "narrow", 1)

    last_pieces = lambda flip, size: [lambda p: (0, (p[0] // 2 + flip) % 2, 0, size)]
    merge_kept, merge_sent = join_call(
        place, [(merge_kept, merge_come)],
        [(F32, last_pieces(0, merge_rows)), (BF, last_pieces(1, merge_rows))],
        "merge_join2",
        after=(qkv_sent,),
    )
    merge_last = merge_sent
    merge_come = swap(merge_sent, "narrow", 2)

    proj_kept, proj_sent = join_call(
        place, [(proj_kept, proj_come)],
        [
            (F32, [lambda p, n=n: (0, 2 * n + p[2] // 2, 0, 32) for n in range(groups)]),
            (BF, [lambda p, n=n: (0, 2 * n + 1 - p[2] // 2, 0, 32) for n in range(groups)]),
        ],
        "proj_join2",
        after=(merge_first,),
    )
    proj_come = swap(proj_sent, "wide", 4)
    proj_pieces = lambda flip: [
        lambda p, k=k: (0, 2 * k + (p[0] + flip) % 2, 0, 32) for k in range(2)
    ]
    proj_kept, proj_sent = join_call(
        place, [(proj_kept, proj_come)], [(F32, proj_pieces(0)), (BF, proj_pieces(1))],
        "proj_join3",
        after=(merge_sent,),
    )
    proj_come = swap(proj_sent, "narrow", 1)
    proj_kept, proj_sent = join_call(
        place, [(proj_kept, proj_come)],
        [(F32, last_pieces(0, 32)), (BF, last_pieces(1, 32))],
        "proj_join4",
    )
    proj_come = swap(proj_sent, "narrow", 2)

    own_sums, *cuts = join_call(
        place, [(qkv_kept, qkv_come)],
        [(BF, [lambda p, j=j: (0, p[2] ^ j, 0, rows)]) for j in range(4)],
        "qkv_join3",
        sums=(own_sums, 4),
        after=(merge_last,),
    )
    cuts = [cuts[0]] + [swap(cuts[j], "wide", 2 * j) for j in (1, 2, 3)]
    qkv_out, all_sums = whole(
        columns_kernel,
        place,
        [shape_of((rows, 3 * width), F32), shape_of(own_sums.shape, F32)],
        *((c, True) for c in cuts), (own_sums, True),
        name="columns",
    )
    qkv_out = settle(qkv_out[None])
    mask = 8
    while mask < wide:
        all_sums = all_sums + swap(all_sums, "wide", mask)
        mask *= 2
    merge_out = settle(merge_kept + merge_come.astype(F32))
    proj_out = settle(proj_kept + proj_come.astype(F32))

    fc1_out = settle(fc1_kept + fc1_come.astype(F32))
    fc2_out = settle(fc2_kept + fc2_come.astype(F32))
    patches_grad = d_flat.reshape(patches.shape)
    output = low(resid1 + row(fc2_bias) + second_own[0] + second_come[0].astype(F32))

    deep = merged.shape[1]
    *vectors, rel_grad, fc1_b_mine = whole(
        functools.partial(deliver_kernel, heads=heads),
        place,
        [
            shape_of((size,), F32)
            for size in (deep, deep, width, width, 3 * width, width, width, width, width)
        ]
        + [shape_of((heads, rel_table.shape[0]), F32), shape_of((units // 128, 128), F32)],
        (all_sums, True),
        name="deliver",
    )
    fc1_b_out = lax.dynamic_index_in_dim(
        fc1_b_mine.reshape(wide, -1), wide_at, 0, keepdims=False
    )

    return (
        output,
        patches_grad,
        vectors[0],
        vectors[1],
        merge_out,
        vectors[2],
        vectors[3],
        qkv_out,
        vectors[4],
        jnp.transpose(rel_grad),
        proj_out,
        vectors[5],
        vectors[6],
        vectors[7],
        fc1_out,
        fc1_b_out,
        fc2_out,
        vectors[8],
    )


def solution(mesh):
    in_specs = (
        P(("wide", "narrow"), None, None),
        P("wide", None),
        P(),
        P(),
        P(),
        P(),
        P(),
        P(),
        P(),
        P(None, "narrow"),
        P("narrow", None),
        P(),
        P(),
        P(),
        P(None, "narrow"),
        P("narrow"),
        P("narrow", None),
        P(),
        P("wide", None),
    )
    out_specs = (
        P(("wide", "narrow"), None),
        P(("wide", "narrow"), None, None),
        P(),
        P(),
        P(("wide", "narrow"), None),
        P(),
        P(),
        P(("wide", "narrow"), None),
        P(),
        P(),
        P(("narrow", "wide"), None),
        P(),
        P(),
        P(),
        P("wide", "narrow"),
        P(("narrow", "wide")),
        P(("narrow", "wide"), None),
        P(),
    )
    return jax.shard_map(
        on_device, mesh=mesh, in_specs=in_specs, out_specs=out_specs, check_vma=False
    )
```

```python
import functools

import jax
import jax.numpy as jnp
from jax import lax
from jax.experimental import pallas as pl
from jax.experimental.pallas import tpu as pltpu
from jax.sharding import PartitionSpec as P

WIN = 10
WINDOW_TOKENS = WIN * WIN
QUERY_ROWS = 112
KEY_ROWS = 128
EPS = 1e-05
MEBI = 1024 * 1024
PROBS_ROOM = 52
WAIT_US = 100.0
WEIGHT_US = {"back1": 20, "proj_grad": 20, "back0": 20, "second_join": 20, "proj_join": 20}
WEIGHT_US |= dict.fromkeys(
    ("pack", "front", "cut", "pieces", "spread", "attend", "mine", "after", "slope", "feed", "second", "fc1_grad",
     "fc2_grad", "fc1_join", "fc2_join", "fc1_join2", "fc2_join2"), WAIT_US
)
FLOPS_PER_US = 10**9
BF = jnp.bfloat16
F32 = jnp.float32


def normalise(values):
    average = jnp.mean(values, -1, keepdims=True)
    centred = values - average
    inverse = lax.rsqrt(jnp.mean(centred * centred, -1, keepdims=True) + EPS)
    return centred * inverse, inverse


def norm_backward(grad_out, normal, inverse, gain):
    scaled = grad_out * gain
    return inverse * (
        scaled
        - jnp.mean(scaled, -1, keepdims=True)
        - normal * jnp.mean(scaled * normal, -1, keepdims=True)
    )


def matmul(left, right):
    return jnp.dot(left, right, preferred_element_type=jnp.float32)


def contract(left, right, left_dim, right_dim):
    return lax.dot_general(
        left, right, (((left_dim,), (right_dim,)), ((), ())), preferred_element_type=jnp.float32
    )


def low(array):
    return array.astype(BF)


def row(vector):
    return vector.reshape(1, -1)


def stays():
    return pl.BlockSpec(memory_space=pl.ANY)


def outside():
    return pl.BlockSpec(memory_space=pltpu.HBM)


def held():
    return pl.BlockSpec(memory_space=pltpu.VMEM)


def shape_of(shape, dtype):
    return jax.ShapeDtypeStruct(shape, dtype)


def whole(
    kernel, place, outs, *operands, leave=(), scratch=(), after=(), through=(), room=20, name=None
):
    arrays = [a for a, _ in operands]
    count, skip, given = len(arrays), len(after) + len(through), len(outs)

    def body(place_ref, *refs):
        own_outs = refs[count + skip : count + skip + given]
        kernel(place_ref, *refs[:count], *own_outs, *refs[count + skip + given + len(through) :])

    return pl.pallas_call(
        body,
        in_specs=[pl.BlockSpec(memory_space=pltpu.SMEM)]
        + [{True: held, False: outside, None: stays}[inside]() for _, inside in operands]
        + [stays()] * skip,
        out_specs=[outside() if k in leave else held() for k in range(given)]
        + [stays()] * len(through),
        out_shape=list(outs) + [shape_of(a.shape, a.dtype) for a in through],
        input_output_aliases={1 + count + len(after) + k: given + k for k in range(len(through))},
        scratch_shapes=list(scratch),
        compiler_params=pltpu.CompilerParams(vmem_limit_bytes=room * MEBI),
        cost_estimate=pl.CostEstimate(
            flops=int(WEIGHT_US.get(name, 5) * FLOPS_PER_US), bytes_accessed=0, transcendentals=0
        ),
        name=name,
    )(place, *arrays, *after, *through)


def tie(array, *after):
    def body(*refs):
        del refs

    return pl.pallas_call(
        body,
        in_specs=[stays()] * (1 + len(after)),
        out_specs=stays(),
        out_shape=shape_of(array.shape, array.dtype),
        input_output_aliases={0: 0},
        name="tie",
    )(array, *after)


def swap(array, axis, mask):
    size = lax.axis_size(axis)
    return lax.ppermute(array, axis, [(i, i ^ mask) for i in range(size)])


def turn(array, axis, step):
    size = lax.axis_size(axis)
    return lax.ppermute(array, axis, [(i, (i + step) % size) for i in range(size)])


def sum_all(vector):
    mask = 1
    while mask < lax.axis_size("wide"):
        vector = vector + swap(vector, "wide", mask)
        mask *= 2
    mask = 1
    while mask < lax.axis_size("narrow"):
        vector = vector + swap(vector, "narrow", mask)
        mask *= 2
    return vector


def sum_high(parts, high):
    take = lambda index: lax.dynamic_index_in_dim(parts, index, 0, keepdims=False)
    total = take(high).astype(F32)
    for j in range(1, parts.shape[0]):
        total = total + swap(low(take(high ^ j)), "wide", 8 * j).astype(F32)
    return total


def grad_kernel(place_ref, *refs, lefts, rights, block, rows, riding):
    left_refs, right_refs = refs[: len(lefts)], refs[len(lefts) : len(lefts) + len(rights)]
    kept_ref, sent_ref, total_ref = refs[-3:]
    core = place_ref[1]
    if riding:
        give_sums(sent_ref, kept_ref.shape[0], refs[-4][...])

    @pl.loop(0, kept_ref.shape[0])
    def _(step):
        at = pl.ds(pl.multiple_of(step * block, block), block)
        total = None
        for l_ref, l_at, r_ref, r_at in zip(left_refs, lefts, right_refs, rights):
            left = l_ref[:, at] if l_at is None else l_ref[l_at, :, at]
            right = r_ref[: left.shape[0]] if r_at is None else r_ref[r_at]
            right = low(right)
            part = contract(left, right, 0, 0)
            total = part if total is None else total + part
        total_ref[...] = total
        for s in range(block // (2 * rows)):
            mine = pl.multiple_of((2 * s + core) * rows, rows)
            theirs = pl.multiple_of((2 * s + 1 - core) * rows, rows)
            kept_ref[step, s * rows : (s + 1) * rows] = total_ref[pl.ds(mine, rows)]
            sent_ref[step, s * rows : (s + 1) * rows] = low(total_ref[pl.ds(theirs, rows)])


def grad_call(place, lefts, rights, block, rows, name, after=(), sums=None):
    split = lambda item: item if isinstance(item, tuple) else (item, None)
    left_arrays, left_at = zip(*map(split, lefts))
    right_arrays, right_at = zip(*map(split, rights))
    deep, width = left_arrays[0].shape[-1], right_arrays[0].shape[-1]
    shape = (deep // block, block // 2, width)
    return whole(
        functools.partial(
            grad_kernel, lefts=left_at, rights=right_at, block=block, rows=rows,
            riding=sums is not None,
        ),
        place,
        [shape_of(shape, F32), shape_of((shape[0] + (sums is not None), *shape[1:]), BF)],
        *((a, True) for a in left_arrays + right_arrays + (() if sums is None else (sums,))),
        scratch=[pltpu.VMEM((block, width), F32)],
        after=after,
        name=name,
    )


def add_up(refs, lead, rows):
    total = None
    for ref in refs:
        part = ref[lead, rows, :].astype(F32)
        total = part if total is None else total + part
    return total


def join_call(place, groups, outs, name, after=(), through=(), sums=None):
    width = groups[0][0].shape[2]
    counts = [len(sources) for sources in groups]
    count = sum(counts)
    rows_of = [pieces[0]((0, 0, 0))[3] for _, pieces in outs]
    more = -(-sums[0].shape[0] // rows_of[1]) if sums else 0
    shapes = [
        shape_of((len(pieces) + (more if k else 0), rows, width), dtype)
        for k, ((dtype, pieces), rows) in enumerate(zip(outs, rows_of))
    ]
    if sums:
        shapes = [shape_of(sums[0].shape, F32)] + shapes

    def kernel(place_ref, *refs):
        place_now = (place_ref[0], place_ref[1], place_ref[2])
        ins, out_refs = refs[:count], refs[count:]
        if sums:
            own_ref, total_ref, out_refs = refs[count], refs[count + 1], refs[count + 2 :]
            total = own_ref[...] + take_sums(ins[counts[0] - 1], sums[1], own_ref.shape[0])
            total_ref[...] = total
        at = [sum(counts[:g]) for g in range(len(counts))]
        for k, (out_ref, (dtype, pieces)) in enumerate(zip(out_refs, outs)):
            for n, piece in enumerate(pieces):
                group, lead, start, rows = piece(place_now)
                if not isinstance(start, int):
                    start = pl.multiple_of(start, rows)
                part = add_up(ins[at[group] : at[group] + counts[group]], lead, pl.ds(start, rows))
                out_ref[n] = part.astype(dtype)
            if sums and k:
                give_sums(out_ref, len(pieces), total)

    arrays = [s for sources in groups for s in sources] + ([sums[0]] if sums else [])
    return whole(
        kernel, place, shapes, *((s, True) for s in arrays), after=after, through=through, name=name
    )


def give_sums(ref, first, values):
    parts = low(values)
    size = ref.shape[1]
    for k in range(parts.shape[0] // size):
        ref[first + k] = parts[k * size : (k + 1) * size]
    rest = parts.shape[0] % size
    if rest:
        ref[first + parts.shape[0] // size, :rest] = parts[parts.shape[0] - rest :]


def take_sums(ref, first, rows):
    size = ref.shape[1]
    blocks = [ref[first + k].astype(F32) for k in range(-(-rows // size))]
    return (jnp.concatenate(blocks, 0) if len(blocks) > 1 else blocks[0])[:rows]


def cut_kernel(place_ref, merged_ref, own_ref, sent_ref, onward_ref):
    quad = place_ref[2]
    lanes = own_ref.shape[1]
    take = lambda j: merged_ref[:, pl.ds(pl.multiple_of((quad ^ j) * lanes, lanes), lanes)]
    own_ref[...] = take(0)
    sent_ref[0] = take(2)
    sent_ref[1] = take(3)
    onward_ref[...] = take(1)


def pack_kernel(
    place_ref, proj_ref, table_ref, message_ref
):
    part = proj_ref.shape[0] // 8
    own_heads = table_ref.shape[1]
    room = message_ref.shape[1] // 2
    eighth = place_ref[2] * 2 + place_ref[1]
    message_ref[:part] = proj_ref[pl.ds(pl.multiple_of(eighth * part, part), part), :]
    offsets = table_ref.shape[0]
    table = jnp.concatenate(
        [table_ref[...], jnp.zeros((offsets, 128 - own_heads), F32)], 1
    )
    table = jnp.concatenate([table, jnp.zeros((room - offsets, 128), F32)], 0)
    table = jnp.transpose(table)[:own_heads]
    high = low(table).astype(F32)
    rows = jnp.concatenate([high, table - high], 1)
    spare = message_ref.shape[0] - part - own_heads
    message_ref[part:] = low(jnp.concatenate([rows, jnp.zeros((spare, 2 * room), F32)], 0))


def pieces_kernel(place_ref, *refs, part):
    del place_ref
    for j, ref in enumerate(refs[:-1]):
        refs[-1][j * part : (j + 1) * part] = ref[:part]


def front_kernel(
    place_ref, flat_ref, mg_ref, ms_ref, n1g_ref, n1s_ref, qb_ref, mw_any, qw_any,
    merged_ref, resid0_ref, normed1_ref, qkv_ref, mw_ref, qw_ref, sems,
):
    copy_m = pltpu.make_async_copy(mw_any, mw_ref, sems.at[0])
    copy_q = pltpu.make_async_copy(qw_any, qw_ref, sems.at[1])
    copy_m.start()
    copy_q.start()
    hat, _ = normalise(flat_ref[...].astype(F32))
    merged = low(hat * mg_ref[...] + ms_ref[...])
    merged_ref[...] = merged
    copy_m.wait()
    resid0 = matmul(merged, mw_ref[...])
    resid0_ref[...] = resid0
    hat1, _ = normalise(resid0)
    normed1 = low(hat1 * n1g_ref[...] + n1s_ref[...])
    normed1_ref[...] = normed1
    copy_q.wait()
    qkv_ref[...] = low(matmul(normed1, qw_ref[...]) + qb_ref[...])


def front_call(place, flat, mg, ms, n1g, n1s, qb, mw, qw):
    rows, deep = flat.shape
    width = mw.shape[1]
    return whole(
        front_kernel,
        place,
        [
            shape_of((rows, deep), BF),
            shape_of((rows, width), F32),
            shape_of((rows, width), BF),
            shape_of((rows, 3 * width), BF),
        ],
        (flat, True), (row(mg), True), (row(ms), True), (row(n1g), True), (row(n1s), True),
        (row(qb), True), (mw, False), (qw, False),
        scratch=[
            pltpu.VMEM(mw.shape, BF), pltpu.VMEM(qw.shape, BF), pltpu.SemaphoreType.DMA((2,)),
        ],
        room=28,
        name="front",
    )


def mine_kernel(place_ref, *refs):
    del place_ref
    rows = refs[0].shape[0]
    for q, ref in enumerate(refs[:-1]):
        refs[-1][q * rows : (q + 1) * rows] = ref[...]


def whole_proj(place_ref, own_ref, mine_ref, theirs_ref, proj_ref, groups):
    rank, core, quad = place_ref[0], place_ref[1], place_ref[2]
    shard = own_ref.shape[0]
    part = shard // 8
    proj_ref[pl.ds(pl.multiple_of(rank * shard, shard), shard), :] = own_ref[...]
    for k in range(4 * (groups - 1)):
        q, j = k // (groups - 1), k % (groups - 1)
        base = lax.rem(rank + groups - 1 - j, groups) * shard + (quad ^ q) * 2 * part
        rows = slice(k * part, (k + 1) * part)
        proj_ref[pl.ds(pl.multiple_of(base + core * part, part), part), :] = mine_ref[rows]
        proj_ref[pl.ds(pl.multiple_of(base + (1 - core) * part, part), part), :] = theirs_ref[rows]


def after_kernel(
    place_ref, heads_ref, resid0_ref, pb_ref, n2g_ref, n2s_ref, own_ref, mine_ref, theirs_ref,
    resid1_ref, normed2_ref, proj_ref, *, groups,
):
    whole_proj(place_ref, own_ref, mine_ref, theirs_ref, proj_ref, groups)
    resid1 = resid0_ref[...] + matmul(heads_ref[...], proj_ref[...]) + pb_ref[...]
    resid1_ref[...] = resid1
    hat2, _ = normalise(resid1)
    normed2_ref[...] = low(hat2 * n2g_ref[...] + n2s_ref[...])


SQRT_HALF = 0.5**0.5
DENSITY = 0.3989422804014327


def gelu_pair(values):
    below = 0.5 * (1.0 + lax.erf(values * SQRT_HALF))
    density = jnp.exp(-0.5 * values * values) * DENSITY
    return values * below, below + values * density


def slope_kernel(
    place_ref, dy_ref, fc2_ref, rows_ref, own_ref, out_ref, wide_ref, *, groups, pad, chunk
):
    tokens, width = own_ref.shape
    wide_ref[...] = dy_ref[...].astype(F32)
    fill = jnp.zeros((pad - tokens, width), F32)
    for j in range(groups):
        at = lax.rem(place_ref[0] + groups - j, groups) * tokens
        block = wide_ref[pl.ds(pl.multiple_of(at, 8), tokens), :]
        rows_ref[j * pad : (j + 1) * pad] = low(jnp.concatenate([block, fill], 0))
        if j == 0:
            own_ref[...] = low(block)

    @pl.loop(0, fc2_ref.shape[0] // chunk)
    def _(step):
        at = pl.ds(pl.multiple_of(step * chunk, chunk), chunk)
        out_ref[:, at] = contract(rows_ref[...], fc2_ref[at, :], 1, 1)


def feed_kernel(
    place_ref, n0_ref, n1_ref, n2_ref, n3_ref, d_act_ref, fc1_ref, fc1b_ref,
    act_ref, dpre_ref, all_ref, db_ref, o0_ref, o1_ref, o2_ref, o3_ref, *, pad, chunk,
):
    del place_ref
    rows, width = n0_ref.shape
    for j, ref in enumerate((n0_ref, n1_ref, n2_ref, n3_ref)):
        all_ref[j * pad : j * pad + rows, :] = ref[...]
        all_ref[j * pad + rows : (j + 1) * pad, :] = jnp.zeros((pad - rows, width), BF)

    @pl.loop(0, fc1_ref.shape[1] // chunk, unroll=True)
    def _(step):
        at = pl.ds(pl.multiple_of(step * chunk, chunk), chunk)
        pre = matmul(all_ref[...], fc1_ref[:, at]) + fc1b_ref[:, at]
        act, slope = gelu_pair(pre)
        act_ref[:, at] = low(act)
        d_low = low(d_act_ref[:, at] * slope)
        dpre_ref[:, at] = d_low
        db_ref[:, at] = jnp.sum(d_low.astype(F32), 0, keepdims=True)

    for j, ref in enumerate((o0_ref, o1_ref, o2_ref, o3_ref)):
        part = contract(dpre_ref[j * pad : (j + 1) * pad, :], fc1_ref[...], 1, 1)
        ref[...] = low(part[:rows])


def second_kernel(place_ref, act_ref, fc2_ref, kept_ref, sent_ref, *, pad, groups):
    rank = place_ref[0]
    rows = kept_ref.shape[1]
    for ref, k, flip in ((sent_ref, 0, 1), (sent_ref, 1, 3), (kept_ref, 0, 0), (kept_ref, 1, 2)):
        block = lax.rem(rank + groups - (rank ^ flip), groups)
        at = pl.ds(pl.multiple_of(block * pad, pad), pad)
        ref[k] = low(matmul(act_ref[at, :], fc2_ref[...])[:rows])


def back2_kernel(
    place_ref, c0_ref, c1_ref, c2_ref, c3_ref, resid1_ref, dy_ref, n2g_ref, own_ref, mine_ref, theirs_ref,
    dresid1_ref, dheads_ref, proj_ref, *, groups,
):
    whole_proj(place_ref, own_ref, mine_ref, theirs_ref, proj_ref, groups)
    rows = dheads_ref.shape[0]
    d_norm2 = (
        c0_ref[...].astype(F32) + c1_ref[...].astype(F32)
        + c2_ref[...].astype(F32) + c3_ref[...].astype(F32)
    )
    hat2, inv2 = normalise(resid1_ref[...])
    dy = dy_ref[...].astype(F32)
    d_resid1 = dy + norm_backward(d_norm2, hat2, inv2, n2g_ref[...])
    dresid1_ref[:rows] = d_resid1
    sums = (d_resid1, d_norm2 * hat2, d_norm2, dy)
    for k, part in enumerate(sums):
        dresid1_ref[rows + k : rows + k + 1] = jnp.sum(part, 0, keepdims=True)
    dheads_ref[...] = low(contract(low(d_resid1), proj_ref[...], 1, 1))


def back1_kernel(
    place_ref, d0_ref, d1_ref, d2_ref, d3_ref, dresid1_ref, resid0_ref, n1g_ref, qw_any,
    dresid0_ref, sums_ref, qw_ref, sems,
):
    rows, width = resid0_ref.shape
    quad = place_ref[2]
    lanes = width // 4
    copies = [
        pltpu.make_async_copy(qw_any.at[:, pl.ds(i * width, width)], qw_ref.at[i], sems.at[i])
        for i in range(3)
    ]
    for copy in copies:
        copy.start()
    hat1, inv1 = normalise(resid0_ref[...])
    d_norm1 = jnp.zeros((rows, width), F32)
    for i in range(3):
        copies[i].wait()
        for j, d_ref in enumerate((d0_ref, d1_ref, d2_ref, d3_ref)):
            part = d_ref[:, i * lanes : (i + 1) * lanes]
            at = pl.ds(pl.multiple_of((quad ^ j) * lanes, lanes), lanes)
            d_norm1 = d_norm1 + contract(part, qw_ref[i, :, at], 1, 1)
            sums_ref[2 + i : 3 + i, at] = jnp.sum(part.astype(F32), 0, keepdims=True)
    dresid0_ref[...] = low(
        dresid1_ref[:rows] + norm_backward(d_norm1, hat1, inv1, n1g_ref[...])
    )
    sums_ref[0:1] = jnp.sum(d_norm1 * hat1, 0, keepdims=True)
    sums_ref[1:2] = jnp.sum(d_norm1, 0, keepdims=True)


def back0_kernel(
    place_ref, dresid0_ref, flat_ref, mg_ref, mw_any, grad_ref, sums_ref, mw_ref, sems
):
    del place_ref
    copy = pltpu.make_async_copy(mw_any, mw_ref, sems.at[0])
    copy.start()
    hat, inv = normalise(flat_ref[...].astype(F32))
    copy.wait()
    d_merged = contract(dresid0_ref[...], mw_ref[...], 1, 1)
    grad_ref[...] = low(norm_backward(d_merged, hat, inv, mg_ref[...]))
    width = dresid0_ref.shape[1]
    gain = jnp.sum(d_merged * hat, 0, keepdims=True)
    shift = jnp.sum(d_merged, 0, keepdims=True)
    for i in range(gain.shape[1] // width):
        sums_ref[i : i + 1] = gain[:, i * width : (i + 1) * width]
        sums_ref[2 + i : 3 + i] = shift[:, i * width : (i + 1) * width]


SPAN = 2 * WIN - 1
OFFSETS = 384
STRIP = 256


def strip_picks(column, offsets_first):
    shape, o_dim = ((OFFSETS, STRIP), 0) if offsets_first else ((STRIP, OFFSETS), 1)
    offset = lax.broadcasted_iota(jnp.int32, shape, o_dim)
    lane = lax.broadcasted_iota(jnp.int32, shape, 1 - o_dim)
    wanted = (SPAN - 1 - lane // WIN) * SPAN + column - lane % WIN + WIN - 1
    hit = (offset == wanted) & (lane < SPAN * WIN)
    return jnp.where(hit, 1.0, 0.0).astype(BF)


def split3(values):
    first = low(values)
    rest = values - first.astype(F32)
    second = low(rest)
    third = low(rest - second.astype(F32))
    return first, second, third


def spread_kernel(place_ref, m0_ref, m1_ref, m2_ref, m3_ref, bias_ref, table_ref, *, part, groups):
    heads = table_ref.shape[0]
    own_heads = heads // groups
    room = m0_ref.shape[1] // 2
    for j, ref in enumerate((m0_ref, m1_ref, m2_ref, m3_ref)):
        both = ref[part : part + 2 * own_heads, :].astype(F32)[:own_heads]
        at = pl.multiple_of(lax.rem(place_ref[0] + groups - j, groups) * own_heads, own_heads)
        table_ref[pl.ds(at, own_heads), :] = both[:, :OFFSETS] + both[:, room : room + OFFSETS]
    table = table_ref[...]
    high = low(table)
    table = jnp.concatenate([high, low(table - high.astype(F32))], 0)
    for column in range(WIN):
        parts = matmul(table, strip_picks(column, True))
        strip = parts[:heads] + parts[heads:]
        for r in range(WIN):
            start = (WIN - 1 - r) * WIN
            at = (r * WIN + column) * heads
            bias_ref[at : at + heads, :] = strip[:, start : start + KEY_ROWS]
    bias_ref[WINDOW_TOKENS * heads :, :] = jnp.zeros(
        ((QUERY_ROWS - WINDOW_TOKENS) * heads, KEY_ROWS), F32
    )


def fold(grad_ref, heads):
    total = jnp.zeros((3 * heads, OFFSETS), F32)
    for column in range(WIN):
        strip = jnp.zeros((heads, STRIP), F32)
        for r in range(WIN):
            start = (WIN - 1 - r) * WIN
            at = (r * WIN + column) * heads
            part = grad_ref[at : at + heads, :]
            wide = jnp.concatenate([part, jnp.zeros((heads, STRIP - KEY_ROWS), F32)], 1)
            strip = strip + (pltpu.roll(wide, start, 1) if start else wide)
        total = total + matmul(jnp.concatenate(split3(strip), 0), strip_picks(column, False))
    return total[:heads] + total[heads : 2 * heads] + total[2 * heads :]


def window_rows(values, window, rows):
    part = values.astype(F32)[window * WINDOW_TOKENS : (window + 1) * WINDOW_TOKENS]
    zeros = jnp.zeros((rows - WINDOW_TOKENS, part.shape[1]), F32)
    return low(jnp.concatenate([part, zeros], 0))


def stack_heads(part, heads, head_dim):
    lane = lax.broadcasted_iota(jnp.int32, part.shape, 1) // head_dim
    zero = jnp.zeros_like(part)
    return jnp.concatenate([jnp.where(lane == h, part, zero) for h in range(heads)], 0)


def attend_kernel(
    place_ref, qkv_ref, bias_ref, mask_ref, out_ref, probs_any, probs_ref, sems, *, windows, head_dim
):
    del place_ref
    width = out_ref.shape[1]
    lanes = width // 4

    def keep(step):
        return pltpu.make_async_copy(probs_ref.at[step], probs_any.at[step], sems.at[step])

    @pl.loop(0, 4, unroll=True)
    def _(step):
        attend_group(
            step, qkv_ref, bias_ref, mask_ref, out_ref, probs_ref, windows, head_dim, width, lanes
        )
        keep(step).start()

    for step in range(4):
        keep(step).wait()


def attend_group(
    step, qkv_ref, bias_ref, mask_ref, out_ref, probs_ref, windows, head_dim, width, lanes
):
    heads, all_heads = lanes // head_dim, width // head_dim
    first = step * heads
    scale = head_dim ** (-0.5)
    at = lambda kind: pl.ds(pl.multiple_of(kind * width + step * lanes, lanes), lanes)
    q_all, k_all, v_all = (qkv_ref[:, at(kind)] for kind in range(3))
    outs = []
    for w in range(windows):
        query = window_rows(q_all, w, QUERY_ROWS)
        keys = stack_heads(window_rows(k_all, w, KEY_ROWS), heads, head_dim)
        values = stack_heads(window_rows(v_all, w, KEY_ROWS), heads, head_dim)
        scores = contract(query, keys, 1, 1) * scale
        mask = mask_ref[w]
        rounded = []
        for h in range(heads):
            bias = bias_ref[pl.ds(first + h, QUERY_ROWS, stride=all_heads), :]
            raw = scores[:, h * KEY_ROWS : (h + 1) * KEY_ROWS] + bias + mask
            expo = jnp.exp(raw - jnp.max(raw, -1, keepdims=True))
            probs = expo / jnp.sum(expo, -1, keepdims=True)
            probs_ref[step, w, h] = probs
            rounded.append(low(probs))
        mixed = matmul(jnp.concatenate(rounded, 1), values)
        outs.append(mixed[:WINDOW_TOKENS])
    out_ref[:, at(0)] = low(jnp.concatenate(outs, 0))


def attend_back_kernel(
    place_ref, qkv_ref, grad_ref, probs_any, d0_ref, d1_ref, d2_ref, d3_ref, table_ref, dbias_ref, probs_ref, sems,
    *, windows, head_dim
):
    width = grad_ref.shape[1]

    def fetch(step):
        return pltpu.make_async_copy(
            probs_any.at[place_ref[2] ^ step], probs_ref.at[step], sems.at[step]
        )

    for step in range(4):
        fetch(step).start()

    @pl.loop(0, 4, unroll=True)
    def _(step):
        fetch(step).wait()
        attend_back_group(
            place_ref[2] ^ step, step, qkv_ref, grad_ref, probs_ref, (d0_ref, d1_ref, d2_ref, d3_ref), dbias_ref,
            windows, head_dim, width, width // 4,
        )

    table_ref[...] = fold(dbias_ref, table_ref.shape[0])


def attend_back_group(
    group, step, qkv_ref, grad_ref, probs_ref, d_refs, dbias_ref,
    windows, head_dim, width, lanes,
):
    heads, all_heads = lanes // head_dim, width // head_dim
    first = group * heads
    scale = head_dim ** (-0.5)
    at = lambda kind: pl.ds(pl.multiple_of(kind * width + group * lanes, lanes), lanes)
    q_all, k_all, v_all = (qkv_ref[:, at(kind)] for kind in range(3))
    g_all = grad_ref[:, at(0)]
    all_q, all_k, all_v = [], [], []
    d_first = []
    for w in range(windows):
        query = stack_heads(window_rows(q_all, w, QUERY_ROWS), heads, head_dim)
        keys = stack_heads(window_rows(k_all, w, KEY_ROWS), heads, head_dim)
        values = stack_heads(window_rows(v_all, w, KEY_ROWS), heads, head_dim)
        plain = window_rows(g_all, w, QUERY_ROWS)
        grad = stack_heads(plain, heads, head_dim)
        d_probs = contract(plain, values, 1, 1)
        d_list, p_list = [], []
        for h in range(heads):
            probs = probs_ref[step, w, h]
            part = d_probs[:, h * KEY_ROWS : (h + 1) * KEY_ROWS]
            total = jnp.sum(part * probs, -1, keepdims=True)
            d_scores = low(probs * (part - total))
            d_list.append(d_scores)
            p_list.append(low(probs))
            if w == 0:
                d_first.append(d_scores.astype(F32))
            else:
                d_first[h] = d_first[h] + d_scores.astype(F32)
            if w == windows - 1:
                dbias_ref[pl.ds(first + h, QUERY_ROWS, stride=all_heads), :] = d_first[h]
        d_query = matmul(jnp.concatenate(d_list, 1), keys) * scale
        d_keys = contract(jnp.concatenate(d_list, 0), query, 0, 0) * scale
        d_values = contract(jnp.concatenate(p_list, 0), grad, 0, 0)
        all_q.append(d_query[:WINDOW_TOKENS])
        all_k.append(d_keys[:WINDOW_TOKENS])
        all_v.append(d_values[:WINDOW_TOKENS])
    result = jnp.concatenate(
        [low(jnp.concatenate(parts, 0)) for parts in (all_q, all_k, all_v)], 1
    )

    for k, d_ref in enumerate(d_refs):

        @pl.when(step == k)
        def _(d_ref=d_ref):
            d_ref[...] = result


def spots(heads, lines, vectors):
    columns = 3
    return [(k // columns, OFFSETS + 128 * (k % columns)) for k in range(vectors * lines)]


def collect_kernel(place_ref, s0_ref, s1_ref, d_ref, rel_ref, b_ref, out_ref):
    heads = rel_ref.shape[0]
    lines = s0_ref.shape[1] // 128
    out_ref[...] = jnp.zeros(out_ref.shape, F32)
    out_ref[:heads, :OFFSETS] = rel_ref[...]
    vectors = [ref[r : r + 1, :] for ref in (s0_ref, s1_ref) for r in range(ref.shape[0])]
    after = d_ref.shape[0] - 8
    vectors += [d_ref[after + r : after + r + 1, :] for r in range(4)]
    for k, (at, lane) in enumerate(spots(heads, lines, len(vectors))):
        piece = vectors[k // lines][:, 128 * (k % lines) : 128 * (k % lines + 1)]
        out_ref[at : at + 1, lane : lane + 128] = piece
    own = b_ref.shape[1] // 128
    first = heads + pl.multiple_of((place_ref[0] // 2) * own, own)
    block = jnp.concatenate([b_ref[:, k * 128 : (k + 1) * 128] for k in range(own)], 0)
    side = place_ref[0] % 2

    @pl.when(side == 0)
    def _():
        out_ref[pl.ds(first, own), 0:128] = block

    @pl.when(side == 1)
    def _():
        out_ref[pl.ds(first, own), 128:256] = block


def deliver_kernel(place_ref, all_ref, *refs, heads):
    *vector_refs, rel_ref, b_ref = refs
    rel_ref[...] = all_ref[:heads, : rel_ref.shape[1]]
    lines = [ref.shape[0] // 128 for ref in vector_refs]
    places = iter(spots(heads, 1, sum(lines)))
    for ref, count in zip(vector_refs, lines):
        for k in range(count):
            at, lane = next(places)
            ref[128 * k : 128 * (k + 1)] = all_ref[at, lane : lane + 128]
    own = b_ref.shape[0]
    first = heads + pl.multiple_of((place_ref[0] // 2) * own, own)
    side = place_ref[0] % 2

    @pl.when(side == 0)
    def _():
        b_ref[...] = all_ref[pl.ds(first, own), 0:128]

    @pl.when(side == 1)
    def _():
        b_ref[...] = all_ref[pl.ds(first, own), 128:256]


def columns_kernel(place_ref, b0_ref, b1_ref, b2_ref, b3_ref, own_ref, out_ref, sums_ref):
    rows = out_ref.shape[0]
    lanes = b0_ref.shape[2] // 3
    total = own_ref[...]
    for j, ref in enumerate((b0_ref, b1_ref, b2_ref, b3_ref)):
        for part in range(3):
            at = pl.multiple_of((part * 4 + (place_ref[2] ^ j)) * lanes, lanes)
            out_ref[:, pl.ds(at, lanes)] = ref[0, :rows, part * lanes : (part + 1) * lanes].astype(F32)
        if j:
            total = total + take_sums(ref, 1, own_ref.shape[0])
    sums_ref[...] = total


def on_device(
    patches,
    window_extent,
    merge_gain,
    merge_shift,
    merge_weight,
    norm1_gain,
    norm1_shift,
    qkv_weight,
    qkv_bias,
    rel_table,
    proj_weight,
    proj_bias,
    norm2_gain,
    norm2_shift,
    fc1_weight,
    fc1_bias,
    fc2_weight,
    fc2_bias,
    out_grad,
):
    groups, wide = lax.axis_size("narrow"), lax.axis_size("wide")
    devices = wide * groups
    highs = wide // 8
    wide_at, rank = lax.axis_index("wide"), lax.axis_index("narrow")
    core, quad, high = wide_at % 2, (wide_at // 2) % 4, wide_at // 8
    place = jnp.stack([rank, core, quad]).astype(jnp.int32)
    tokens = patches.shape[0]
    width = qkv_weight.shape[0]
    own_heads = rel_table.shape[1]
    heads = own_heads * groups
    head_dim = width // heads
    windows = tokens // WINDOW_TOKENS
    pad = tokens + (-tokens) % 16

    def arrange(array, order):
        if highs == 1:
            return array
        sizes = {"h": highs, "q": 4, "c": 2, "n": groups}
        cut = [sizes[k] for k in order]
        rest = array.shape[1]
        for size in cut:
            rest //= size
        at = order.index("h") + 1
        moved = [i + 1 for i in range(len(order)) if i + 1 != at] + [at, len(order) + 1]
        return jnp.transpose(array.reshape(-1, *cut, rest), [0] + moved).reshape(array.shape)

    def settle(array):
        if highs == 1:
            return array[0]
        return sum_high(array[0].reshape(highs, -1, array.shape[2]), high)

    part = proj_weight.shape[0] // 8
    message = whole(
        pack_kernel,
        place,
        [shape_of((part + own_heads + (-(part + own_heads)) % 16, width), BF)],
        (proj_weight, True),
        (rel_table, True),
        name="pack",
    )[0]
    messages = [turn(message, "narrow", step) for step in range(1, groups)]

    flat = patches.reshape(tokens, -1)
    merged, resid0, normed1, qkv = front_call(
        place, flat, merge_gain, merge_shift, norm1_gain, norm1_shift, qkv_bias,
        merge_weight, qkv_weight,
    )
    mine = whole(
        functools.partial(pieces_kernel, part=part),
        place,
        [shape_of(((groups - 1) * part, width), BF)],
        *((m, True) for m in messages),
        name="pieces",
    )
    mine = list(mine) + [swap(mine[0], "wide", 2 * j) for j in (1, 2, 3)]

    merged_own, merged_sent, merged_onward = whole(
        cut_kernel,
        place,
        [
            shape_of((tokens, merged.shape[1] // 4), BF),
            shape_of((2, tokens, merged.shape[1] // 4), BF),
            shape_of((tokens, merged.shape[1] // 4), BF),
        ],
        (arrange(merged, "hqcn"), True),
        name="cut",
    )
    normed1_cut = arrange(normed1, "hqcn")

    positions = jnp.arange(KEY_ROWS)
    extent = lax.dynamic_slice_in_dim(window_extent, rank * windows, windows, 0)
    valid = (
        (positions[None, :] // WIN < extent[:, 0:1])
        & (positions[None, :] % WIN < extent[:, 1:2])
        & (positions[None, :] < WINDOW_TOKENS)
    )
    mask = jnp.where(valid, 0.0, -1e30).astype(F32)[:, None, :]
    bias = whole(
        functools.partial(spread_kernel, part=part, groups=groups),
        place,
        [shape_of((QUERY_ROWS * heads, KEY_ROWS), F32)],
        (message, True),
        *((m, True) for m in messages),
        scratch=[pltpu.VMEM((heads, OFFSETS), F32)],
        name="spread",
    )[0]
    heads_out, probs = whole(
        functools.partial(attend_kernel, windows=windows, head_dim=head_dim),
        place,
        [
            shape_of((tokens, width), BF),
            shape_of((PROBS_ROOM, windows, heads // 4, QUERY_ROWS, KEY_ROWS), F32),
        ],
        (qkv, True), (bias, True), (mask, True),
        leave=(1,),
        scratch=[
            pltpu.VMEM((4, windows, heads // 4, QUERY_ROWS, KEY_ROWS), F32),
            pltpu.SemaphoreType.DMA((4,)),
        ],
        name="attend",
    )

    mine = whole(
        mine_kernel,
        place,
        [shape_of((4 * mine[0].shape[0], width), BF)],
        *((m, True) for m in mine),
        after=(heads_out,),
        name="mine",
    )[0]
    theirs = swap(mine, "wide", 1)
    resid1, normed2, merged_sent, normed1_cut, merged_onward = whole(
        functools.partial(after_kernel, groups=groups),
        place,
        [shape_of((tokens, width), F32), shape_of((tokens, width), BF)],
        (heads_out, True), (resid0, True),
        (row(proj_bias), True), (row(norm2_gain), True), (row(norm2_shift), True),
        (proj_weight, True), (mine, True), (theirs, True),
        scratch=[pltpu.VMEM((width, width), BF)],
        through=(merged_sent, normed1_cut, merged_onward),
        name="after",
    )
    merged_near = swap(merged_sent, "wide", 4)
    normed1_near = swap(normed1_cut, "wide", 2)
    blocks = [normed2] + [turn(normed2, "narrow", step) for step in range(1, groups)]

    merged_onward = jnp.stack([merged_onward, merged_near[1]])
    merged_far = swap(merged_onward, "wide", 2)
    normed1_both = jnp.stack([normed1_cut, normed1_near])
    normed1_far = swap(normed1_both, "wide", 4)

    total, units = groups * pad, fc1_weight.shape[1]
    dy_rows, dy_own, d_act = whole(
        functools.partial(slope_kernel, groups=groups, pad=pad, chunk=256),
        place,
        [
            shape_of((total, width), BF),
            shape_of((tokens, width), BF),
            shape_of((total, units), F32),
        ],
        (out_grad, True), (fc2_weight, True),
        scratch=[pltpu.VMEM(out_grad.shape, F32)],
        after=(normed2,),
        name="slope",
    )
    act, d_pre, rows_all, fc1_b_grad, *chunks = whole(
        functools.partial(feed_kernel, pad=pad, chunk=256),
        place,
        [
            shape_of((total, units), BF),
            shape_of((total, units), BF),
            shape_of((total, width), BF),
            shape_of((1, units), F32),
        ]
        + [shape_of((tokens, width), BF)] * 4,
        *((b, True) for b in blocks), (d_act, True), (fc1_weight, True), (row(fc1_bias), True),
        after=(normed1_far, merged_far),
        name="feed",
    )
    arrived = [chunks[0]] + [turn(chunks[j], "narrow", -j) for j in range(1, groups)]

    fc1_kept, fc1_sent = grad_call(place, [arrange(rows_all, "hqc")], [d_pre], 256, 128, "fc1_grad")
    fc2_kept, fc2_sent = grad_call(place, [arrange(act, "hqc")], [dy_rows], 256, 128, "fc2_grad")
    fc1_come, fc2_come = swap(fc1_sent, "wide", 1), swap(fc2_sent, "wide", 1)
    fc1_kept, fc1_sent = join_call(
        place, [(fc1_kept, fc1_come)],
        [
            (F32, [lambda p, y=y: (0, 2 * y + p[2] % 2, 0, 128) for y in range(2)]),
            (BF, [lambda p, y=y: (0, 2 * y + 1 - p[2] % 2, 0, 128) for y in range(2)]),
        ],
        "fc1_join",
    )
    fc2_kept, fc2_sent = join_call(
        place, [(fc2_kept, fc2_come)],
        [
            (F32, [lambda p, x=x: (0, 2 * (p[2] // 2) + x, 0, 128) for x in range(2)]),
            (BF, [lambda p, x=x: (0, 2 * (1 - p[2] // 2) + x, 0, 128) for x in range(2)]),
        ],
        "fc2_join",
    )
    fc1_come, fc2_come = swap(fc1_sent, "wide", 2), swap(fc2_sent, "wide", 4)
    fc1_kept, fc1_sent = join_call(
        place, [(fc1_kept, fc1_come)],
        [
            (F32, [lambda p: (0, p[2] // 2, 0, 128)]),
            (BF, [lambda p: (0, 1 - p[2] // 2, 0, 128)]),
        ],
        "fc1_join2",
    )
    fc2_kept, fc2_sent = join_call(
        place, [(fc2_kept, fc2_come)],
        [
            (F32, [lambda p: (0, p[2] % 2, 0, 128)]),
            (BF, [lambda p: (0, 1 - p[2] % 2, 0, 128)]),
        ],
        "fc2_join2",
    )
    fc1_come, fc2_come = swap(fc1_sent, "wide", 4), swap(fc2_sent, "wide", 2)
    second_kept, second_sent = whole(
        functools.partial(second_kernel, pad=pad, groups=groups),
        place,
        [shape_of((2, tokens, width), BF)] * 2,
        (act, True),
        (fc2_weight, True),
        name="second",
    )
    d_resid1, d_heads, second_sent = whole(
        functools.partial(back2_kernel, groups=groups),
        place,
        [shape_of((tokens + 8, width), F32), shape_of((tokens, width), BF)],
        *((a, True) for a in arrived),
        (resid1, True), (dy_own, True), (row(norm2_gain), True),
        (proj_weight, True), (mine, True), (theirs, True),
        scratch=[pltpu.VMEM((width, width), BF)],
        after=(fc1_sent, fc2_sent),
        through=(second_sent,),
        name="back2",
    )
    second_come = swap(second_sent, "narrow", 1)
    *d_parts, rel_part = whole(
        functools.partial(attend_back_kernel, windows=windows, head_dim=head_dim),
        place,
        [shape_of((tokens, 3 * width // 4), BF)] * 4 + [shape_of((heads, OFFSETS), F32)],
        (qkv, True), (d_heads, True), (probs, False),
        scratch=[
            pltpu.VMEM((QUERY_ROWS * heads, KEY_ROWS), F32),
            pltpu.VMEM((4, *probs.shape[1:]), F32),
            pltpu.SemaphoreType.DMA((4,)),
        ],
        after=(fc1_come, fc2_come),
        name="attend_back",
    )
    d_come = [swap(d_parts[j], "wide", 2 * j) for j in (1, 2, 3)]

    d_resid0, sums1 = whole(
        back1_kernel,
        place,
        [shape_of((tokens, width), BF), shape_of((5, width), F32)],
        *((d, True) for d in d_parts), (d_resid1, True), (resid0, True),
        (row(norm1_gain), True), (qkv_weight, False),
        scratch=[
            pltpu.VMEM((3, width, width), BF),
            pltpu.SemaphoreType.DMA((3,)),
        ],
        name="back1",
    )
    d_flat, sums0 = whole(
        back0_kernel,
        place,
        [shape_of(flat.shape, BF), shape_of((2 * flat.shape[1] // width, width), F32)],
        (d_resid0, True), (flat, True), (row(merge_gain), True), (merge_weight, False),
        scratch=[pltpu.VMEM(merge_weight.shape, BF), pltpu.SemaphoreType.DMA((1,))],
        name="back0",
    )

    second_own, second_sent = join_call(
        place, [(second_kept, second_come)],
        [(F32, [lambda p: (0, 0, 0, tokens)]), (BF, [lambda p: (0, 1, 0, tokens)])],
        "second_join",
    )
    second_come = swap(second_sent, "narrow", 2)

    proj_kept, proj_sent = grad_call(
        place, [arrange(heads_out, "nhqc")], [d_resid1], 256, 32, "proj_grad", after=(d_resid0,)
    )
    proj_come = swap(proj_sent, "wide", 1)

    side = lambda pick_x: [
        lambda p, n=n, y=y: (0, n, (2 * y + pick_x(p[2] % 2)) * 32, 32)
        for n in range(groups) for y in range(2)
    ]
    proj_kept, proj_sent = join_call(
        place, [(proj_kept, proj_come)],
        [(F32, side(lambda x: x)), (BF, side(lambda x: 1 - x))],
        "proj_join",
    )
    proj_come = swap(proj_sent, "wide", 2)

    own_sums, d_resid0 = whole(
        collect_kernel,
        place,
        [shape_of((48, 3 * width // 4), F32)],
        (sums0, True), (sums1, True), (d_resid1, True), (rel_part, True), (fc1_b_grad, True),
        after=(*d_come, second_sent, proj_sent),
        through=(d_resid0,),
        name="collect",
    )
    r_come = [swap(d_resid0, "wide", 2 * j) for j in (1, 2, 3)]
    qkv_kept, qkv_sent = grad_call(
        place,
        [normed1_cut, (normed1_both, 1), (normed1_far, 0), (normed1_far, 1)],
        [d_parts[0], *d_come],
        256, 128, "qkv_grad", sums=own_sums, after=(second_sent,),
    )
    qkv_come = swap(qkv_sent, "wide", 1)
    rows = 128 // groups
    qkv_pieces = lambda flip: [
        lambda p, g=g, k=k: (0, g, (2 * k + (p[0] + flip) % 2) * rows, rows)
        for k in range(2) for g in range(4)
    ]
    own_sums, qkv_kept, qkv_sent = join_call(
        place, [(qkv_kept, qkv_come)], [(F32, qkv_pieces(0)), (BF, qkv_pieces(1))], "qkv_join",
        sums=(own_sums, 4),
    )
    qkv_come = swap(qkv_sent, "narrow", 1)

    merge_kept, merge_sent = grad_call(
        place,
        [merged_own, (merged_far, 0), (merged_near, 0), (merged_far, 1)],
        [d_resid0, *r_come],
        merged_own.shape[1], merged_own.shape[1] // 2, "merge_grad", after=(qkv_sent,),
    )
    merge_come = swap(merge_sent, "wide", 1)

    second_pieces = lambda flip: [
        lambda p, g=g: (0, ((p[0] // 2 + flip) % 2) * 4 + g, 0, rows) for g in range(4)
    ]
    own_sums, qkv_kept, qkv_sent = join_call(
        place, [(qkv_kept, qkv_come)],
        [(F32, second_pieces(0)), (BF, second_pieces(1))],
        "qkv_join2",
        sums=(own_sums, 8),
        after=(merge_sent,),
    )
    qkv_come = swap(qkv_sent, "narrow", 2)
    merge_rows = merged_own.shape[1] // 2 // groups
    merge_pieces = lambda flip: [
        lambda p, k=k: (0, 0, (2 * k + (p[0] + flip) % 2) * merge_rows, merge_rows)
        for k in range(2)
    ]
    merge_kept, merge_sent, fc1_come, fc2_come, d_flat = join_call(
        place, [(merge_kept, merge_come)],
        [(F32, merge_pieces(0)), (BF, merge_pieces(1))],
        "merge_join",
        after=(qkv_sent,),
        through=(fc1_come, fc2_come, d_flat),
    )
    merge_first = merge_sent
    merge_come = swap(merge_sent, "narrow", 1)

    last_pieces = lambda flip, size: [lambda p: (0, (p[0] // 2 + flip) % 2, 0, size)]
    merge_kept, merge_sent = join_call(
        place, [(merge_kept, merge_come)],
        [(F32, last_pieces(0, merge_rows)), (BF, last_pieces(1, merge_rows))],
        "merge_join2",
        after=(qkv_sent,),
    )
    merge_last = merge_sent
    merge_come = swap(merge_sent, "narrow", 2)

    proj_kept, proj_sent = join_call(
        place, [(proj_kept, proj_come)],
        [
            (F32, [lambda p, n=n: (0, 2 * n + p[2] // 2, 0, 32) for n in range(groups)]),
            (BF, [lambda p, n=n: (0, 2 * n + 1 - p[2] // 2, 0, 32) for n in range(groups)]),
        ],
        "proj_join2",
        after=(merge_first,),
    )
    proj_come = swap(proj_sent, "wide", 4)
    proj_pieces = lambda flip: [
        lambda p, k=k: (0, 2 * k + (p[0] + flip) % 2, 0, 32) for k in range(2)
    ]
    proj_kept, proj_sent = join_call(
        place, [(proj_kept, proj_come)], [(F32, proj_pieces(0)), (BF, proj_pieces(1))],
        "proj_join3",
        after=(merge_sent,),
    )
    proj_come = swap(proj_sent, "narrow", 1)
    proj_kept, proj_sent = join_call(
        place, [(proj_kept, proj_come)],
        [(F32, last_pieces(0, 32)), (BF, last_pieces(1, 32))],
        "proj_join4",
    )
    proj_come = swap(proj_sent, "narrow", 2)

    own_sums, *cuts = join_call(
        place, [(qkv_kept, qkv_come)],
        [(BF, [lambda p, j=j: (0, p[2] ^ j, 0, rows)]) for j in range(4)],
        "qkv_join3",
        sums=(own_sums, 4),
        after=(merge_last,),
    )
    cuts = [cuts[0]] + [swap(cuts[j], "wide", 2 * j) for j in (1, 2, 3)]
    qkv_out, all_sums = whole(
        columns_kernel,
        place,
        [shape_of((rows, 3 * width), F32), shape_of(own_sums.shape, F32)],
        *((c, True) for c in cuts), (own_sums, True),
        name="columns",
    )
    qkv_out = settle(qkv_out[None])
    mask = 8
    while mask < wide:
        all_sums = all_sums + swap(all_sums, "wide", mask)
        mask *= 2
    merge_out = settle(merge_kept + merge_come.astype(F32))
    proj_out = settle(proj_kept + proj_come.astype(F32))

    fc1_out = settle(fc1_kept + fc1_come.astype(F32))
    fc2_out = settle(fc2_kept + fc2_come.astype(F32))
    patches_grad = d_flat.reshape(patches.shape)
    output = low(resid1 + row(fc2_bias) + second_own[0] + second_come[0].astype(F32))

    deep = merged.shape[1]
    *vectors, rel_grad, fc1_b_mine = whole(
        functools.partial(deliver_kernel, heads=heads),
        place,
        [
            shape_of((size,), F32)
            for size in (deep, deep, width, width, 3 * width, width, width, width, width)
        ]
        + [shape_of((heads, rel_table.shape[0]), F32), shape_of((units // 128, 128), F32)],
        (all_sums, True),
        name="deliver",
    )
    fc1_b_out = lax.dynamic_index_in_dim(
        fc1_b_mine.reshape(wide, -1), wide_at, 0, keepdims=False
    )

    return (
        output,
        patches_grad,
        vectors[0],
        vectors[1],
        merge_out,
        vectors[2],
        vectors[3],
        qkv_out,
        vectors[4],
        jnp.transpose(rel_grad),
        proj_out,
        vectors[5],
        vectors[6],
        vectors[7],
        fc1_out,
        fc1_b_out,
        fc2_out,
        vectors[8],
    )


def solution(mesh):
    in_specs = (
        P(("wide", "narrow"), None, None),
        P("wide", None),
        P(),
        P(),
        P(),
        P(),
        P(),
        P(),
        P(),
        P(None, "narrow"),
        P("narrow", None),
        P(),
        P(),
        P(),
        P(None, "narrow"),
        P("narrow"),
        P("narrow", None),
        P(),
        P("wide", None),
    )
    out_specs = (
        P(("wide", "narrow"), None),
        P(("wide", "narrow"), None, None),
        P(),
        P(),
        P(("wide", "narrow"), None),
        P(),
        P(),
        P(("wide", "narrow"), None),
        P(),
        P(),
        P(("narrow", "wide"), None),
        P(),
        P(),
        P(),
        P("wide", "narrow"),
        P(("narrow", "wide")),
        P(("narrow", "wide"), None),
        P(),
    )
    return jax.shard_map(
        on_device, mesh=mesh, in_specs=in_specs, out_specs=out_specs, check_vma=False
    )
```

```python
import functools

import jax
import jax.numpy as jnp
from jax import lax
from jax.experimental import pallas as pl
from jax.experimental.pallas import tpu as pltpu
from jax.sharding import PartitionSpec as P

WIN = 10
WINDOW_TOKENS = WIN * WIN
QUERY_ROWS = 112
KEY_ROWS = 128
EPS = 1e-05
MEBI = 1024 * 1024
PROBS_ROOM = 52
WAIT_US = 100.0
WEIGHT_US = {"back1": 20, "proj_grad": 20, "back0": 20, "second_join": 20, "proj_join": 20}
WEIGHT_US |= dict.fromkeys(
    ("pack", "front", "cut", "pieces", "spread", "attend", "mine", "after", "slope", "feed", "second", "fc1_grad",
     "fc2_grad", "fc1_join", "fc2_join", "fc1_join2", "fc2_join2"), WAIT_US
)
FLOPS_PER_US = 10**9
BF = jnp.bfloat16
F32 = jnp.float32


def normalise(values):
    average = jnp.mean(values, -1, keepdims=True)
    centred = values - average
    inverse = lax.rsqrt(jnp.mean(centred * centred, -1, keepdims=True) + EPS)
    return centred * inverse, inverse


def norm_backward(grad_out, normal, inverse, gain):
    scaled = grad_out * gain
    return inverse * (
        scaled
        - jnp.mean(scaled, -1, keepdims=True)
        - normal * jnp.mean(scaled * normal, -1, keepdims=True)
    )


def matmul(left, right):
    return jnp.dot(left, right, preferred_element_type=jnp.float32)


def contract(left, right, left_dim, right_dim):
    return lax.dot_general(
        left, right, (((left_dim,), (right_dim,)), ((), ())), preferred_element_type=jnp.float32
    )


def low(array):
    return array.astype(BF)


def row(vector):
    return vector.reshape(1, -1)


def stays():
    return pl.BlockSpec(memory_space=pl.ANY)


def outside():
    return pl.BlockSpec(memory_space=pltpu.HBM)


def held():
    return pl.BlockSpec(memory_space=pltpu.VMEM)


def shape_of(shape, dtype):
    return jax.ShapeDtypeStruct(shape, dtype)


def whole(
    kernel, place, outs, *operands, leave=(), scratch=(), after=(), through=(), room=20, name=None
):
    arrays = [a for a, _ in operands]
    count, skip, given = len(arrays), len(after) + len(through), len(outs)

    def body(place_ref, *refs):
        own_outs = refs[count + skip : count + skip + given]
        kernel(place_ref, *refs[:count], *own_outs, *refs[count + skip + given + len(through) :])

    return pl.pallas_call(
        body,
        in_specs=[pl.BlockSpec(memory_space=pltpu.SMEM)]
        + [{True: held, False: outside, None: stays}[inside]() for _, inside in operands]
        + [stays()] * skip,
        out_specs=[outside() if k in leave else held() for k in range(given)]
        + [stays()] * len(through),
        out_shape=list(outs) + [shape_of(a.shape, a.dtype) for a in through],
        input_output_aliases={1 + count + len(after) + k: given + k for k in range(len(through))},
        scratch_shapes=list(scratch),
        compiler_params=pltpu.CompilerParams(vmem_limit_bytes=room * MEBI),
        cost_estimate=pl.CostEstimate(
            flops=int(WEIGHT_US.get(name, 5) * FLOPS_PER_US), bytes_accessed=0, transcendentals=0
        ),
        name=name,
    )(place, *arrays, *after, *through)


def tie(array, *after):
    def body(*refs):
        del refs

    return pl.pallas_call(
        body,
        in_specs=[stays()] * (1 + len(after)),
        out_specs=stays(),
        out_shape=shape_of(array.shape, array.dtype),
        input_output_aliases={0: 0},
        name="tie",
    )(array, *after)


def swap(array, axis, mask):
    size = lax.axis_size(axis)
    return lax.ppermute(array, axis, [(i, i ^ mask) for i in range(size)])


def turn(array, axis, step):
    size = lax.axis_size(axis)
    return lax.ppermute(array, axis, [(i, (i + step) % size) for i in range(size)])


def sum_all(vector):
    mask = 1
    while mask < lax.axis_size("wide"):
        vector = vector + swap(vector, "wide", mask)
        mask *= 2
    mask = 1
    while mask < lax.axis_size("narrow"):
        vector = vector + swap(vector, "narrow", mask)
        mask *= 2
    return vector


def sum_high(parts, high):
    take = lambda index: lax.dynamic_index_in_dim(parts, index, 0, keepdims=False)
    total = take(high).astype(F32)
    for j in range(1, parts.shape[0]):
        total = total + swap(low(take(high ^ j)), "wide", 8 * j).astype(F32)
    return total


def grad_kernel(place_ref, *refs, lefts, rights, block, rows, riding):
    left_refs, right_refs = refs[: len(lefts)], refs[len(lefts) : len(lefts) + len(rights)]
    kept_ref, sent_ref, total_ref = refs[-3:]
    core = place_ref[1]
    if riding:
        give_sums(sent_ref, kept_ref.shape[0], refs[-4][...])

    @pl.loop(0, kept_ref.shape[0])
    def _(step):
        at = pl.ds(pl.multiple_of(step * block, block), block)
        total = None
        for l_ref, l_at, r_ref, r_at in zip(left_refs, lefts, right_refs, rights):
            left = l_ref[:, at] if l_at is None else l_ref[l_at, :, at]
            right = r_ref[: left.shape[0]] if r_at is None else r_ref[r_at]
            right = low(right)
            part = contract(left, right, 0, 0)
            total = part if total is None else total + part
        total_ref[...] = total
        for s in range(block // (2 * rows)):
            mine = pl.multiple_of((2 * s + core) * rows, rows)
            theirs = pl.multiple_of((2 * s + 1 - core) * rows, rows)
            kept_ref[step, s * rows : (s + 1) * rows] = total_ref[pl.ds(mine, rows)]
            sent_ref[step, s * rows : (s + 1) * rows] = low(total_ref[pl.ds(theirs, rows)])


def grad_call(place, lefts, rights, block, rows, name, after=(), sums=None):
    split = lambda item: item if isinstance(item, tuple) else (item, None)
    left_arrays, left_at = zip(*map(split, lefts))
    right_arrays, right_at = zip(*map(split, rights))
    deep, width = left_arrays[0].shape[-1], right_arrays[0].shape[-1]
    shape = (deep // block, block // 2, width)
    return whole(
        functools.partial(
            grad_kernel, lefts=left_at, rights=right_at, block=block, rows=rows,
            riding=sums is not None,
        ),
        place,
        [shape_of(shape, F32), shape_of((shape[0] + (sums is not None), *shape[1:]), BF)],
        *((a, True) for a in left_arrays + right_arrays + (() if sums is None else (sums,))),
        scratch=[pltpu.VMEM((block, width), F32)],
        after=after,
        name=name,
    )


def add_up(refs, lead, rows):
    total = None
    for ref in refs:
        part = ref[lead, rows, :].astype(F32)
        total = part if total is None else total + part
    return total


def join_call(place, groups, outs, name, after=(), through=(), sums=None):
    width = groups[0][0].shape[2]
    counts = [len(sources) for sources in groups]
    count = sum(counts)
    rows_of = [pieces[0]((0, 0, 0))[3] for _, pieces in outs]
    more = -(-sums[0].shape[0] // rows_of[1]) if sums else 0
    shapes = [
        shape_of((len(pieces) + (more if k else 0), rows, width), dtype)
        for k, ((dtype, pieces), rows) in enumerate(zip(outs, rows_of))
    ]
    if sums:
        shapes = [shape_of(sums[0].shape, F32)] + shapes

    def kernel(place_ref, *refs):
        place_now = (place_ref[0], place_ref[1], place_ref[2])
        ins, out_refs = refs[:count], refs[count:]
        if sums:
            own_ref, total_ref, out_refs = refs[count], refs[count + 1], refs[count + 2 :]
            total = own_ref[...] + take_sums(ins[counts[0] - 1], sums[1], own_ref.shape[0])
            total_ref[...] = total
        at = [sum(counts[:g]) for g in range(len(counts))]
        for k, (out_ref, (dtype, pieces)) in enumerate(zip(out_refs, outs)):
            for n, piece in enumerate(pieces):
                group, lead, start, rows = piece(place_now)
                if not isinstance(start, int):
                    start = pl.multiple_of(start, rows)
                part = add_up(ins[at[group] : at[group] + counts[group]], lead, pl.ds(start, rows))
                out_ref[n] = part.astype(dtype)
            if sums and k:
                give_sums(out_ref, len(pieces), total)

    arrays = [s for sources in groups for s in sources] + ([sums[0]] if sums else [])
    return whole(
        kernel, place, shapes, *((s, True) for s in arrays), after=after, through=through, name=name
    )


def give_sums(ref, first, values):
    parts = low(values)
    size = ref.shape[1]
    for k in range(parts.shape[0] // size):
        ref[first + k] = parts[k * size : (k + 1) * size]
    rest = parts.shape[0] % size
    if rest:
        ref[first + parts.shape[0] // size, :rest] = parts[parts.shape[0] - rest :]


def take_sums(ref, first, rows):
    size = ref.shape[1]
    blocks = [ref[first + k].astype(F32) for k in range(-(-rows // size))]
    return (jnp.concatenate(blocks, 0) if len(blocks) > 1 else blocks[0])[:rows]


def cut_kernel(place_ref, merged_ref, own_ref, sent_ref, onward_ref):
    quad = place_ref[2]
    lanes = own_ref.shape[1]
    take = lambda j: merged_ref[:, pl.ds(pl.multiple_of((quad ^ j) * lanes, lanes), lanes)]
    own_ref[...] = take(0)
    sent_ref[0] = take(2)
    sent_ref[1] = take(3)
    onward_ref[...] = take(1)


def pack_kernel(
    place_ref, proj_ref, table_ref, message_ref
):
    part = proj_ref.shape[0] // 8
    own_heads = table_ref.shape[1]
    room = message_ref.shape[1] // 2
    eighth = place_ref[2] * 2 + place_ref[1]
    message_ref[:part] = proj_ref[pl.ds(pl.multiple_of(eighth * part, part), part), :]
    offsets = table_ref.shape[0]
    table = jnp.concatenate(
        [table_ref[...], jnp.zeros((offsets, 128 - own_heads), F32)], 1
    )
    table = jnp.concatenate([table, jnp.zeros((room - offsets, 128), F32)], 0)
    table = jnp.transpose(table)[:own_heads]
    high = low(table).astype(F32)
    rows = jnp.concatenate([high, table - high], 1)
    spare = message_ref.shape[0] - part - own_heads
    message_ref[part:] = low(jnp.concatenate([rows, jnp.zeros((spare, 2 * room), F32)], 0))


def pieces_kernel(place_ref, *refs, part):
    del place_ref
    for j, ref in enumerate(refs[:-1]):
        refs[-1][j * part : (j + 1) * part] = ref[:part]


def front_kernel(
    place_ref, flat_ref, mg_ref, ms_ref, n1g_ref, n1s_ref, qb_ref, mw_any, qw_any,
    merged_ref, resid0_ref, normed1_ref, qkv_ref, mw_ref, qw_ref, sems,
):
    copy_m = pltpu.make_async_copy(mw_any, mw_ref, sems.at[0])
    copy_q = pltpu.make_async_copy(qw_any, qw_ref, sems.at[1])
    copy_m.start()
    copy_q.start()
    hat, _ = normalise(flat_ref[...].astype(F32))
    merged = low(hat * mg_ref[...] + ms_ref[...])
    merged_ref[...] = merged
    copy_m.wait()
    resid0 = matmul(merged, mw_ref[...])
    resid0_ref[...] = resid0
    hat1, _ = normalise(resid0)
    normed1 = low(hat1 * n1g_ref[...] + n1s_ref[...])
    normed1_ref[...] = normed1
    copy_q.wait()
    qkv_ref[...] = low(matmul(normed1, qw_ref[...]) + qb_ref[...])


def front_call(place, flat, mg, ms, n1g, n1s, qb, mw, qw):
    rows, deep = flat.shape
    width = mw.shape[1]
    return whole(
        front_kernel,
        place,
        [
            shape_of((rows, deep), BF),
            shape_of((rows, width), F32),
            shape_of((rows, width), BF),
            shape_of((rows, 3 * width), BF),
        ],
        (flat, True), (row(mg), True), (row(ms), True), (row(n1g), True), (row(n1s), True),
        (row(qb), True), (mw, False), (qw, False),
        scratch=[
            pltpu.VMEM(mw.shape, BF), pltpu.VMEM(qw.shape, BF), pltpu.SemaphoreType.DMA((2,)),
        ],
        room=28,
        name="front",
    )


def mine_kernel(place_ref, *refs):
    del place_ref
    rows = refs[0].shape[0]
    for q, ref in enumerate(refs[:-1]):
        refs[-1][q * rows : (q + 1) * rows] = ref[...]


def whole_proj(place_ref, own_ref, mine_ref, theirs_ref, proj_ref, groups):
    rank, core, quad = place_ref[0], place_ref[1], place_ref[2]
    shard = own_ref.shape[0]
    part = shard // 8
    proj_ref[pl.ds(pl.multiple_of(rank * shard, shard), shard), :] = own_ref[...]
    for k in range(4 * (groups - 1)):
        q, j = k // (groups - 1), k % (groups - 1)
        base = lax.rem(rank + groups - 1 - j, groups) * shard + (quad ^ q) * 2 * part
        rows = slice(k * part, (k + 1) * part)
        proj_ref[pl.ds(pl.multiple_of(base + core * part, part), part), :] = mine_ref[rows]
        proj_ref[pl.ds(pl.multiple_of(base + (1 - core) * part, part), part), :] = theirs_ref[rows]


def after_kernel(
    place_ref, heads_ref, resid0_ref, pb_ref, n2g_ref, n2s_ref, own_ref, mine_ref, theirs_ref,
    resid1_ref, normed2_ref, proj_ref, *, groups,
):
    whole_proj(place_ref, own_ref, mine_ref, theirs_ref, proj_ref, groups)
    resid1 = resid0_ref[...] + matmul(heads_ref[...], proj_ref[...]) + pb_ref[...]
    resid1_ref[...] = resid1
    hat2, _ = normalise(resid1)
    normed2_ref[...] = low(hat2 * n2g_ref[...] + n2s_ref[...])


SQRT_HALF = 0.5**0.5
DENSITY = 0.3989422804014327


def gelu_pair(values):
    below = 0.5 * (1.0 + lax.erf(values * SQRT_HALF))
    density = jnp.exp(-0.5 * values * values) * DENSITY
    return values * below, below + values * density


def slope_kernel(
    place_ref, dy_ref, fc2_ref, rows_ref, own_ref, out_ref, wide_ref, *, groups, pad, chunk
):
    tokens, width = own_ref.shape
    wide_ref[...] = dy_ref[...].astype(F32)
    fill = jnp.zeros((pad - tokens, width), F32)
    for j in range(groups):
        at = lax.rem(place_ref[0] + groups - j, groups) * tokens
        block = wide_ref[pl.ds(pl.multiple_of(at, 8), tokens), :]
        rows_ref[j * pad : (j + 1) * pad] = low(jnp.concatenate([block, fill], 0))
        if j == 0:
            own_ref[...] = low(block)

    @pl.loop(0, fc2_ref.shape[0] // chunk)
    def _(step):
        at = pl.ds(pl.multiple_of(step * chunk, chunk), chunk)
        out_ref[:, at] = contract(rows_ref[...], fc2_ref[at, :], 1, 1)


def feed_kernel(
    place_ref, n0_ref, n1_ref, n2_ref, n3_ref, d_act_ref, fc1_ref, fc1b_ref,
    act_ref, dpre_ref, all_ref, db_ref, o0_ref, o1_ref, o2_ref, o3_ref, *, pad, chunk,
):
    del place_ref
    rows, width = n0_ref.shape
    for j, ref in enumerate((n0_ref, n1_ref, n2_ref, n3_ref)):
        all_ref[j * pad : j * pad + rows, :] = ref[...]
        all_ref[j * pad + rows : (j + 1) * pad, :] = jnp.zeros((pad - rows, width), BF)

    @pl.loop(0, fc1_ref.shape[1] // chunk)
    def _(step):
        at = pl.ds(pl.multiple_of(step * chunk, chunk), chunk)
        pre = matmul(all_ref[...], fc1_ref[:, at]) + fc1b_ref[:, at]
        act, slope = gelu_pair(pre)
        act_ref[:, at] = low(act)
        d_low = low(d_act_ref[:, at] * slope)
        dpre_ref[:, at] = d_low
        db_ref[:, at] = jnp.sum(d_low.astype(F32), 0, keepdims=True)

    for j, ref in enumerate((o0_ref, o1_ref, o2_ref, o3_ref)):
        part = contract(dpre_ref[j * pad : (j + 1) * pad, :], fc1_ref[...], 1, 1)
        ref[...] = low(part[:rows])


def second_kernel(place_ref, act_ref, fc2_ref, kept_ref, sent_ref, *, pad, groups):
    rank = place_ref[0]
    rows = kept_ref.shape[1]
    for ref, k, flip in ((sent_ref, 0, 1), (sent_ref, 1, 3), (kept_ref, 0, 0), (kept_ref, 1, 2)):
        block = lax.rem(rank + groups - (rank ^ flip), groups)
        at = pl.ds(pl.multiple_of(block * pad, pad), pad)
        ref[k] = low(matmul(act_ref[at, :], fc2_ref[...])[:rows])


def back2_kernel(
    place_ref, c0_ref, c1_ref, c2_ref, c3_ref, resid1_ref, dy_ref, n2g_ref, own_ref, mine_ref, theirs_ref,
    dresid1_ref, dheads_ref, proj_ref, *, groups,
):
    whole_proj(place_ref, own_ref, mine_ref, theirs_ref, proj_ref, groups)
    rows = dheads_ref.shape[0]
    d_norm2 = (
        c0_ref[...].astype(F32) + c1_ref[...].astype(F32)
        + c2_ref[...].astype(F32) + c3_ref[...].astype(F32)
    )
    hat2, inv2 = normalise(resid1_ref[...])
    dy = dy_ref[...].astype(F32)
    d_resid1 = dy + norm_backward(d_norm2, hat2, inv2, n2g_ref[...])
    dresid1_ref[:rows] = d_resid1
    sums = (d_resid1, d_norm2 * hat2, d_norm2, dy)
    for k, part in enumerate(sums):
        dresid1_ref[rows + k : rows + k + 1] = jnp.sum(part, 0, keepdims=True)
    dheads_ref[...] = low(contract(low(d_resid1), proj_ref[...], 1, 1))


def back1_kernel(
    place_ref, d0_ref, d1_ref, d2_ref, d3_ref, dresid1_ref, resid0_ref, n1g_ref, qw_any,
    dresid0_ref, sums_ref, qw_ref, sems,
):
    rows, width = resid0_ref.shape
    quad = place_ref[2]
    lanes = width // 4
    copies = [
        pltpu.make_async_copy(qw_any.at[:, pl.ds(i * width, width)], qw_ref.at[i], sems.at[i])
        for i in range(3)
    ]
    for copy in copies:
        copy.start()
    hat1, inv1 = normalise(resid0_ref[...])
    d_norm1 = jnp.zeros((rows, width), F32)
    for i in range(3):
        copies[i].wait()
        for j, d_ref in enumerate((d0_ref, d1_ref, d2_ref, d3_ref)):
            part = d_ref[:, i * lanes : (i + 1) * lanes]
            at = pl.ds(pl.multiple_of((quad ^ j) * lanes, lanes), lanes)
            d_norm1 = d_norm1 + contract(part, qw_ref[i, :, at], 1, 1)
            sums_ref[2 + i : 3 + i, at] = jnp.sum(part.astype(F32), 0, keepdims=True)
    dresid0_ref[...] = low(
        dresid1_ref[:rows] + norm_backward(d_norm1, hat1, inv1, n1g_ref[...])
    )
    sums_ref[0:1] = jnp.sum(d_norm1 * hat1, 0, keepdims=True)
    sums_ref[1:2] = jnp.sum(d_norm1, 0, keepdims=True)


def back0_kernel(
    place_ref, dresid0_ref, flat_ref, mg_ref, mw_any, grad_ref, sums_ref, mw_ref, sems
):
    del place_ref
    copy = pltpu.make_async_copy(mw_any, mw_ref, sems.at[0])
    copy.start()
    hat, inv = normalise(flat_ref[...].astype(F32))
    copy.wait()
    d_merged = contract(dresid0_ref[...], mw_ref[...], 1, 1)
    grad_ref[...] = low(norm_backward(d_merged, hat, inv, mg_ref[...]))
    width = dresid0_ref.shape[1]
    gain = jnp.sum(d_merged * hat, 0, keepdims=True)
    shift = jnp.sum(d_merged, 0, keepdims=True)
    for i in range(gain.shape[1] // width):
        sums_ref[i : i + 1] = gain[:, i * width : (i + 1) * width]
        sums_ref[2 + i : 3 + i] = shift[:, i * width : (i + 1) * width]


SPAN = 2 * WIN - 1
OFFSETS = 384
STRIP = 256


def strip_picks(column, offsets_first):
    shape, o_dim = ((OFFSETS, STRIP), 0) if offsets_first else ((STRIP, OFFSETS), 1)
    offset = lax.broadcasted_iota(jnp.int32, shape, o_dim)
    lane = lax.broadcasted_iota(jnp.int32, shape, 1 - o_dim)
    wanted = (SPAN - 1 - lane // WIN) * SPAN + column - lane % WIN + WIN - 1
    hit = (offset == wanted) & (lane < SPAN * WIN)
    return jnp.where(hit, 1.0, 0.0).astype(BF)


def split3(values):
    first = low(values)
    rest = values - first.astype(F32)
    second = low(rest)
    third = low(rest - second.astype(F32))
    return first, second, third


def spread_kernel(place_ref, m0_ref, m1_ref, m2_ref, m3_ref, bias_ref, table_ref, *, part, groups):
    heads = table_ref.shape[0]
    own_heads = heads // groups
    room = m0_ref.shape[1] // 2
    for j, ref in enumerate((m0_ref, m1_ref, m2_ref, m3_ref)):
        both = ref[part : part + 2 * own_heads, :].astype(F32)[:own_heads]
        at = pl.multiple_of(lax.rem(place_ref[0] + groups - j, groups) * own_heads, own_heads)
        table_ref[pl.ds(at, own_heads), :] = both[:, :OFFSETS] + both[:, room : room + OFFSETS]
    table = table_ref[...]
    high = low(table)
    table = jnp.concatenate([high, low(table - high.astype(F32))], 0)
    for column in range(WIN):
        parts = matmul(table, strip_picks(column, True))
        strip = parts[:heads] + parts[heads:]
        for r in range(WIN):
            start = (WIN - 1 - r) * WIN
            at = (r * WIN + column) * heads
            bias_ref[at : at + heads, :] = strip[:, start : start + KEY_ROWS]
    bias_ref[WINDOW_TOKENS * heads :, :] = jnp.zeros(
        ((QUERY_ROWS - WINDOW_TOKENS) * heads, KEY_ROWS), F32
    )


def fold(grad_ref, heads):
    total = jnp.zeros((3 * heads, OFFSETS), F32)
    for column in range(WIN):
        strip = jnp.zeros((heads, STRIP), F32)
        for r in range(WIN):
            start = (WIN - 1 - r) * WIN
            at = (r * WIN + column) * heads
            part = grad_ref[at : at + heads, :]
            wide = jnp.concatenate([part, jnp.zeros((heads, STRIP - KEY_ROWS), F32)], 1)
            strip = strip + (pltpu.roll(wide, start, 1) if start else wide)
        total = total + matmul(jnp.concatenate(split3(strip), 0), strip_picks(column, False))
    return total[:heads] + total[heads : 2 * heads] + total[2 * heads :]


def window_rows(values, window, rows):
    part = values.astype(F32)[window * WINDOW_TOKENS : (window + 1) * WINDOW_TOKENS]
    zeros = jnp.zeros((rows - WINDOW_TOKENS, part.shape[1]), F32)
    return low(jnp.concatenate([part, zeros], 0))


def stack_heads(part, heads, head_dim):
    lane = lax.broadcasted_iota(jnp.int32, part.shape, 1) // head_dim
    zero = jnp.zeros_like(part)
    return jnp.concatenate([jnp.where(lane == h, part, zero) for h in range(heads)], 0)


def attend_kernel(
    place_ref, qkv_ref, bias_ref, mask_ref, out_ref, probs_any, probs_ref, sems, *, windows, head_dim
):
    del place_ref
    width = out_ref.shape[1]
    lanes = width // 4

    def keep(step):
        return pltpu.make_async_copy(probs_ref.at[step], probs_any.at[step], sems.at[step])

    @pl.loop(0, 4)
    def _(step):
        attend_group(
            step, qkv_ref, bias_ref, mask_ref, out_ref, probs_ref, windows, head_dim, width, lanes
        )
        keep(step).start()

    for step in range(4):
        keep(step).wait()


def attend_group(
    step, qkv_ref, bias_ref, mask_ref, out_ref, probs_ref, windows, head_dim, width, lanes
):
    heads, all_heads = lanes // head_dim, width // head_dim
    first = step * heads
    scale = head_dim ** (-0.5)
    at = lambda kind: pl.ds(pl.multiple_of(kind * width + step * lanes, lanes), lanes)
    q_all, k_all, v_all = (qkv_ref[:, at(kind)] for kind in range(3))
    outs = []
    for w in range(windows):
        query = window_rows(q_all, w, QUERY_ROWS)
        keys = stack_heads(window_rows(k_all, w, KEY_ROWS), heads, head_dim)
        values = stack_heads(window_rows(v_all, w, KEY_ROWS), heads, head_dim)
        scores = contract(query, keys, 1, 1) * scale
        mask = mask_ref[w]
        rounded = []
        for h in range(heads):
            bias = bias_ref[pl.ds(first + h, QUERY_ROWS, stride=all_heads), :]
            raw = scores[:, h * KEY_ROWS : (h + 1) * KEY_ROWS] + bias + mask
            expo = jnp.exp(raw - jnp.max(raw, -1, keepdims=True))
            probs = expo / jnp.sum(expo, -1, keepdims=True)
            probs_ref[step, w, h] = probs
            rounded.append(low(probs))
        mixed = matmul(jnp.concatenate(rounded, 1), values)
        outs.append(mixed[:WINDOW_TOKENS])
    out_ref[:, at(0)] = low(jnp.concatenate(outs, 0))


def attend_back_kernel(
    place_ref, qkv_ref, grad_ref, probs_any, d0_ref, d1_ref, d2_ref, d3_ref, table_ref, dbias_ref, probs_ref, sems,
    *, windows, head_dim
):
    width = grad_ref.shape[1]

    def fetch(step):
        return pltpu.make_async_copy(
            probs_any.at[place_ref[2] ^ step], probs_ref.at[step], sems.at[step]
        )

    for step in range(4):
        fetch(step).start()

    @pl.loop(0, 4)
    def _(step):
        fetch(step).wait()
        attend_back_group(
            place_ref[2] ^ step, step, qkv_ref, grad_ref, probs_ref, (d0_ref, d1_ref, d2_ref, d3_ref), dbias_ref,
            windows, head_dim, width, width // 4,
        )

    table_ref[...] = fold(dbias_ref, table_ref.shape[0])


def attend_back_group(
    group, step, qkv_ref, grad_ref, probs_ref, d_refs, dbias_ref,
    windows, head_dim, width, lanes,
):
    heads, all_heads = lanes // head_dim, width // head_dim
    first = group * heads
    scale = head_dim ** (-0.5)
    at = lambda kind: pl.ds(pl.multiple_of(kind * width + group * lanes, lanes), lanes)
    q_all, k_all, v_all = (qkv_ref[:, at(kind)] for kind in range(3))
    g_all = grad_ref[:, at(0)]
    all_q, all_k, all_v = [], [], []
    d_first = []
    for w in range(windows):
        query = stack_heads(window_rows(q_all, w, QUERY_ROWS), heads, head_dim)
        keys = stack_heads(window_rows(k_all, w, KEY_ROWS), heads, head_dim)
        values = stack_heads(window_rows(v_all, w, KEY_ROWS), heads, head_dim)
        plain = window_rows(g_all, w, QUERY_ROWS)
        grad = stack_heads(plain, heads, head_dim)
        d_probs = contract(plain, values, 1, 1)
        d_list, p_list = [], []
        for h in range(heads):
            probs = probs_ref[step, w, h]
            part = d_probs[:, h * KEY_ROWS : (h + 1) * KEY_ROWS]
            total = jnp.sum(part * probs, -1, keepdims=True)
            d_scores = low(probs * (part - total))
            d_list.append(d_scores)
            p_list.append(low(probs))
            if w == 0:
                d_first.append(d_scores.astype(F32))
            else:
                d_first[h] = d_first[h] + d_scores.astype(F32)
            if w == windows - 1:
                dbias_ref[pl.ds(first + h, QUERY_ROWS, stride=all_heads), :] = d_first[h]
        d_query = matmul(jnp.concatenate(d_list, 1), keys) * scale
        d_keys = contract(jnp.concatenate(d_list, 0), query, 0, 0) * scale
        d_values = contract(jnp.concatenate(p_list, 0), grad, 0, 0)
        all_q.append(d_query[:WINDOW_TOKENS])
        all_k.append(d_keys[:WINDOW_TOKENS])
        all_v.append(d_values[:WINDOW_TOKENS])
    result = jnp.concatenate(
        [low(jnp.concatenate(parts, 0)) for parts in (all_q, all_k, all_v)], 1
    )

    for k, d_ref in enumerate(d_refs):

        @pl.when(step == k)
        def _(d_ref=d_ref):
            d_ref[...] = result


def spots(heads, lines, vectors):
    columns = 3
    return [(k // columns, OFFSETS + 128 * (k % columns)) for k in range(vectors * lines)]


def collect_kernel(place_ref, s0_ref, s1_ref, d_ref, rel_ref, b_ref, out_ref):
    heads = rel_ref.shape[0]
    lines = s0_ref.shape[1] // 128
    out_ref[...] = jnp.zeros(out_ref.shape, F32)
    out_ref[:heads, :OFFSETS] = rel_ref[...]
    vectors = [ref[r : r + 1, :] for ref in (s0_ref, s1_ref) for r in range(ref.shape[0])]
    after = d_ref.shape[0] - 8
    vectors += [d_ref[after + r : after + r + 1, :] for r in range(4)]
    for k, (at, lane) in enumerate(spots(heads, lines, len(vectors))):
        piece = vectors[k // lines][:, 128 * (k % lines) : 128 * (k % lines + 1)]
        out_ref[at : at + 1, lane : lane + 128] = piece
    own = b_ref.shape[1] // 128
    first = heads + pl.multiple_of((place_ref[0] // 2) * own, own)
    block = jnp.concatenate([b_ref[:, k * 128 : (k + 1) * 128] for k in range(own)], 0)
    side = place_ref[0] % 2

    @pl.when(side == 0)
    def _():
        out_ref[pl.ds(first, own), 0:128] = block

    @pl.when(side == 1)
    def _():
        out_ref[pl.ds(first, own), 128:256] = block


def deliver_kernel(place_ref, all_ref, *refs, heads):
    *vector_refs, rel_ref, b_ref = refs
    rel_ref[...] = all_ref[:heads, : rel_ref.shape[1]]
    lines = [ref.shape[0] // 128 for ref in vector_refs]
    places = iter(spots(heads, 1, sum(lines)))
    for ref, count in zip(vector_refs, lines):
        for k in range(count):
            at, lane = next(places)
            ref[128 * k : 128 * (k + 1)] = all_ref[at, lane : lane + 128]
    own = b_ref.shape[0]
    first = heads + pl.multiple_of((place_ref[0] // 2) * own, own)
    side = place_ref[0] % 2

    @pl.when(side == 0)
    def _():
        b_ref[...] = all_ref[pl.ds(first, own), 0:128]

    @pl.when(side == 1)
    def _():
        b_ref[...] = all_ref[pl.ds(first, own), 128:256]


def columns_kernel(place_ref, b0_ref, b1_ref, b2_ref, b3_ref, own_ref, out_ref, sums_ref):
    rows = out_ref.shape[0]
    lanes = b0_ref.shape[2] // 3
    total = own_ref[...]
    for j, ref in enumerate((b0_ref, b1_ref, b2_ref, b3_ref)):
        for part in range(3):
            at = pl.multiple_of((part * 4 + (place_ref[2] ^ j)) * lanes, lanes)
            out_ref[:, pl.ds(at, lanes)] = ref[0, :rows, part * lanes : (part + 1) * lanes].astype(F32)
        if j:
            total = total + take_sums(ref, 1, own_ref.shape[0])
    sums_ref[...] = total


def on_device(
    patches,
    window_extent,
    merge_gain,
    merge_shift,
    merge_weight,
    norm1_gain,
    norm1_shift,
    qkv_weight,
    qkv_bias,
    rel_table,
    proj_weight,
    proj_bias,
    norm2_gain,
    norm2_shift,
    fc1_weight,
    fc1_bias,
    fc2_weight,
    fc2_bias,
    out_grad,
):
    groups, wide = lax.axis_size("narrow"), lax.axis_size("wide")
    devices = wide * groups
    highs = wide // 8
    wide_at, rank = lax.axis_index("wide"), lax.axis_index("narrow")
    core, quad, high = wide_at % 2, (wide_at // 2) % 4, wide_at // 8
    place = jnp.stack([rank, core, quad]).astype(jnp.int32)
    tokens = patches.shape[0]
    width = qkv_weight.shape[0]
    own_heads = rel_table.shape[1]
    heads = own_heads * groups
    head_dim = width // heads
    windows = tokens // WINDOW_TOKENS
    pad = tokens + (-tokens) % 16

    def arrange(array, order):
        if highs == 1:
            return array
        sizes = {"h": highs, "q": 4, "c": 2, "n": groups}
        cut = [sizes[k] for k in order]
        rest = array.shape[1]
        for size in cut:
            rest //= size
        at = order.index("h") + 1
        moved = [i + 1 for i in range(len(order)) if i + 1 != at] + [at, len(order) + 1]
        return jnp.transpose(array.reshape(-1, *cut, rest), [0] + moved).reshape(array.shape)

    def settle(array):
        if highs == 1:
            return array[0]
        return sum_high(array[0].reshape(highs, -1, array.shape[2]), high)

    part = proj_weight.shape[0] // 8
    message = whole(
        pack_kernel,
        place,
        [shape_of((part + own_heads + (-(part + own_heads)) % 16, width), BF)],
        (proj_weight, True),
        (rel_table, True),
        name="pack",
    )[0]
    messages = [turn(message, "narrow", step) for step in range(1, groups)]

    flat = patches.reshape(tokens, -1)
    merged, resid0, normed1, qkv = front_call(
        place, flat, merge_gain, merge_shift, norm1_gain, norm1_shift, qkv_bias,
        merge_weight, qkv_weight,
    )
    mine = whole(
        functools.partial(pieces_kernel, part=part),
        place,
        [shape_of(((groups - 1) * part, width), BF)],
        *((m, True) for m in messages),
        name="pieces",
    )
    mine = list(mine) + [swap(mine[0], "wide", 2 * j) for j in (1, 2, 3)]

    merged_own, merged_sent, merged_onward = whole(
        cut_kernel,
        place,
        [
            shape_of((tokens, merged.shape[1] // 4), BF),
            shape_of((2, tokens, merged.shape[1] // 4), BF),
            shape_of((tokens, merged.shape[1] // 4), BF),
        ],
        (arrange(merged, "hqcn"), True),
        name="cut",
    )
    normed1_cut = arrange(normed1, "hqcn")

    positions = jnp.arange(KEY_ROWS)
    extent = lax.dynamic_slice_in_dim(window_extent, rank * windows, windows, 0)
    valid = (
        (positions[None, :] // WIN < extent[:, 0:1])
        & (positions[None, :] % WIN < extent[:, 1:2])
        & (positions[None, :] < WINDOW_TOKENS)
    )
    mask = jnp.where(valid, 0.0, -1e30).astype(F32)[:, None, :]
    bias = whole(
        functools.partial(spread_kernel, part=part, groups=groups),
        place,
        [shape_of((QUERY_ROWS * heads, KEY_ROWS), F32)],
        (message, True),
        *((m, True) for m in messages),
        scratch=[pltpu.VMEM((heads, OFFSETS), F32)],
        name="spread",
    )[0]
    heads_out, probs = whole(
        functools.partial(attend_kernel, windows=windows, head_dim=head_dim),
        place,
        [
            shape_of((tokens, width), BF),
            shape_of((PROBS_ROOM, windows, heads // 4, QUERY_ROWS, KEY_ROWS), F32),
        ],
        (qkv, True), (bias, True), (mask, True),
        leave=(1,),
        scratch=[
            pltpu.VMEM((4, windows, heads // 4, QUERY_ROWS, KEY_ROWS), F32),
            pltpu.SemaphoreType.DMA((4,)),
        ],
        name="attend",
    )

    mine = whole(
        mine_kernel,
        place,
        [shape_of((4 * mine[0].shape[0], width), BF)],
        *((m, True) for m in mine),
        after=(heads_out,),
        name="mine",
    )[0]
    theirs = swap(mine, "wide", 1)
    resid1, normed2, merged_sent, normed1_cut, merged_onward = whole(
        functools.partial(after_kernel, groups=groups),
        place,
        [shape_of((tokens, width), F32), shape_of((tokens, width), BF)],
        (heads_out, True), (resid0, True),
        (row(proj_bias), True), (row(norm2_gain), True), (row(norm2_shift), True),
        (proj_weight, True), (mine, True), (theirs, True),
        scratch=[pltpu.VMEM((width, width), BF)],
        through=(merged_sent, normed1_cut, merged_onward),
        name="after",
    )
    merged_near = swap(merged_sent, "wide", 4)
    normed1_near = swap(normed1_cut, "wide", 2)
    blocks = [normed2] + [turn(normed2, "narrow", step) for step in range(1, groups)]

    merged_onward = jnp.stack([merged_onward, merged_near[1]])
    merged_far = swap(merged_onward, "wide", 2)
    normed1_both = jnp.stack([normed1_cut, normed1_near])
    normed1_far = swap(normed1_both, "wide", 4)

    total, units = groups * pad, fc1_weight.shape[1]
    dy_rows, dy_own, d_act = whole(
        functools.partial(slope_kernel, groups=groups, pad=pad, chunk=256),
        place,
        [
            shape_of((total, width), BF),
            shape_of((tokens, width), BF),
            shape_of((total, units), F32),
        ],
        (out_grad, True), (fc2_weight, True),
        scratch=[pltpu.VMEM(out_grad.shape, F32)],
        after=(normed2,),
        name="slope",
    )
    act, d_pre, rows_all, fc1_b_grad, *chunks = whole(
        functools.partial(feed_kernel, pad=pad, chunk=256),
        place,
        [
            shape_of((total, units), BF),
            shape_of((total, units), BF),
            shape_of((total, width), BF),
            shape_of((1, units), F32),
        ]
        + [shape_of((tokens, width), BF)] * 4,
        *((b, True) for b in blocks), (d_act, True), (fc1_weight, True), (row(fc1_bias), True),
        after=(normed1_far, merged_far),
        name="feed",
    )
    arrived = [chunks[0]] + [turn(chunks[j], "narrow", -j) for j in range(1, groups)]

    fc1_kept, fc1_sent = grad_call(place, [arrange(rows_all, "hqc")], [d_pre], 256, 128, "fc1_grad")
    fc2_kept, fc2_sent = grad_call(place, [arrange(act, "hqc")], [dy_rows], 256, 128, "fc2_grad")
    fc1_come, fc2_come = swap(fc1_sent, "wide", 1), swap(fc2_sent, "wide", 1)
    fc1_kept, fc1_sent = join_call(
        place, [(fc1_kept, fc1_come)],
        [
            (F32, [lambda p, y=y: (0, 2 * y + p[2] % 2, 0, 128) for y in range(2)]),
            (BF, [lambda p, y=y: (0, 2 * y + 1 - p[2] % 2, 0, 128) for y in range(2)]),
        ],
        "fc1_join",
    )
    fc2_kept, fc2_sent = join_call(
        place, [(fc2_kept, fc2_come)],
        [
            (F32, [lambda p, x=x: (0, 2 * (p[2] // 2) + x, 0, 128) for x in range(2)]),
            (BF, [lambda p, x=x: (0, 2 * (1 - p[2] // 2) + x, 0, 128) for x in range(2)]),
        ],
        "fc2_join",
    )
    fc1_come, fc2_come = swap(fc1_sent, "wide", 2), swap(fc2_sent, "wide", 4)
    fc1_kept, fc1_sent = join_call(
        place, [(fc1_kept, fc1_come)],
        [
            (F32, [lambda p: (0, p[2] // 2, 0, 128)]),
            (BF, [lambda p: (0, 1 - p[2] // 2, 0, 128)]),
        ],
        "fc1_join2",
    )
    fc2_kept, fc2_sent = join_call(
        place, [(fc2_kept, fc2_come)],
        [
            (F32, [lambda p: (0, p[2] % 2, 0, 128)]),
            (BF, [lambda p: (0, 1 - p[2] % 2, 0, 128)]),
        ],
        "fc2_join2",
    )
    fc1_come, fc2_come = swap(fc1_sent, "wide", 4), swap(fc2_sent, "wide", 2)
    second_kept, second_sent = whole(
        functools.partial(second_kernel, pad=pad, groups=groups),
        place,
        [shape_of((2, tokens, width), BF)] * 2,
        (act, True),
        (fc2_weight, True),
        name="second",
    )
    d_resid1, d_heads, second_sent = whole(
        functools.partial(back2_kernel, groups=groups),
        place,
        [shape_of((tokens + 8, width), F32), shape_of((tokens, width), BF)],
        *((a, True) for a in arrived),
        (resid1, True), (dy_own, True), (row(norm2_gain), True),
        (proj_weight, True), (mine, True), (theirs, True),
        scratch=[pltpu.VMEM((width, width), BF)],
        after=(fc1_sent, fc2_sent),
        through=(second_sent,),
        name="back2",
    )
    second_come = swap(second_sent, "narrow", 1)
    *d_parts, rel_part = whole(
        functools.partial(attend_back_kernel, windows=windows, head_dim=head_dim),
        place,
        [shape_of((tokens, 3 * width // 4), BF)] * 4 + [shape_of((heads, OFFSETS), F32)],
        (qkv, True), (d_heads, True), (probs, False),
        scratch=[
            pltpu.VMEM((QUERY_ROWS * heads, KEY_ROWS), F32),
            pltpu.VMEM((4, *probs.shape[1:]), F32),
            pltpu.SemaphoreType.DMA((4,)),
        ],
        after=(fc1_come, fc2_come),
        name="attend_back",
    )
    d_come = [swap(d_parts[j], "wide", 2 * j) for j in (1, 2, 3)]

    d_resid0, sums1 = whole(
        back1_kernel,
        place,
        [shape_of((tokens, width), BF), shape_of((5, width), F32)],
        *((d, True) for d in d_parts), (d_resid1, True), (resid0, True),
        (row(norm1_gain), True), (qkv_weight, False),
        scratch=[
            pltpu.VMEM((3, width, width), BF),
            pltpu.SemaphoreType.DMA((3,)),
        ],
        name="back1",
    )
    d_flat, sums0 = whole(
        back0_kernel,
        place,
        [shape_of(flat.shape, BF), shape_of((2 * flat.shape[1] // width, width), F32)],
        (d_resid0, True), (flat, True), (row(merge_gain), True), (merge_weight, False),
        scratch=[pltpu.VMEM(merge_weight.shape, BF), pltpu.SemaphoreType.DMA((1,))],
        name="back0",
    )

    second_own, second_sent = join_call(
        place, [(second_kept, second_come)],
        [(F32, [lambda p: (0, 0, 0, tokens)]), (BF, [lambda p: (0, 1, 0, tokens)])],
        "second_join",
    )
    second_come = swap(second_sent, "narrow", 2)

    proj_kept, proj_sent = grad_call(
        place, [arrange(heads_out, "nhqc")], [d_resid1], 256, 32, "proj_grad", after=(d_resid0,)
    )
    proj_come = swap(proj_sent, "wide", 1)

    side = lambda pick_x: [
        lambda p, n=n, y=y: (0, n, (2 * y + pick_x(p[2] % 2)) * 32, 32)
        for n in range(groups) for y in range(2)
    ]
    proj_kept, proj_sent = join_call(
        place, [(proj_kept, proj_come)],
        [(F32, side(lambda x: x)), (BF, side(lambda x: 1 - x))],
        "proj_join",
    )
    proj_come = swap(proj_sent, "wide", 2)

    own_sums, d_resid0 = whole(
        collect_kernel,
        place,
        [shape_of((48, 3 * width // 4), F32)],
        (sums0, True), (sums1, True), (d_resid1, True), (rel_part, True), (fc1_b_grad, True),
        after=(*d_come, second_sent, proj_sent),
        through=(d_resid0,),
        name="collect",
    )
    r_come = [swap(d_resid0, "wide", 2 * j) for j in (1, 2, 3)]
    qkv_kept, qkv_sent = grad_call(
        place,
        [normed1_cut, (normed1_both, 1), (normed1_far, 0), (normed1_far, 1)],
        [d_parts[0], *d_come],
        256, 128, "qkv_grad", sums=own_sums, after=(second_sent,),
    )
    qkv_come = swap(qkv_sent, "wide", 1)
    rows = 128 // groups
    qkv_pieces = lambda flip: [
        lambda p, g=g, k=k: (0, g, (2 * k + (p[0] + flip) % 2) * rows, rows)
        for k in range(2) for g in range(4)
    ]
    own_sums, qkv_kept, qkv_sent = join_call(
        place, [(qkv_kept, qkv_come)], [(F32, qkv_pieces(0)), (BF, qkv_pieces(1))], "qkv_join",
        sums=(own_sums, 4),
    )
    qkv_come = swap(qkv_sent, "narrow", 1)

    merge_kept, merge_sent = grad_call(
        place,
        [merged_own, (merged_far, 0), (merged_near, 0), (merged_far, 1)],
        [d_resid0, *r_come],
        merged_own.shape[1], merged_own.shape[1] // 2, "merge_grad", after=(qkv_sent,),
    )
    merge_come = swap(merge_sent, "wide", 1)

    second_pieces = lambda flip: [
        lambda p, g=g: (0, ((p[0] // 2 + flip) % 2) * 4 + g, 0, rows) for g in range(4)
    ]
    own_sums, qkv_kept, qkv_sent = join_call(
        place, [(qkv_kept, qkv_come)],
        [(F32, second_pieces(0)), (BF, second_pieces(1))],
        "qkv_join2",
        sums=(own_sums, 8),
        after=(merge_sent,),
    )
    qkv_come = swap(qkv_sent, "narrow", 2)
    merge_rows = merged_own.shape[1] // 2 // groups
    merge_pieces = lambda flip: [
        lambda p, k=k: (0, 0, (2 * k + (p[0] + flip) % 2) * merge_rows, merge_rows)
        for k in range(2)
    ]
    merge_kept, merge_sent, fc1_come, fc2_come, d_flat = join_call(
        place, [(merge_kept, merge_come)],
        [(F32, merge_pieces(0)), (BF, merge_pieces(1))],
        "merge_join",
        after=(qkv_sent,),
        through=(fc1_come, fc2_come, d_flat),
    )
    merge_first = merge_sent
    merge_come = swap(merge_sent, "narrow", 1)

    last_pieces = lambda flip, size: [lambda p: (0, (p[0] // 2 + flip) % 2, 0, size)]
    merge_kept, merge_sent = join_call(
        place, [(merge_kept, merge_come)],
        [(F32, last_pieces(0, merge_rows)), (BF, last_pieces(1, merge_rows))],
        "merge_join2",
        after=(qkv_sent,),
    )
    merge_last = merge_sent
    merge_come = swap(merge_sent, "narrow", 2)

    proj_kept, proj_sent = join_call(
        place, [(proj_kept, proj_come)],
        [
            (F32, [lambda p, n=n: (0, 2 * n + p[2] // 2, 0, 32) for n in range(groups)]),
            (BF, [lambda p, n=n: (0, 2 * n + 1 - p[2] // 2, 0, 32) for n in range(groups)]),
        ],
        "proj_join2",
        after=(merge_first,),
    )
    proj_come = swap(proj_sent, "wide", 4)
    proj_pieces = lambda flip: [
        lambda p, k=k: (0, 2 * k + (p[0] + flip) % 2, 0, 32) for k in range(2)
    ]
    proj_kept, proj_sent = join_call(
        place, [(proj_kept, proj_come)], [(F32, proj_pieces(0)), (BF, proj_pieces(1))],
        "proj_join3",
        after=(merge_sent,),
    )
    proj_come = swap(proj_sent, "narrow", 1)
    proj_kept, proj_sent = join_call(
        place, [(proj_kept, proj_come)],
        [(F32, last_pieces(0, 32)), (BF, last_pieces(1, 32))],
        "proj_join4",
    )
    proj_come = swap(proj_sent, "narrow", 2)

    own_sums, *cuts = join_call(
        place, [(qkv_kept, qkv_come)],
        [(BF, [lambda p, j=j: (0, p[2] ^ j, 0, rows)]) for j in range(4)],
        "qkv_join3",
        sums=(own_sums, 4),
        after=(merge_last,),
    )
    cuts = [cuts[0]] + [swap(cuts[j], "wide", 2 * j) for j in (1, 2, 3)]
    qkv_out, all_sums = whole(
        columns_kernel,
        place,
        [shape_of((rows, 3 * width), F32), shape_of(own_sums.shape, F32)],
        *((c, True) for c in cuts), (own_sums, True),
        name="columns",
    )
    qkv_out = settle(qkv_out[None])
    mask = 8
    while mask < wide:
        all_sums = all_sums + swap(all_sums, "wide", mask)
        mask *= 2
    merge_out = settle(merge_kept + merge_come.astype(F32))
    proj_out = settle(proj_kept + proj_come.astype(F32))

    fc1_out = settle(fc1_kept + fc1_come.astype(F32))
    fc2_out = settle(fc2_kept + fc2_come.astype(F32))
    patches_grad = d_flat.reshape(patches.shape)
    output = low(resid1 + row(fc2_bias) + second_own[0] + second_come[0].astype(F32))

    deep = merged.shape[1]
    *vectors, rel_grad, fc1_b_mine = whole(
        functools.partial(deliver_kernel, heads=heads),
        place,
        [
            shape_of((size,), F32)
            for size in (deep, deep, width, width, 3 * width, width, width, width, width)
        ]
        + [shape_of((heads, rel_table.shape[0]), F32), shape_of((units // 128, 128), F32)],
        (all_sums, True),
        name="deliver",
    )
    fc1_b_out = lax.dynamic_index_in_dim(
        fc1_b_mine.reshape(wide, -1), wide_at, 0, keepdims=False
    )

    return (
        output,
        patches_grad,
        vectors[0],
        vectors[1],
        merge_out,
        vectors[2],
        vectors[3],
        qkv_out,
        vectors[4],
        jnp.transpose(rel_grad),
        proj_out,
        vectors[5],
        vectors[6],
        vectors[7],
        fc1_out,
        fc1_b_out,
        fc2_out,
        vectors[8],
    )


def solution(mesh):
    in_specs = (
        P(("wide", "narrow"), None, None),
        P("wide", None),
        P(),
        P(),
        P(),
        P(),
        P(),
        P(),
        P(),
        P(None, "narrow"),
        P("narrow", None),
        P(),
        P(),
        P(),
        P(None, "narrow"),
        P("narrow"),
        P("narrow", None),
        P(),
        P("wide", None),
    )
    out_specs = (
        P(("wide", "narrow"), None),
        P(("wide", "narrow"), None, None),
        P(),
        P(),
        P(("wide", "narrow"), None),
        P(),
        P(),
        P(("wide", "narrow"), None),
        P(),
        P(),
        P(("narrow", "wide"), None),
        P(),
        P(),
        P(),
        P("wide", "narrow"),
        P(("narrow", "wide")),
        P(("narrow", "wide"), None),
        P(),
    )
    return jax.shard_map(
        on_device, mesh=mesh, in_specs=in_specs, out_specs=out_specs, check_vma=False
    )
```

```python
import functools

import jax
import jax.numpy as jnp
from jax import lax
from jax.experimental import pallas as pl
from jax.experimental.pallas import tpu as pltpu
from jax.sharding import PartitionSpec as P

WIN = 10
WINDOW_TOKENS = WIN * WIN
QUERY_ROWS = 112
KEY_ROWS = 128
EPS = 1e-05
MEBI = 1024 * 1024
PROBS_ROOM = 52
WAIT_US = 100.0
WEIGHT_US = {"back1": 20, "proj_grad": 20, "back0": 20, "second_join": 20, "proj_join": 20}
WEIGHT_US |= dict.fromkeys(
    ("pack", "front", "cut", "pieces", "spread", "attend", "mine", "after", "slope", "feed", "second", "fc1_grad",
     "fc2_grad", "fc1_join", "fc2_join", "fc1_join2", "fc2_join2"), WAIT_US
)
FLOPS_PER_US = 10**9
BF = jnp.bfloat16
F32 = jnp.float32


def normalise(values):
    average = jnp.mean(values, -1, keepdims=True)
    centred = values - average
    inverse = lax.rsqrt(jnp.mean(centred * centred, -1, keepdims=True) + EPS)
    return centred * inverse, inverse


def norm_backward(grad_out, normal, inverse, gain):
    scaled = grad_out * gain
    return inverse * (
        scaled
        - jnp.mean(scaled, -1, keepdims=True)
        - normal * jnp.mean(scaled * normal, -1, keepdims=True)
    )


def matmul(left, right):
    return jnp.dot(left, right, preferred_element_type=jnp.float32)


def contract(left, right, left_dim, right_dim):
    return lax.dot_general(
        left, right, (((left_dim,), (right_dim,)), ((), ())), preferred_element_type=jnp.float32
    )


def low(array):
    return array.astype(BF)


def row(vector):
    return vector.reshape(1, -1)


def stays():
    return pl.BlockSpec(memory_space=pl.ANY)


def outside():
    return pl.BlockSpec(memory_space=pltpu.HBM)


def held():
    return pl.BlockSpec(memory_space=pltpu.VMEM)


def shape_of(shape, dtype):
    return jax.ShapeDtypeStruct(shape, dtype)


def whole(
    kernel, place, outs, *operands, leave=(), scratch=(), after=(), through=(), room=20, name=None
):
    arrays = [a for a, _ in operands]
    count, skip, given = len(arrays), len(after) + len(through), len(outs)

    def body(place_ref, *refs):
        own_outs = refs[count + skip : count + skip + given]
        kernel(place_ref, *refs[:count], *own_outs, *refs[count + skip + given + len(through) :])

    return pl.pallas_call(
        body,
        in_specs=[pl.BlockSpec(memory_space=pltpu.SMEM)]
        + [{True: held, False: outside, None: stays}[inside]() for _, inside in operands]
        + [stays()] * skip,
        out_specs=[outside() if k in leave else held() for k in range(given)]
        + [stays()] * len(through),
        out_shape=list(outs) + [shape_of(a.shape, a.dtype) for a in through],
        input_output_aliases={1 + count + len(after) + k: given + k for k in range(len(through))},
        scratch_shapes=list(scratch),
        compiler_params=pltpu.CompilerParams(vmem_limit_bytes=room * MEBI),
        cost_estimate=pl.CostEstimate(
            flops=int(WEIGHT_US.get(name, 5) * FLOPS_PER_US), bytes_accessed=0, transcendentals=0
        ),
        name=name,
    )(place, *arrays, *after, *through)


def tie(array, *after):
    def body(*refs):
        del refs

    return pl.pallas_call(
        body,
        in_specs=[stays()] * (1 + len(after)),
        out_specs=stays(),
        out_shape=shape_of(array.shape, array.dtype),
        input_output_aliases={0: 0},
        name="tie",
    )(array, *after)


def swap(array, axis, mask):
    size = lax.axis_size(axis)
    return lax.ppermute(array, axis, [(i, i ^ mask) for i in range(size)])


def turn(array, axis, step):
    size = lax.axis_size(axis)
    return lax.ppermute(array, axis, [(i, (i + step) % size) for i in range(size)])


def sum_all(vector):
    mask = 1
    while mask < lax.axis_size("wide"):
        vector = vector + swap(vector, "wide", mask)
        mask *= 2
    mask = 1
    while mask < lax.axis_size("narrow"):
        vector = vector + swap(vector, "narrow", mask)
        mask *= 2
    return vector


def sum_high(parts, high):
    take = lambda index: lax.dynamic_index_in_dim(parts, index, 0, keepdims=False)
    total = take(high).astype(F32)
    for j in range(1, parts.shape[0]):
        total = total + swap(low(take(high ^ j)), "wide", 8 * j).astype(F32)
    return total


def grad_kernel(place_ref, *refs, lefts, rights, block, rows, riding):
    left_refs, right_refs = refs[: len(lefts)], refs[len(lefts) : len(lefts) + len(rights)]
    kept_ref, sent_ref, total_ref = refs[-3:]
    core = place_ref[1]
    if riding:
        give_sums(sent_ref, kept_ref.shape[0], refs[-4][...])

    @pl.loop(0, kept_ref.shape[0])
    def _(step):
        at = pl.ds(pl.multiple_of(step * block, block), block)
        total = None
        for l_ref, l_at, r_ref, r_at in zip(left_refs, lefts, right_refs, rights):
            left = l_ref[:, at] if l_at is None else l_ref[l_at, :, at]
            right = r_ref[: left.shape[0]] if r_at is None else r_ref[r_at]
            right = low(right)
            part = contract(left, right, 0, 0)
            total = part if total is None else total + part
        total_ref[...] = total
        for s in range(block // (2 * rows)):
            mine = pl.multiple_of((2 * s + core) * rows, rows)
            theirs = pl.multiple_of((2 * s + 1 - core) * rows, rows)
            kept_ref[step, s * rows : (s + 1) * rows] = total_ref[pl.ds(mine, rows)]
            sent_ref[step, s * rows : (s + 1) * rows] = low(total_ref[pl.ds(theirs, rows)])


def grad_call(place, lefts, rights, block, rows, name, after=(), sums=None):
    split = lambda item: item if isinstance(item, tuple) else (item, None)
    left_arrays, left_at = zip(*map(split, lefts))
    right_arrays, right_at = zip(*map(split, rights))
    deep, width = left_arrays[0].shape[-1], right_arrays[0].shape[-1]
    shape = (deep // block, block // 2, width)
    return whole(
        functools.partial(
            grad_kernel, lefts=left_at, rights=right_at, block=block, rows=rows,
            riding=sums is not None,
        ),
        place,
        [shape_of(shape, F32), shape_of((shape[0] + (sums is not None), *shape[1:]), BF)],
        *((a, True) for a in left_arrays + right_arrays + (() if sums is None else (sums,))),
        scratch=[pltpu.VMEM((block, width), F32)],
        after=after,
        name=name,
    )


def add_up(refs, lead, rows):
    total = None
    for ref in refs:
        part = ref[lead, rows, :].astype(F32)
        total = part if total is None else total + part
    return total


def join_call(place, groups, outs, name, after=(), through=(), sums=None):
    width = groups[0][0].shape[2]
    counts = [len(sources) for sources in groups]
    count = sum(counts)
    rows_of = [pieces[0]((0, 0, 0))[3] for _, pieces in outs]
    more = -(-sums[0].shape[0] // rows_of[1]) if sums else 0
    shapes = [
        shape_of((len(pieces) + (more if k else 0), rows, width), dtype)
        for k, ((dtype, pieces), rows) in enumerate(zip(outs, rows_of))
    ]
    if sums:
        shapes = [shape_of(sums[0].shape, F32)] + shapes

    def kernel(place_ref, *refs):
        place_now = (place_ref[0], place_ref[1], place_ref[2])
        ins, out_refs = refs[:count], refs[count:]
        if sums:
            own_ref, total_ref, out_refs = refs[count], refs[count + 1], refs[count + 2 :]
            total = own_ref[...] + take_sums(ins[counts[0] - 1], sums[1], own_ref.shape[0])
            total_ref[...] = total
        at = [sum(counts[:g]) for g in range(len(counts))]
        for k, (out_ref, (dtype, pieces)) in enumerate(zip(out_refs, outs)):
            for n, piece in enumerate(pieces):
                group, lead, start, rows = piece(place_now)
                if not isinstance(start, int):
                    start = pl.multiple_of(start, rows)
                part = add_up(ins[at[group] : at[group] + counts[group]], lead, pl.ds(start, rows))
                out_ref[n] = part.astype(dtype)
            if sums and k:
                give_sums(out_ref, len(pieces), total)

    arrays = [s for sources in groups for s in sources] + ([sums[0]] if sums else [])
    return whole(
        kernel, place, shapes, *((s, True) for s in arrays), after=after, through=through, name=name
    )


def give_sums(ref, first, values):
    parts = low(values)
    size = ref.shape[1]
    for k in range(parts.shape[0] // size):
        ref[first + k] = parts[k * size : (k + 1) * size]
    rest = parts.shape[0] % size
    if rest:
        ref[first + parts.shape[0] // size, :rest] = parts[parts.shape[0] - rest :]


def take_sums(ref, first, rows):
    size = ref.shape[1]
    blocks = [ref[first + k].astype(F32) for k in range(-(-rows // size))]
    return (jnp.concatenate(blocks, 0) if len(blocks) > 1 else blocks[0])[:rows]


def cut_kernel(place_ref, merged_ref, own_ref, sent_ref, onward_ref):
    quad = place_ref[2]
    lanes = own_ref.shape[1]
    take = lambda j: merged_ref[:, pl.ds(pl.multiple_of((quad ^ j) * lanes, lanes), lanes)]
    own_ref[...] = take(0)
    sent_ref[0] = take(2)
    sent_ref[1] = take(3)
    onward_ref[...] = take(1)


def pack_kernel(
    place_ref, proj_ref, table_ref, message_ref
):
    part = proj_ref.shape[0] // 8
    own_heads = table_ref.shape[1]
    room = message_ref.shape[1] // 2
    eighth = place_ref[2] * 2 + place_ref[1]
    message_ref[:part] = proj_ref[pl.ds(pl.multiple_of(eighth * part, part), part), :]
    offsets = table_ref.shape[0]
    table = jnp.concatenate(
        [table_ref[...], jnp.zeros((offsets, 128 - own_heads), F32)], 1
    )
    table = jnp.concatenate([table, jnp.zeros((room - offsets, 128), F32)], 0)
    table = jnp.transpose(table)[:own_heads]
    high = low(table).astype(F32)
    rows = jnp.concatenate([high, table - high], 1)
    spare = message_ref.shape[0] - part - own_heads
    message_ref[part:] = low(jnp.concatenate([rows, jnp.zeros((spare, 2 * room), F32)], 0))


def pieces_kernel(place_ref, *refs, part):
    del place_ref
    for j, ref in enumerate(refs[:-1]):
        refs[-1][j * part : (j + 1) * part] = ref[:part]


def front_kernel(
    place_ref, flat_ref, mg_ref, ms_ref, n1g_ref, n1s_ref, qb_ref, mw_any, qw_any,
    merged_ref, resid0_ref, normed1_ref, qkv_ref, mw_ref, qw_ref, sems,
):
    copy_m = pltpu.make_async_copy(mw_any, mw_ref, sems.at[0])
    copy_q = pltpu.make_async_copy(qw_any, qw_ref, sems.at[1])
    copy_m.start()
    copy_q.start()
    hat, _ = normalise(flat_ref[...].astype(F32))
    merged = low(hat * mg_ref[...] + ms_ref[...])
    merged_ref[...] = merged
    copy_m.wait()
    resid0 = matmul(merged, mw_ref[...])
    resid0_ref[...] = resid0
    hat1, _ = normalise(resid0)
    normed1 = low(hat1 * n1g_ref[...] + n1s_ref[...])
    normed1_ref[...] = normed1
    copy_q.wait()
    qkv_ref[...] = low(matmul(normed1, qw_ref[...]) + qb_ref[...])


def front_call(place, flat, mg, ms, n1g, n1s, qb, mw, qw):
    rows, deep = flat.shape
    width = mw.shape[1]
    return whole(
        front_kernel,
        place,
        [
            shape_of((rows, deep), BF),
            shape_of((rows, width), F32),
            shape_of((rows, width), BF),
            shape_of((rows, 3 * width), BF),
        ],
        (flat, True), (row(mg), True), (row(ms), True), (row(n1g), True), (row(n1s), True),
        (row(qb), True), (mw, False), (qw, False),
        scratch=[
            pltpu.VMEM(mw.shape, BF), pltpu.VMEM(qw.shape, BF), pltpu.SemaphoreType.DMA((2,)),
        ],
        room=28,
        name="front",
    )


def mine_kernel(place_ref, *refs):
    del place_ref
    rows = refs[0].shape[0]
    for q, ref in enumerate(refs[:-1]):
        refs[-1][q * rows : (q + 1) * rows] = ref[...]


def whole_proj(place_ref, own_ref, mine_ref, theirs_ref, proj_ref, groups):
    rank, core, quad = place_ref[0], place_ref[1], place_ref[2]
    shard = own_ref.shape[0]
    part = shard // 8
    proj_ref[pl.ds(pl.multiple_of(rank * shard, shard), shard), :] = own_ref[...]
    for k in range(4 * (groups - 1)):
        q, j = k // (groups - 1), k % (groups - 1)
        base = lax.rem(rank + groups - 1 - j, groups) * shard + (quad ^ q) * 2 * part
        rows = slice(k * part, (k + 1) * part)
        proj_ref[pl.ds(pl.multiple_of(base + core * part, part), part), :] = mine_ref[rows]
        proj_ref[pl.ds(pl.multiple_of(base + (1 - core) * part, part), part), :] = theirs_ref[rows]


def after_kernel(
    place_ref, heads_ref, resid0_ref, pb_ref, n2g_ref, n2s_ref, own_ref, mine_ref, theirs_ref,
    resid1_ref, normed2_ref, proj_ref, *, groups,
):
    whole_proj(place_ref, own_ref, mine_ref, theirs_ref, proj_ref, groups)
    resid1 = resid0_ref[...] + matmul(heads_ref[...], proj_ref[...]) + pb_ref[...]
    resid1_ref[...] = resid1
    hat2, _ = normalise(resid1)
    normed2_ref[...] = low(hat2 * n2g_ref[...] + n2s_ref[...])


SQRT_HALF = 0.5**0.5
DENSITY = 0.3989422804014327


def gelu_pair(values):
    below = 0.5 * (1.0 + lax.erf(values * SQRT_HALF))
    density = jnp.exp(-0.5 * values * values) * DENSITY
    return values * below, below + values * density


def slope_kernel(
    place_ref, dy_ref, fc2_ref, rows_ref, own_ref, out_ref, wide_ref, *, groups, pad, chunk
):
    tokens, width = own_ref.shape
    wide_ref[...] = dy_ref[...].astype(F32)
    fill = jnp.zeros((pad - tokens, width), F32)
    for j in range(groups):
        at = lax.rem(place_ref[0] + groups - j, groups) * tokens
        block = wide_ref[pl.ds(pl.multiple_of(at, 8), tokens), :]
        rows_ref[j * pad : (j + 1) * pad] = low(jnp.concatenate([block, fill], 0))
        if j == 0:
            own_ref[...] = low(block)

    @pl.loop(0, fc2_ref.shape[0] // chunk)
    def _(step):
        at = pl.ds(pl.multiple_of(step * chunk, chunk), chunk)
        out_ref[:, at] = contract(rows_ref[...], fc2_ref[at, :], 1, 1)


def feed_kernel(
    place_ref, n0_ref, n1_ref, n2_ref, n3_ref, d_act_ref, fc1_ref, fc1b_ref,
    act_ref, dpre_ref, all_ref, db_ref, o0_ref, o1_ref, o2_ref, o3_ref, *, pad, chunk,
):
    del place_ref
    rows, width = n0_ref.shape
    for j, ref in enumerate((n0_ref, n1_ref, n2_ref, n3_ref)):
        all_ref[j * pad : j * pad + rows, :] = ref[...]
        all_ref[j * pad + rows : (j + 1) * pad, :] = jnp.zeros((pad - rows, width), BF)

    @pl.loop(0, fc1_ref.shape[1] // chunk)
    def _(step):
        at = pl.ds(pl.multiple_of(step * chunk, chunk), chunk)
        pre = matmul(all_ref[...], fc1_ref[:, at]) + fc1b_ref[:, at]
        act, slope = gelu_pair(pre)
        act_ref[:, at] = low(act)
        d_low = low(d_act_ref[:, at] * slope)
        dpre_ref[:, at] = d_low
        db_ref[:, at] = jnp.sum(d_low.astype(F32), 0, keepdims=True)

    for j, ref in enumerate((o0_ref, o1_ref, o2_ref, o3_ref)):
        part = contract(dpre_ref[j * pad : (j + 1) * pad, :], fc1_ref[...], 1, 1)
        ref[...] = low(part[:rows])


def second_kernel(place_ref, act_ref, fc2_ref, kept_ref, sent_ref, *, pad, groups):
    rank = place_ref[0]
    rows = kept_ref.shape[1]
    for ref, k, flip in ((sent_ref, 0, 1), (sent_ref, 1, 3), (kept_ref, 0, 0), (kept_ref, 1, 2)):
        block = lax.rem(rank + groups - (rank ^ flip), groups)
        at = pl.ds(pl.multiple_of(block * pad, pad), pad)
        ref[k] = low(matmul(act_ref[at, :], fc2_ref[...])[:rows])


def back2_kernel(
    place_ref, c0_ref, c1_ref, c2_ref, c3_ref, resid1_ref, dy_ref, n2g_ref, own_ref, mine_ref, theirs_ref,
    dresid1_ref, dheads_ref, proj_ref, *, groups,
):
    whole_proj(place_ref, own_ref, mine_ref, theirs_ref, proj_ref, groups)
    rows = dheads_ref.shape[0]
    d_norm2 = (
        c0_ref[...].astype(F32) + c1_ref[...].astype(F32)
        + c2_ref[...].astype(F32) + c3_ref[...].astype(F32)
    )
    hat2, inv2 = normalise(resid1_ref[...])
    dy = dy_ref[...].astype(F32)
    d_resid1 = dy + norm_backward(d_norm2, hat2, inv2, n2g_ref[...])
    dresid1_ref[:rows] = d_resid1
    sums = (d_resid1, d_norm2 * hat2, d_norm2, dy)
    for k, part in enumerate(sums):
        dresid1_ref[rows + k : rows + k + 1] = jnp.sum(part, 0, keepdims=True)
    dheads_ref[...] = low(contract(low(d_resid1), proj_ref[...], 1, 1))


def back1_kernel(
    place_ref, d0_ref, d1_ref, d2_ref, d3_ref, dresid1_ref, resid0_ref, n1g_ref, qw_any,
    dresid0_ref, sums_ref, qw_ref, sems,
):
    rows, width = resid0_ref.shape
    quad = place_ref[2]
    lanes = width // 4
    copies = [
        pltpu.make_async_copy(qw_any.at[:, pl.ds(i * width, width)], qw_ref.at[i], sems.at[i])
        for i in range(3)
    ]
    for copy in copies:
        copy.start()
    hat1, inv1 = normalise(resid0_ref[...])
    d_norm1 = jnp.zeros((rows, width), F32)
    for i in range(3):
        copies[i].wait()
        for j, d_ref in enumerate((d0_ref, d1_ref, d2_ref, d3_ref)):
            part = d_ref[:, i * lanes : (i + 1) * lanes]
            at = pl.ds(pl.multiple_of((quad ^ j) * lanes, lanes), lanes)
            d_norm1 = d_norm1 + contract(part, qw_ref[i, :, at], 1, 1)
            sums_ref[2 + i : 3 + i, at] = jnp.sum(part.astype(F32), 0, keepdims=True)
    dresid0_ref[...] = low(
        dresid1_ref[:rows] + norm_backward(d_norm1, hat1, inv1, n1g_ref[...])
    )
    sums_ref[0:1] = jnp.sum(d_norm1 * hat1, 0, keepdims=True)
    sums_ref[1:2] = jnp.sum(d_norm1, 0, keepdims=True)


def back0_kernel(
    place_ref, dresid0_ref, flat_ref, mg_ref, mw_any, grad_ref, sums_ref, mw_ref, sems
):
    del place_ref
    copy = pltpu.make_async_copy(mw_any, mw_ref, sems.at[0])
    copy.start()
    hat, inv = normalise(flat_ref[...].astype(F32))
    copy.wait()
    d_merged = contract(dresid0_ref[...], mw_ref[...], 1, 1)
    grad_ref[...] = low(norm_backward(d_merged, hat, inv, mg_ref[...]))
    width = dresid0_ref.shape[1]
    gain = jnp.sum(d_merged * hat, 0, keepdims=True)
    shift = jnp.sum(d_merged, 0, keepdims=True)
    for i in range(gain.shape[1] // width):
        sums_ref[i : i + 1] = gain[:, i * width : (i + 1) * width]
        sums_ref[2 + i : 3 + i] = shift[:, i * width : (i + 1) * width]


SPAN = 2 * WIN - 1
OFFSETS = 384
STRIP = 256


def strip_picks(column, offsets_first):
    shape, o_dim = ((OFFSETS, STRIP), 0) if offsets_first else ((STRIP, OFFSETS), 1)
    offset = lax.broadcasted_iota(jnp.int32, shape, o_dim)
    lane = lax.broadcasted_iota(jnp.int32, shape, 1 - o_dim)
    wanted = (SPAN - 1 - lane // WIN) * SPAN + column - lane % WIN + WIN - 1
    hit = (offset == wanted) & (lane < SPAN * WIN)
    return jnp.where(hit, 1.0, 0.0).astype(BF)


def split3(values):
    first = low(values)
    rest = values - first.astype(F32)
    second = low(rest)
    third = low(rest - second.astype(F32))
    return first, second, third


def spread_kernel(place_ref, m0_ref, m1_ref, m2_ref, m3_ref, bias_ref, table_ref, *, part, groups):
    heads = table_ref.shape[0]
    own_heads = heads // groups
    room = m0_ref.shape[1] // 2
    for j, ref in enumerate((m0_ref, m1_ref, m2_ref, m3_ref)):
        both = ref[part : part + 2 * own_heads, :].astype(F32)[:own_heads]
        at = pl.multiple_of(lax.rem(place_ref[0] + groups - j, groups) * own_heads, own_heads)
        table_ref[pl.ds(at, own_heads), :] = both[:, :OFFSETS] + both[:, room : room + OFFSETS]
    table = table_ref[...]
    high = low(table)
    table = jnp.concatenate([high, low(table - high.astype(F32))], 0)
    for column in range(WIN):
        parts = matmul(table, strip_picks(column, True))
        strip = parts[:heads] + parts[heads:]
        for r in range(WIN):
            start = (WIN - 1 - r) * WIN
            at = (r * WIN + column) * heads
            bias_ref[at : at + heads, :] = strip[:, start : start + KEY_ROWS]
    bias_ref[WINDOW_TOKENS * heads :, :] = jnp.zeros(
        ((QUERY_ROWS - WINDOW_TOKENS) * heads, KEY_ROWS), F32
    )


def fold(grad_ref, heads):
    total = jnp.zeros((3 * heads, OFFSETS), F32)
    for column in range(WIN):
        strip = jnp.zeros((heads, STRIP), F32)
        for r in range(WIN):
            start = (WIN - 1 - r) * WIN
            at = (r * WIN + column) * heads
            part = grad_ref[at : at + heads, :]
            wide = jnp.concatenate([part, jnp.zeros((heads, STRIP - KEY_ROWS), F32)], 1)
            strip = strip + (pltpu.roll(wide, start, 1) if start else wide)
        total = total + matmul(jnp.concatenate(split3(strip), 0), strip_picks(column, False))
    return total[:heads] + total[heads : 2 * heads] + total[2 * heads :]


def window_rows(values, window, rows):
    part = values.astype(F32)[window * WINDOW_TOKENS : (window + 1) * WINDOW_TOKENS]
    zeros = jnp.zeros((rows - WINDOW_TOKENS, part.shape[1]), F32)
    return low(jnp.concatenate([part, zeros], 0))


def stack_heads(part, heads, head_dim):
    lane = lax.broadcasted_iota(jnp.int32, part.shape, 1) // head_dim
    zero = jnp.zeros_like(part)
    return jnp.concatenate([jnp.where(lane == h, part, zero) for h in range(heads)], 0)


def attend_kernel(
    place_ref, qkv_ref, bias_ref, mask_ref, out_ref, probs_any, probs_ref, sems, *, windows, head_dim
):
    del place_ref
    width = out_ref.shape[1]
    lanes = width // 4

    def keep(step):
        return pltpu.make_async_copy(probs_ref.at[step], probs_any.at[step], sems.at[step])

    @pl.loop(0, 4, unroll=True)
    def _(step):
        attend_group(
            step, qkv_ref, bias_ref, mask_ref, out_ref, probs_ref, windows, head_dim, width, lanes
        )
        keep(step).start()

    for step in range(4):
        keep(step).wait()


def attend_group(
    step, qkv_ref, bias_ref, mask_ref, out_ref, probs_ref, windows, head_dim, width, lanes
):
    heads, all_heads = lanes // head_dim, width // head_dim
    first = step * heads
    scale = head_dim ** (-0.5)
    at = lambda kind: pl.ds(pl.multiple_of(kind * width + step * lanes, lanes), lanes)
    q_all, k_all, v_all = (qkv_ref[:, at(kind)] for kind in range(3))
    outs = []
    for w in range(windows):
        query = window_rows(q_all, w, QUERY_ROWS)
        keys = stack_heads(window_rows(k_all, w, KEY_ROWS), heads, head_dim)
        values = stack_heads(window_rows(v_all, w, KEY_ROWS), heads, head_dim)
        scores = contract(query, keys, 1, 1) * scale
        mask = mask_ref[w]
        rounded = []
        for h in range(heads):
            bias = bias_ref[pl.ds(first + h, QUERY_ROWS, stride=all_heads), :]
            raw = scores[:, h * KEY_ROWS : (h + 1) * KEY_ROWS] + bias + mask
            expo = jnp.exp(raw - jnp.max(raw, -1, keepdims=True))
            probs = expo / jnp.sum(expo, -1, keepdims=True)
            probs_ref[step, w, h] = probs
            rounded.append(low(probs))
        mixed = matmul(jnp.concatenate(rounded, 1), values)
        outs.append(mixed[:WINDOW_TOKENS])
    out_ref[:, at(0)] = low(jnp.concatenate(outs, 0))


def attend_back_kernel(
    place_ref, qkv_ref, grad_ref, probs_any, d0_ref, d1_ref, d2_ref, d3_ref, table_ref, dbias_ref, probs_ref, sems,
    *, windows, head_dim
):
    width = grad_ref.shape[1]

    def fetch(step):
        return pltpu.make_async_copy(
            probs_any.at[place_ref[2] ^ step], probs_ref.at[step], sems.at[step]
        )

    for step in range(4):
        fetch(step).start()

    @pl.loop(0, 4)
    def _(step):
        fetch(step).wait()
        attend_back_group(
            place_ref[2] ^ step, step, qkv_ref, grad_ref, probs_ref, (d0_ref, d1_ref, d2_ref, d3_ref), dbias_ref,
            windows, head_dim, width, width // 4,
        )

    table_ref[...] = fold(dbias_ref, table_ref.shape[0])


def attend_back_group(
    group, step, qkv_ref, grad_ref, probs_ref, d_refs, dbias_ref,
    windows, head_dim, width, lanes,
):
    heads, all_heads = lanes // head_dim, width // head_dim
    first = group * heads
    scale = head_dim ** (-0.5)
    at = lambda kind: pl.ds(pl.multiple_of(kind * width + group * lanes, lanes), lanes)
    q_all, k_all, v_all = (qkv_ref[:, at(kind)] for kind in range(3))
    g_all = grad_ref[:, at(0)]
    all_q, all_k, all_v = [], [], []
    d_first = []
    for w in range(windows):
        query = stack_heads(window_rows(q_all, w, QUERY_ROWS), heads, head_dim)
        keys = stack_heads(window_rows(k_all, w, KEY_ROWS), heads, head_dim)
        values = stack_heads(window_rows(v_all, w, KEY_ROWS), heads, head_dim)
        plain = window_rows(g_all, w, QUERY_ROWS)
        grad = stack_heads(plain, heads, head_dim)
        d_probs = contract(plain, values, 1, 1)
        d_list, p_list = [], []
        for h in range(heads):
            probs = probs_ref[step, w, h]
            part = d_probs[:, h * KEY_ROWS : (h + 1) * KEY_ROWS]
            total = jnp.sum(part * probs, -1, keepdims=True)
            d_scores = low(probs * (part - total))
            d_list.append(d_scores)
            p_list.append(low(probs))
            if w == 0:
                d_first.append(d_scores.astype(F32))
            else:
                d_first[h] = d_first[h] + d_scores.astype(F32)
            if w == windows - 1:
                dbias_ref[pl.ds(first + h, QUERY_ROWS, stride=all_heads), :] = d_first[h]
        d_query = matmul(jnp.concatenate(d_list, 1), keys) * scale
        d_keys = contract(jnp.concatenate(d_list, 0), query, 0, 0) * scale
        d_values = contract(jnp.concatenate(p_list, 0), grad, 0, 0)
        all_q.append(d_query[:WINDOW_TOKENS])
        all_k.append(d_keys[:WINDOW_TOKENS])
        all_v.append(d_values[:WINDOW_TOKENS])
    result = jnp.concatenate(
        [low(jnp.concatenate(parts, 0)) for parts in (all_q, all_k, all_v)], 1
    )

    for k, d_ref in enumerate(d_refs):

        @pl.when(step == k)
        def _(d_ref=d_ref):
            d_ref[...] = result


def spots(heads, lines, vectors):
    columns = 3
    return [(k // columns, OFFSETS + 128 * (k % columns)) for k in range(vectors * lines)]


def collect_kernel(place_ref, s0_ref, s1_ref, d_ref, rel_ref, b_ref, out_ref):
    heads = rel_ref.shape[0]
    lines = s0_ref.shape[1] // 128
    out_ref[...] = jnp.zeros(out_ref.shape, F32)
    out_ref[:heads, :OFFSETS] = rel_ref[...]
    vectors = [ref[r : r + 1, :] for ref in (s0_ref, s1_ref) for r in range(ref.shape[0])]
    after = d_ref.shape[0] - 8
    vectors += [d_ref[after + r : after + r + 1, :] for r in range(4)]
    for k, (at, lane) in enumerate(spots(heads, lines, len(vectors))):
        piece = vectors[k // lines][:, 128 * (k % lines) : 128 * (k % lines + 1)]
        out_ref[at : at + 1, lane : lane + 128] = piece
    own = b_ref.shape[1] // 128
    first = heads + pl.multiple_of((place_ref[0] // 2) * own, own)
    block = jnp.concatenate([b_ref[:, k * 128 : (k + 1) * 128] for k in range(own)], 0)
    side = place_ref[0] % 2

    @pl.when(side == 0)
    def _():
        out_ref[pl.ds(first, own), 0:128] = block

    @pl.when(side == 1)
    def _():
        out_ref[pl.ds(first, own), 128:256] = block


def deliver_kernel(place_ref, all_ref, *refs, heads):
    *vector_refs, rel_ref, b_ref = refs
    rel_ref[...] = all_ref[:heads, : rel_ref.shape[1]]
    lines = [ref.shape[0] // 128 for ref in vector_refs]
    places = iter(spots(heads, 1, sum(lines)))
    for ref, count in zip(vector_refs, lines):
        for k in range(count):
            at, lane = next(places)
            ref[128 * k : 128 * (k + 1)] = all_ref[at, lane : lane + 128]
    own = b_ref.shape[0]
    first = heads + pl.multiple_of((place_ref[0] // 2) * own, own)
    side = place_ref[0] % 2

    @pl.when(side == 0)
    def _():
        b_ref[...] = all_ref[pl.ds(first, own), 0:128]

    @pl.when(side == 1)
    def _():
        b_ref[...] = all_ref[pl.ds(first, own), 128:256]


def columns_kernel(place_ref, b0_ref, b1_ref, b2_ref, b3_ref, own_ref, out_ref, sums_ref):
    rows, step = out_ref.shape[0], b0_ref.shape[1]
    lanes = b0_ref.shape[2] // 3
    total = own_ref[...]
    for j, ref in enumerate((b0_ref, b1_ref, b2_ref, b3_ref)):
        for part in range(3):
            at = pl.multiple_of((part * 4 + (place_ref[2] ^ j)) * lanes, lanes)
            for s in range(rows // step):
                block = ref[s, :, part * lanes : (part + 1) * lanes].astype(F32)
                out_ref[s * step : (s + 1) * step, pl.ds(at, lanes)] = block
        if j:
            total = total + take_sums(ref, rows // step, own_ref.shape[0])
    sums_ref[...] = total


def on_device(
    patches,
    window_extent,
    merge_gain,
    merge_shift,
    merge_weight,
    norm1_gain,
    norm1_shift,
    qkv_weight,
    qkv_bias,
    rel_table,
    proj_weight,
    proj_bias,
    norm2_gain,
    norm2_shift,
    fc1_weight,
    fc1_bias,
    fc2_weight,
    fc2_bias,
    out_grad,
):
    groups, wide = lax.axis_size("narrow"), lax.axis_size("wide")
    devices = wide * groups
    highs = wide // 8
    wide_at, rank = lax.axis_index("wide"), lax.axis_index("narrow")
    core, quad, high = wide_at % 2, (wide_at // 2) % 4, wide_at // 8
    place = jnp.stack([rank, core, quad]).astype(jnp.int32)
    tokens = patches.shape[0]
    width = qkv_weight.shape[0]
    own_heads = rel_table.shape[1]
    heads = own_heads * groups
    head_dim = width // heads
    windows = tokens // WINDOW_TOKENS
    pad = tokens + (-tokens) % 16

    def arrange(array, order):
        if highs == 1:
            return array
        sizes = {"h": highs, "q": 4, "c": 2, "n": groups}
        cut = [sizes[k] for k in order]
        rest = array.shape[1]
        for size in cut:
            rest //= size
        at = order.index("h") + 1
        moved = [i + 1 for i in range(len(order)) if i + 1 != at] + [at, len(order) + 1]
        return jnp.transpose(array.reshape(-1, *cut, rest), [0] + moved).reshape(array.shape)

    def settle(array):
        if highs == 1:
            return array[0]
        return sum_high(array[0].reshape(highs, -1, array.shape[2]), high)

    part = proj_weight.shape[0] // 8
    message = whole(
        pack_kernel,
        place,
        [shape_of((part + own_heads + (-(part + own_heads)) % 16, width), BF)],
        (proj_weight, True),
        (rel_table, True),
        name="pack",
    )[0]
    messages = [turn(message, "narrow", step) for step in range(1, groups)]

    flat = patches.reshape(tokens, -1)
    merged, resid0, normed1, qkv = front_call(
        place, flat, merge_gain, merge_shift, norm1_gain, norm1_shift, qkv_bias,
        merge_weight, qkv_weight,
    )
    mine = whole(
        functools.partial(pieces_kernel, part=part),
        place,
        [shape_of(((groups - 1) * part, width), BF)],
        *((m, True) for m in messages),
        name="pieces",
    )
    mine = list(mine) + [swap(mine[0], "wide", 2 * j) for j in (1, 2, 3)]

    merged_own, merged_sent, merged_onward = whole(
        cut_kernel,
        place,
        [
            shape_of((tokens, merged.shape[1] // 4), BF),
            shape_of((2, tokens, merged.shape[1] // 4), BF),
            shape_of((tokens, merged.shape[1] // 4), BF),
        ],
        (arrange(merged, "hqcn"), True),
        name="cut",
    )
    normed1_cut = arrange(normed1, "hqcn")

    positions = jnp.arange(KEY_ROWS)
    extent = lax.dynamic_slice_in_dim(window_extent, rank * windows, windows, 0)
    valid = (
        (positions[None, :] // WIN < extent[:, 0:1])
        & (positions[None, :] % WIN < extent[:, 1:2])
        & (positions[None, :] < WINDOW_TOKENS)
    )
    mask = jnp.where(valid, 0.0, -1e30).astype(F32)[:, None, :]
    bias = whole(
        functools.partial(spread_kernel, part=part, groups=groups),
        place,
        [shape_of((QUERY_ROWS * heads, KEY_ROWS), F32)],
        (message, True),
        *((m, True) for m in messages),
        scratch=[pltpu.VMEM((heads, OFFSETS), F32)],
        name="spread",
    )[0]
    heads_out, probs = whole(
        functools.partial(attend_kernel, windows=windows, head_dim=head_dim),
        place,
        [
            shape_of((tokens, width), BF),
            shape_of((PROBS_ROOM, windows, heads // 4, QUERY_ROWS, KEY_ROWS), F32),
        ],
        (qkv, True), (bias, True), (mask, True),
        leave=(1,),
        scratch=[
            pltpu.VMEM((4, windows, heads // 4, QUERY_ROWS, KEY_ROWS), F32),
            pltpu.SemaphoreType.DMA((4,)),
        ],
        name="attend",
    )

    mine = whole(
        mine_kernel,
        place,
        [shape_of((4 * mine[0].shape[0], width), BF)],
        *((m, True) for m in mine),
        after=(heads_out,),
        name="mine",
    )[0]
    theirs = swap(mine, "wide", 1)
    resid1, normed2, merged_sent, normed1_cut, merged_onward = whole(
        functools.partial(after_kernel, groups=groups),
        place,
        [shape_of((tokens, width), F32), shape_of((tokens, width), BF)],
        (heads_out, True), (resid0, True),
        (row(proj_bias), True), (row(norm2_gain), True), (row(norm2_shift), True),
        (proj_weight, True), (mine, True), (theirs, True),
        scratch=[pltpu.VMEM((width, width), BF)],
        through=(merged_sent, normed1_cut, merged_onward),
        name="after",
    )
    merged_near = swap(merged_sent, "wide", 4)
    normed1_near = swap(normed1_cut, "wide", 2)
    blocks = [normed2] + [turn(normed2, "narrow", step) for step in range(1, groups)]

    merged_onward = jnp.stack([merged_onward, merged_near[1]])
    merged_far = swap(merged_onward, "wide", 2)
    normed1_both = jnp.stack([normed1_cut, normed1_near])
    normed1_far = swap(normed1_both, "wide", 4)

    total, units = groups * pad, fc1_weight.shape[1]
    dy_rows, dy_own, d_act = whole(
        functools.partial(slope_kernel, groups=groups, pad=pad, chunk=256),
        place,
        [
            shape_of((total, width), BF),
            shape_of((tokens, width), BF),
            shape_of((total, units), F32),
        ],
        (out_grad, True), (fc2_weight, True),
        scratch=[pltpu.VMEM(out_grad.shape, F32)],
        after=(normed2,),
        name="slope",
    )
    act, d_pre, rows_all, fc1_b_grad, *chunks = whole(
        functools.partial(feed_kernel, pad=pad, chunk=256),
        place,
        [
            shape_of((total, units), BF),
            shape_of((total, units), BF),
            shape_of((total, width), BF),
            shape_of((1, units), F32),
        ]
        + [shape_of((tokens, width), BF)] * 4,
        *((b, True) for b in blocks), (d_act, True), (fc1_weight, True), (row(fc1_bias), True),
        after=(normed1_far, merged_far),
        name="feed",
    )
    arrived = [chunks[0]] + [turn(chunks[j], "narrow", -j) for j in range(1, groups)]

    fc1_kept, fc1_sent = grad_call(place, [arrange(rows_all, "hqc")], [d_pre], 256, 128, "fc1_grad")
    fc2_kept, fc2_sent = grad_call(place, [arrange(act, "hqc")], [dy_rows], 256, 128, "fc2_grad")
    fc1_come, fc2_come = swap(fc1_sent, "wide", 1), swap(fc2_sent, "wide", 1)
    fc1_kept, fc1_sent = join_call(
        place, [(fc1_kept, fc1_come)],
        [
            (F32, [lambda p, y=y: (0, 2 * y + p[2] % 2, 0, 128) for y in range(2)]),
            (BF, [lambda p, y=y: (0, 2 * y + 1 - p[2] % 2, 0, 128) for y in range(2)]),
        ],
        "fc1_join",
    )
    fc2_kept, fc2_sent = join_call(
        place, [(fc2_kept, fc2_come)],
        [
            (F32, [lambda p, x=x: (0, 2 * (p[2] // 2) + x, 0, 128) for x in range(2)]),
            (BF, [lambda p, x=x: (0, 2 * (1 - p[2] // 2) + x, 0, 128) for x in range(2)]),
        ],
        "fc2_join",
    )
    fc1_come, fc2_come = swap(fc1_sent, "wide", 2), swap(fc2_sent, "wide", 4)
    fc1_kept, fc1_sent = join_call(
        place, [(fc1_kept, fc1_come)],
        [
            (F32, [lambda p: (0, p[2] // 2, 0, 128)]),
            (BF, [lambda p: (0, 1 - p[2] // 2, 0, 128)]),
        ],
        "fc1_join2",
    )
    fc2_kept, fc2_sent = join_call(
        place, [(fc2_kept, fc2_come)],
        [
            (F32, [lambda p: (0, p[2] % 2, 0, 128)]),
            (BF, [lambda p: (0, 1 - p[2] % 2, 0, 128)]),
        ],
        "fc2_join2",
    )
    fc1_come, fc2_come = swap(fc1_sent, "wide", 4), swap(fc2_sent, "wide", 2)
    second_kept, second_sent = whole(
        functools.partial(second_kernel, pad=pad, groups=groups),
        place,
        [shape_of((2, tokens, width), BF)] * 2,
        (act, True),
        (fc2_weight, True),
        name="second",
    )
    d_resid1, d_heads, second_sent = whole(
        functools.partial(back2_kernel, groups=groups),
        place,
        [shape_of((tokens + 8, width), F32), shape_of((tokens, width), BF)],
        *((a, True) for a in arrived),
        (resid1, True), (dy_own, True), (row(norm2_gain), True),
        (proj_weight, True), (mine, True), (theirs, True),
        scratch=[pltpu.VMEM((width, width), BF)],
        after=(fc1_sent, fc2_sent),
        through=(second_sent,),
        name="back2",
    )
    second_come = swap(second_sent, "narrow", 1)
    *d_parts, rel_part = whole(
        functools.partial(attend_back_kernel, windows=windows, head_dim=head_dim),
        place,
        [shape_of((tokens, 3 * width // 4), BF)] * 4 + [shape_of((heads, OFFSETS), F32)],
        (qkv, True), (d_heads, True), (probs, False),
        scratch=[
            pltpu.VMEM((QUERY_ROWS * heads, KEY_ROWS), F32),
            pltpu.VMEM((4, *probs.shape[1:]), F32),
            pltpu.SemaphoreType.DMA((4,)),
        ],
        after=(fc1_come, fc2_come),
        name="attend_back",
    )
    d_come = [swap(d_parts[j], "wide", 2 * j) for j in (1, 2, 3)]

    d_resid0, sums1 = whole(
        back1_kernel,
        place,
        [shape_of((tokens, width), BF), shape_of((5, width), F32)],
        *((d, True) for d in d_parts), (d_resid1, True), (resid0, True),
        (row(norm1_gain), True), (qkv_weight, False),
        scratch=[
            pltpu.VMEM((3, width, width), BF),
            pltpu.SemaphoreType.DMA((3,)),
        ],
        name="back1",
    )
    d_flat, sums0 = whole(
        back0_kernel,
        place,
        [shape_of(flat.shape, BF), shape_of((2 * flat.shape[1] // width, width), F32)],
        (d_resid0, True), (flat, True), (row(merge_gain), True), (merge_weight, False),
        scratch=[pltpu.VMEM(merge_weight.shape, BF), pltpu.SemaphoreType.DMA((1,))],
        name="back0",
    )

    second_own, second_sent = join_call(
        place, [(second_kept, second_come)],
        [(F32, [lambda p: (0, 0, 0, tokens)]), (BF, [lambda p: (0, 1, 0, tokens)])],
        "second_join",
    )
    second_come = swap(second_sent, "narrow", 2)

    proj_kept, proj_sent = grad_call(
        place, [arrange(heads_out, "nhqc")], [d_resid1], 256, 32, "proj_grad", after=(d_resid0,)
    )
    proj_come = swap(proj_sent, "wide", 1)

    side = lambda pick_x: [
        lambda p, n=n, y=y: (0, n, (2 * y + pick_x(p[2] % 2)) * 32, 32)
        for n in range(groups) for y in range(2)
    ]
    proj_kept, proj_sent = join_call(
        place, [(proj_kept, proj_come)],
        [(F32, side(lambda x: x)), (BF, side(lambda x: 1 - x))],
        "proj_join",
    )
    proj_come = swap(proj_sent, "wide", 2)

    own_sums, d_resid0 = whole(
        collect_kernel,
        place,
        [shape_of((48, 3 * width // 4), F32)],
        (sums0, True), (sums1, True), (d_resid1, True), (rel_part, True), (fc1_b_grad, True),
        after=(*d_come, second_sent, proj_sent),
        through=(d_resid0,),
        name="collect",
    )
    r_come = [swap(d_resid0, "wide", 2 * j) for j in (1, 2, 3)]
    qkv_kept, qkv_sent = grad_call(
        place,
        [normed1_cut, (normed1_both, 1), (normed1_far, 0), (normed1_far, 1)],
        [d_parts[0], *d_come],
        256, 128, "qkv_grad", sums=own_sums, after=(second_sent,),
    )
    qkv_come = swap(qkv_sent, "wide", 1)
    rows = 128 // groups
    step = 16 if rows % 16 == 0 else rows
    cuts_of = rows // step
    qkv_pieces = lambda flip: [
        lambda p, g=g, k=k, s=s: (0, g, (2 * k + (p[0] + flip) % 2) * rows + s * step, step)
        for k in range(2) for g in range(4) for s in range(cuts_of)
    ]
    own_sums, qkv_kept, qkv_sent = join_call(
        place, [(qkv_kept, qkv_come)], [(F32, qkv_pieces(0)), (BF, qkv_pieces(1))], "qkv_join",
        sums=(own_sums, 4),
    )
    qkv_come = swap(qkv_sent, "narrow", 1)

    merge_kept, merge_sent = grad_call(
        place,
        [merged_own, (merged_far, 0), (merged_near, 0), (merged_far, 1)],
        [d_resid0, *r_come],
        merged_own.shape[1], merged_own.shape[1] // 2, "merge_grad", after=(qkv_sent,),
    )
    merge_come = swap(merge_sent, "wide", 1)

    second_pieces = lambda flip: [
        lambda p, g=g: (0, ((p[0] // 2 + flip) % 2) * 4 * cuts_of + g, 0, step)
        for g in range(4 * cuts_of)
    ]
    own_sums, qkv_kept, qkv_sent = join_call(
        place, [(qkv_kept, qkv_come)],
        [(F32, second_pieces(0)), (BF, second_pieces(1))],
        "qkv_join2",
        sums=(own_sums, 8 * cuts_of),
        after=(merge_sent,),
    )
    qkv_come = swap(qkv_sent, "narrow", 2)
    merge_rows = merged_own.shape[1] // 2 // groups
    merge_pieces = lambda flip: [
        lambda p, k=k: (0, 0, (2 * k + (p[0] + flip) % 2) * merge_rows, merge_rows)
        for k in range(2)
    ]
    merge_kept, merge_sent, fc1_come, fc2_come, d_flat = join_call(
        place, [(merge_kept, merge_come)],
        [(F32, merge_pieces(0)), (BF, merge_pieces(1))],
        "merge_join",
        after=(qkv_sent,),
        through=(fc1_come, fc2_come, d_flat),
    )
    merge_first = merge_sent
    merge_come = swap(merge_sent, "narrow", 1)

    last_pieces = lambda flip, size: [lambda p: (0, (p[0] // 2 + flip) % 2, 0, size)]
    merge_kept, merge_sent = join_call(
        place, [(merge_kept, merge_come)],
        [(F32, last_pieces(0, merge_rows)), (BF, last_pieces(1, merge_rows))],
        "merge_join2",
        after=(qkv_sent,),
    )
    merge_last = merge_sent
    merge_come = swap(merge_sent, "narrow", 2)

    proj_kept, proj_sent = join_call(
        place, [(proj_kept, proj_come)],
        [
            (F32, [lambda p, n=n: (0, 2 * n + p[2] // 2, 0, 32) for n in range(groups)]),
            (BF, [lambda p, n=n: (0, 2 * n + 1 - p[2] // 2, 0, 32) for n in range(groups)]),
        ],
        "proj_join2",
        after=(merge_first,),
    )
    proj_come = swap(proj_sent, "wide", 4)
    proj_pieces = lambda flip: [
        lambda p, k=k: (0, 2 * k + (p[0] + flip) % 2, 0, 32) for k in range(2)
    ]
    proj_kept, proj_sent = join_call(
        place, [(proj_kept, proj_come)], [(F32, proj_pieces(0)), (BF, proj_pieces(1))],
        "proj_join3",
        after=(merge_sent,),
    )
    proj_come = swap(proj_sent, "narrow", 1)
    proj_kept, proj_sent = join_call(
        place, [(proj_kept, proj_come)],
        [(F32, last_pieces(0, 32)), (BF, last_pieces(1, 32))],
        "proj_join4",
    )
    proj_come = swap(proj_sent, "narrow", 2)

    own_sums, *cuts = join_call(
        place, [(qkv_kept, qkv_come)],
        [
            (BF, [lambda p, j=j, s=s: (0, (p[2] ^ j) * cuts_of + s, 0, step) for s in range(cuts_of)])
            for j in range(4)
        ],
        "qkv_join3",
        sums=(own_sums, 4 * cuts_of),
        after=(merge_last,),
    )
    cuts = [cuts[0]] + [swap(cuts[j], "wide", 2 * j) for j in (1, 2, 3)]
    qkv_out, all_sums = whole(
        columns_kernel,
        place,
        [shape_of((rows, 3 * width), F32), shape_of(own_sums.shape, F32)],
        *((c, True) for c in cuts), (own_sums, True),
        name="columns",
    )
    qkv_out = settle(qkv_out[None])
    mask = 8
    while mask < wide:
        all_sums = all_sums + swap(all_sums, "wide", mask)
        mask *= 2
    merge_out = settle(merge_kept + merge_come.astype(F32))
    proj_out = settle(proj_kept + proj_come.astype(F32))

    fc1_out = settle(fc1_kept + fc1_come.astype(F32))
    fc2_out = settle(fc2_kept + fc2_come.astype(F32))
    patches_grad = d_flat.reshape(patches.shape)
    output = low(resid1 + row(fc2_bias) + second_own[0] + second_come[0].astype(F32))

    deep = merged.shape[1]
    *vectors, rel_grad, fc1_b_mine = whole(
        functools.partial(deliver_kernel, heads=heads),
        place,
        [
            shape_of((size,), F32)
            for size in (deep, deep, width, width, 3 * width, width, width, width, width)
        ]
        + [shape_of((heads, rel_table.shape[0]), F32), shape_of((units // 128, 128), F32)],
        (all_sums, True),
        name="deliver",
    )
    fc1_b_out = lax.dynamic_index_in_dim(
        fc1_b_mine.reshape(wide, -1), wide_at, 0, keepdims=False
    )

    return (
        output,
        patches_grad,
        vectors[0],
        vectors[1],
        merge_out,
        vectors[2],
        vectors[3],
        qkv_out,
        vectors[4],
        jnp.transpose(rel_grad),
        proj_out,
        vectors[5],
        vectors[6],
        vectors[7],
        fc1_out,
        fc1_b_out,
        fc2_out,
        vectors[8],
    )


def solution(mesh):
    in_specs = (
        P(("wide", "narrow"), None, None),
        P("wide", None),
        P(),
        P(),
        P(),
        P(),
        P(),
        P(),
        P(),
        P(None, "narrow"),
        P("narrow", None),
        P(),
        P(),
        P(),
        P(None, "narrow"),
        P("narrow"),
        P("narrow", None),
        P(),
        P("wide", None),
    )
    out_specs = (
        P(("wide", "narrow"), None),
        P(("wide", "narrow"), None, None),
        P(),
        P(),
        P(("wide", "narrow"), None),
        P(),
        P(),
        P(("wide", "narrow"), None),
        P(),
        P(),
        P(("narrow", "wide"), None),
        P(),
        P(),
        P(),
        P("wide", "narrow"),
        P(("narrow", "wide")),
        P(("narrow", "wide"), None),
        P(),
    )
    return jax.shard_map(
        on_device, mesh=mesh, in_specs=in_specs, out_specs=out_specs, check_vma=False
    )
```
